256 devices in a mesh: gx: 16 (over z, core), gy: 16 (over x, y).
Axes of the slice: x: 4, y: 4, z: 8, core: 2. Of those that a mesh axis runs over, the one named last changes fastest.
Arguments:
- inputs: bfloat16 [64, 64, 64, 64], P('gx', 'gy'), may hold values from -6 to 6
- cotangent: bfloat16 [64, 64, 64, 128], P('gx', 'gy'), may hold values from -6 to 6
- w_enc: bfloat16 [3, 3, 3, 64, 128], replicated, may hold values from -0.15625 to 0.15625
- w_bot: bfloat16 [3, 3, 3, 128, 256], replicated, may hold values from -0.109375 to 0.109375
- w_up: bfloat16 [2, 2, 2, 256, 128], replicated, may hold values from -0.375 to 0.375
- w_dec: bfloat16 [3, 3, 3, 256, 128], replicated, may hold values from -0.078125 to 0.078125
Outputs:
- decoded: bfloat16 [64, 64, 64, 128], P('gx', 'gy')
- input_grad: bfloat16 [64, 64, 64, 64], P('gx', 'gy')
- grad_enc: float32 [3, 3, 3, 64, 128], P(None, None, None, None, 'gy')
- grad_bot: float32 [3, 3, 3, 128, 256], P(None, None, None, None, 'gy')
- grad_up: float32 [2, 2, 2, 256, 128], P(None, None, None, None, 'gy')
- grad_dec: float32 [3, 3, 3, 256, 128], P(None, None, None, None, 'gy')
- pool_grad: float32 [32, 32, 32, 128], P('gx', 'gy')
The draws below stay inside these ranges and needn't reach their ends.
All inputs are finite; a program needn't handle non-finite values.
Results may differ from the reference program's by a relative error of at most 0.018.
Values may be sent and summed in bfloat16 or wider, within the bound.
No kernel may reach another device: no remote copies, remote signals or barrier semaphores. Data moves between devices by JAX's collectives and lax.ppermute only.
A program may use at most 128 MiB of HBM per device.

```python
import jax
import jax.numpy as jnp
from jax import lax

C2 = 64
C3 = 128
C4 = 256
WID = 64
NX = 64
NY = 64


def levels(stream_key, extent, cuts, smallest, high):
    factor_of, own = 1.0, jax.random.fold_in(stream_key, 6)
    for dim, shards_of in cuts:
        draws = jnp.exp(jax.random.uniform(jax.random.fold_in(own, dim), (shards_of,), jnp.float32, smallest / len(cuts), high / len(cuts)))
        factor_of = factor_of * jnp.repeat(draws, extent[dim] // shards_of).reshape([-1 if axis == dim else 1 for axis in range(len(extent))])
    return factor_of


def noise(own_key, shape, deviation, most, cuts=(), dtype=jnp.bfloat16):
    level = levels(own_key, shape, cuts, -0.22, 0.18) if cuts else 1.0
    drawn = jax.random.normal(own_key, shape, jnp.float32) * deviation * level
    return jnp.minimum(jnp.maximum(drawn, -most), most).astype(dtype)


def setup_inputs(seed: int = 0) -> dict:
    splits = jax.random.split(jax.random.key(seed), 7)
    inputs = noise(splits[0], (NX, NY, WID, C2), 1.0, 6.0, ((0, 16), (1, 16)))
    cotangent = noise(splits[1], (NX, NY, WID, C3), 1.0, 6.0, ((0, 16), (1, 16)))
    w_enc = noise(splits[2], (3, 3, 3, C2, C3), (27 * C2) ** -0.5, 0.15625)
    w_bot = noise(splits[3], (3, 3, 3, C3, C4), (27 * C3) ** -0.5, 0.109375)
    w_up = noise(splits[4], (2, 2, 2, C4, C3), C4 ** -0.5, 0.375)
    w_dec = noise(splits[5], (3, 3, 3, 2 * C3, C3), (54 * C3) ** -0.5, 0.078125)
    return dict(inputs=inputs, cotangent=cotangent, w_enc=w_enc, w_bot=w_bot, w_up=w_up, w_dec=w_dec)


def conv_valid(padded, weight):
    result = lax.conv_general_dilated(padded.astype(jnp.float32)[None], weight.astype(jnp.float32), (1, 1, 1), 'VALID', dimension_numbers=('NDHWC', 'DHWIO', 'NDHWC'))
    return result[0]

def pad_all(values):
    return jnp.pad(values, ((1, 1), (1, 1), (1, 1), (0, 0)))

def flip_weight(weight):
    return jnp.transpose(weight[::-1, ::-1, ::-1], (0, 1, 2, 4, 3))

def weight_grad(padded, gradient):
    depth, height, across, outer = gradient.shape
    inner = padded.shape[-1]
    flat = gradient.reshape(-1, outer)
    pieces = []
    for offset in range(27):
        first, second, third = (offset // 9, offset // 3 % 3, offset % 3)
        window = padded[first:first + depth, second:second + height, third:third + across].reshape(-1, inner)
        pieces.append(jnp.dot(window.T, flat, preferred_element_type=jnp.float32))
    return jnp.stack(pieces).reshape(3, 3, 3, inner, outer)

def silu_slope(values):
    sigma = jax.nn.sigmoid(values)
    return sigma * (1.0 + values * (1.0 - sigma))

def reference(inputs, cotangent, w_enc, w_bot, w_up, w_dec):
    padded_in = pad_all(inputs)
    enc_pre = conv_valid(padded_in, w_enc)
    encoded = jax.nn.silu(enc_pre).astype(jnp.bfloat16)
    depth, height, across, chans = encoded.shape
    pooled = encoded.astype(jnp.float32).reshape(depth // 2, 2, height // 2, 2, across // 2, 2, chans).mean(axis=(1, 3, 5)).astype(jnp.bfloat16)
    padded_pool = pad_all(pooled)
    bot_pre = conv_valid(padded_pool, w_bot)
    bottom = jax.nn.silu(bot_pre).astype(jnp.bfloat16)
    lifted = jnp.einsum('ijkc,abdco->iajbkdo', bottom.astype(jnp.float32), w_up.astype(jnp.float32))
    lifted = lifted.reshape(depth, height, across, chans).astype(jnp.bfloat16)
    joined = jnp.concatenate([lifted, encoded], axis=-1)
    padded_join = pad_all(joined)
    dec_pre = conv_valid(padded_join, w_dec)
    decoded = jax.nn.silu(dec_pre).astype(jnp.bfloat16)
    dec_grad = (cotangent.astype(jnp.float32) * silu_slope(dec_pre)).astype(jnp.bfloat16)
    grad_dec = weight_grad(padded_join, dec_grad)
    joined_grad = conv_valid(pad_all(dec_grad), flip_weight(w_dec))
    lift_grad = joined_grad[..., :C3].astype(jnp.bfloat16)
    skip_grad = joined_grad[..., C3:]
    lift_seven = lift_grad.astype(jnp.float32).reshape(depth // 2, 2, height // 2, 2, across // 2, 2, chans)
    grad_up = jnp.einsum('ijkc,iajbkdo->abdco', bottom.astype(jnp.float32), lift_seven)
    back_bottom = jnp.einsum('abdco,iajbkdo->ijkc', w_up.astype(jnp.float32), lift_seven)
    bottom_grad = (back_bottom * silu_slope(bot_pre)).astype(jnp.bfloat16)
    grad_bot = weight_grad(padded_pool, bottom_grad)
    pool_grad = conv_valid(pad_all(bottom_grad), flip_weight(w_bot))
    spread = jnp.broadcast_to(pool_grad[:, None, :, None, :, None, :], (depth // 2, 2, height // 2, 2, across // 2, 2, chans)).reshape(depth, height, across, chans)
    enc_grad = ((skip_grad + spread * 0.125) * silu_slope(enc_pre)).astype(jnp.bfloat16)
    grad_enc = weight_grad(padded_in, enc_grad)
    input_grad = conv_valid(pad_all(enc_grad), flip_weight(w_enc)).astype(jnp.bfloat16)
    return (decoded, input_grad, grad_enc, grad_bot, grad_up, grad_dec, pool_grad)
```

```python
import jax
import jax.numpy as jnp
import numpy as np
from jax import lax
from jax.experimental import pallas as pl
from jax.experimental.pallas import tpu as pltpu
from jax.sharding import PartitionSpec as P

BF = jnp.bfloat16
F32 = jnp.float32
VMEM_LIMIT = 56 * 1024 * 1024


def dot(a, b):
    return jnp.dot(a, b, preferred_element_type=F32)


def call(kernel, outs, scratch, smem_first, *args):
    specs = [pl.BlockSpec(memory_space=pltpu.VMEM)] * len(args)
    if smem_first:
        specs[0] = pl.BlockSpec(memory_space=pltpu.SMEM)
    return pl.pallas_call(
        kernel,
        out_shape=[jax.ShapeDtypeStruct(shape, dtype) for shape, dtype in outs],
        in_specs=specs,
        out_specs=[pl.BlockSpec(memory_space=pltpu.VMEM)] * len(outs),
        scratch_shapes=[pltpu.VMEM(shape, dtype) for shape, dtype in scratch],
        compiler_params=pltpu.CompilerParams(vmem_limit_bytes=VMEM_LIMIT),
    )(*args)


def across(values, width):
    place = lax.broadcasted_iota(jnp.int32, values.shape, 0) & (width - 1)
    count = values.shape[0]
    before = jnp.where(place == 0, 0.0, pltpu.roll(values, 1, 0))
    after = jnp.where(place == width - 1, 0.0, pltpu.roll(values, count - 1, 0))
    return before, after


def fill(store, where_to, values, width):
    before, after = across(values, width)
    shape = (values.shape[0] // width, width, values.shape[1])
    store[0, where_to] = before.astype(BF).reshape(shape)
    store[1, where_to] = values.astype(BF).reshape(shape)
    store[2, where_to] = after.astype(BF).reshape(shape)


def conv_row(store, weight, row, rows):
    width, chans = store.shape[-2:]
    total = None
    for depth in range(3):
        for height in range(3):
            window = jnp.concatenate(
                [
                    store[k, row + depth, height : height + rows].reshape(rows * width, chans)
                    for k in range(3)
                ],
                axis=1,
            )
            part = dot(window, weight[depth * 3 + height])
            total = part if total is None else total + part
    return total


def sigmoid(values):
    return 1.0 / (1.0 + jnp.exp(-values))


def slope_of(values, sigma):
    return sigma * (1.0 + values * (1.0 - sigma))


def fill_input(store, source, double, first, count):
    def step(row, carry):
        cells = source[row + first, first : first + count].reshape(count * 64, 64)
        twice = dot(cells, double[...])
        before, after = across(twice, 64)
        lane = lax.broadcasted_iota(jnp.int32, twice.shape, 1)
        store[0, row] = jnp.where(lane < 64, before, twice).astype(BF).reshape(count, 64, 128)
        store[1, row] = after.astype(BF).reshape(count, 64, 128)
        return carry

    lax.fori_loop(0, count, step, 0)


def encode(pos, xin, double, w_enc, w_bot, mean, encoded, slope, pooled, bot_slope, bottom, twin, pstore):
    fill_input(twin, xin, double, 0, 10)
    high = pos[0] * 4 - 2
    tall = pos[1] * 4 - 2

    def row(d, carry):
        pre = None
        for depth in range(3):
            for height in range(3):
                window = jnp.concatenate(
                    [twin[k, d + depth, height : height + 8].reshape(512, 128) for k in range(2)],
                    axis=1,
                )
                part = dot(window, w_enc[depth * 3 + height])
                pre = part if pre is None else pre + part
        sigma = sigmoid(pre)
        place = lax.broadcasted_iota(jnp.int32, pre.shape, 0) // 64 + tall
        inside = (place >= 0) & (place < 64) & (d + high >= 0) & (d + high < 64)
        encoded[d] = jnp.where(inside, pre * sigma, 0.0).astype(BF).reshape(8, 64, 128)
        bend = jnp.where(inside, slope_of(pre, sigma), 0.0).reshape(8, 64, 128)

        @pl.when((d >= 1) & (d <= 6))
        def _():
            slope[d - 1] = bend[1:7]

        return carry

    lax.fori_loop(0, 8, row, 0)
    for i in range(4):
        cells = []
        for j in range(4):
            block = encoded[2 * i : 2 * i + 2, 2 * j : 2 * j + 2].reshape(256, 128)
            cells.append(dot(mean[...], block).astype(BF).reshape(1, 32, 128))
        line = jnp.concatenate(cells, axis=0)
        pooled[i] = line
        fill(pstore, i, line.reshape(128, 128).astype(F32), 32)
    pre = None
    for depth in range(3):
        for height in range(3):
            window = jnp.concatenate(
                [
                    pstore[k, depth : depth + 2, height : height + 2].reshape(128, 128)
                    for k in range(3)
                ],
                axis=1,
            )
            part = dot(window, w_bot[depth * 3 + height])
            pre = part if pre is None else pre + part
    sigma = sigmoid(pre)
    bottom[...] = (pre * sigma).astype(BF).reshape(2, 2, 32, 256)
    bot_slope[...] = slope_of(pre, sigma)


def decode(
    bottom, encoded, cotangent, bot_slope, stretch, sort, w_up, w_dec, t_dec, t_up,
    decoded, lifted, dec_grad, skip, sorted_lift, bottom_grad,
    jstore, gstore, line,
):
    for i in range(4):
        wide = []
        for j in range(4):
            spread = dot(stretch[...], bottom[i, j]).astype(BF)
            wide.append(jnp.concatenate([spread[:64], spread[64:]], axis=1))
        wide = jnp.concatenate(wide, axis=0)
        for a in range(2):
            pair = [dot(wide, w_up[2 * a + b]).astype(BF).reshape(4, 64, 128) for b in range(2)]
            for j in range(4):
                for b in range(2):
                    line[2 * j + b] = pair[b][j]
            d = 2 * i + a
            if 1 <= d <= 6:
                lifted[d - 1] = line[1:7]
            joined = jnp.concatenate(
                [line[...].reshape(512, 128), encoded[d].reshape(512, 128)], axis=1
            )
            fill(jstore, d, joined.astype(F32), 64)

    def forward(d, carry):
        pre = conv_row(jstore, w_dec, d, 6)
        sigma = sigmoid(pre)
        grad = (cotangent[d].reshape(384, 128).astype(F32) * slope_of(pre, sigma)).astype(BF)
        fill(gstore, d, grad.astype(F32), 64)

        @pl.when((d >= 1) & (d <= 4))
        def _():
            decoded[d - 1] = (pre * sigma).astype(BF).reshape(6, 64, 128)[1:5]
            dec_grad[d - 1] = grad.reshape(6, 64, 128)[1:5]

        return carry

    lax.fori_loop(0, 6, forward, 0)
    pieces = [[], []]
    for d in range(4):
        back = conv_row(gstore, t_dec, d, 4)
        skip[d] = back[:, 128:].astype(BF).reshape(4, 64, 128)
        lift = back[:, :128].astype(BF).reshape(4, 64, 128)
        flat = jnp.concatenate([lift[h] for h in range(4)], axis=1)
        pieces[d // 2].append(dot(sort[...], flat).astype(BF))
    rows = []
    for i in range(2):
        for j in range(2):
            cells = []
            for a in range(2):
                for b in range(2):
                    for c in range(2):
                        h = 2 * j + b
                        cells.append(
                            pieces[i][a][32 * c : 32 * c + 32, 128 * h : 128 * h + 128]
                        )
            rows.append(jnp.concatenate(cells, axis=1))
    rows = jnp.concatenate(rows, axis=0)
    sorted_lift[...] = rows
    back = dot(rows, t_up[...])
    bottom_grad[...] = (back * bot_slope[...]).astype(BF).reshape(2, 2, 32, 256)


def turned(values):
    return jnp.transpose(values.astype(F32)).astype(BF)


def decode_weights(pos, lifted, encoded, dec_grad, keep, send, jstore):
    first = pos[0] % 2 == 0

    def step(d, carry):
        joined = jnp.concatenate(
            [lifted[d].reshape(384, 128), encoded[d + 1, 1:7].reshape(384, 128)], axis=1
        )
        fill(jstore, d, joined.astype(F32), 64)
        return carry

    lax.fori_loop(0, 6, step, 0)
    grad = turned(dec_grad[...].reshape(1024, 128))
    for depth in range(3):
        for height in range(3):
            for k in range(3):
                window = jstore[k, depth : depth + 4, height : height + 4].reshape(1024, 256)
                part = dot(grad, window)
                one, two = part[:, :128], part[:, 128:]
                at = ((depth * 3 + height) * 3 + k) * 128
                keep[:, at : at + 128] = jnp.where(first, one, two).astype(BF)
                send[:, at : at + 128] = jnp.where(first, two, one).astype(BF)


def bottom_weights(pos, sorted_lift, bottom, pooled, bottom_grad, keep, send, pstore):
    first = pos[0] % 2 == 0
    for i in range(4):
        fill(pstore, i, pooled[i].reshape(128, 128).astype(F32), 32)
    grad = turned(bottom_grad[...].reshape(128, 256))
    for depth in range(3):
        for height in range(3):
            window = jnp.concatenate(
                [
                    pstore[k, depth : depth + 2, height : height + 2].reshape(128, 128)
                    for k in range(3)
                ],
                axis=1,
            )
            part = dot(grad, window).reshape(16, 2, 8, 384)
            one, two = part[:, 0].reshape(128, 384), part[:, 1].reshape(128, 384)
            at = (depth * 3 + height) * 384
            keep[:, at : at + 384] = jnp.where(first, one, two).astype(BF)
            send[:, at : at + 384] = jnp.where(first, two, one).astype(BF)
    flat = bottom[...].reshape(128, 256)
    for t in range(8):
        part = dot(turned(sorted_lift[:, t * 128 : t * 128 + 128]), flat)
        one, two = part[:, :128], part[:, 128:]
        at = 3456 + t * 128
        keep[:, at : at + 128] = jnp.where(first, one, two).astype(BF)
        send[:, at : at + 128] = jnp.where(first, two, one).astype(BF)


def encode_back(
    pos, grad, skip, slope, xin, double, spread, t_bot,
    pool_grad, enc_grad, keep, send,
    bstore, twin,
):
    first = pos[0] % 2 == 0
    high = pos[0] * 4 - 1
    tall = pos[1] * 4 - 1
    fill_input(twin, xin, double, 2, 6)

    def step(d, carry):
        fill(bstore, d, grad[d].reshape(192, 256).astype(F32), 32)
        return carry

    lax.fori_loop(0, 6, step, 0)
    for d in range(4):
        back = conv_row(bstore, t_bot, d, 4)
        cells = back.reshape(4, 32, 128)
        if 1 <= d <= 2:
            pool_grad[d - 1] = cells[1:3]
        flat = jnp.concatenate([cells[h] for h in range(4)], axis=1)
        upper = flat.astype(BF)
        lower = (flat - upper.astype(F32)).astype(BF)
        wide = dot(spread[...], jnp.concatenate([upper, lower], axis=0))
        for f in range(6):
            if (f + 1) // 2 != d:
                continue
            for h in range(6):
                at = (h + 1) // 2 * 128
                value = (skip[f, h].astype(F32) + wide[:, at : at + 128]) * slope[f, h]
                enc_grad[f, h] = value.astype(BF)
    turn = turned(enc_grad[1:5, 1:5].reshape(1024, 128))

    lane = lax.broadcasted_iota(jnp.int32, (1024, 128), 1)

    def window(k, m):
        return twin[k, m // 3 : m // 3 + 4, m % 3 : m % 3 + 4].reshape(1024, 128)

    def block(b):
        if b < 9:
            return window(0, b)
        m = 2 * (b - 9)
        if m == 8:
            return window(1, 8)
        return jnp.where(lane < 64, window(1, m), window(1, m + 1))

    for b in range(7):
        part = dot(turn, jnp.concatenate([block(b), block(b + 7)], axis=1))
        one, two = part[:, :128], part[:, 128:]
        keep[:, b * 128 : b * 128 + 128] = jnp.where(first, one, two).astype(BF)
        send[:, b * 128 : b * 128 + 128] = jnp.where(first, two, one).astype(BF)


def input_back(enc_grad, t_enc, input_grad, gstore):
    def step(d, carry):
        fill(gstore, d, enc_grad[d].reshape(384, 128).astype(F32), 64)
        return carry

    lax.fori_loop(0, 6, step, 0)

    def row(d, carry):
        input_grad[d] = conv_row(gstore, t_enc, d, 4).astype(BF).reshape(4, 64, 64)
        return carry

    lax.fori_loop(0, 4, row, 0)


def swapped(low, high, axis):
    count = lax.axis_size(axis)
    even = lax.axis_index(axis) % 2 == 0
    inner = lax.ppermute(jnp.where(even, high, low), axis, [(i, i ^ 1) for i in range(count)])
    pairs = [(i, i + 1) for i in range(1, count - 1, 2)]
    pairs += [(j, i) for i, j in pairs]
    outer = lax.ppermute(jnp.where(even, low, high), axis, pairs)
    return jnp.where(even, outer, inner), jnp.where(even, inner, outer)


def ends(values, dim, width):
    size = values.shape[dim]
    low = lax.slice_in_dim(values, 0, width, axis=dim)
    high = lax.slice_in_dim(values, size - width, size, axis=dim)
    return low, high


def extend(arrays, widths):
    for axis, dim in (("gy", 1), ("gx", 0)):
        slabs = [ends(a, dim, w) for a, w in zip(arrays, widths)]
        shapes = [s[0].shape for s in slabs]
        sizes = [int(np.prod(s)) // 128 for s in shapes]
        low, high = (
            jnp.concatenate([s[e].reshape(-1, 128) for s in slabs], axis=0) for e in range(2)
        )
        low, high = swapped(low, high, axis)
        marks = np.cumsum([0] + sizes)
        arrays = [
            jnp.concatenate(
                [
                    low[marks[n] : marks[n + 1]].reshape(shapes[n]),
                    a,
                    high[marks[n] : marks[n + 1]].reshape(shapes[n]),
                ],
                axis=dim,
            )
            for n, a in enumerate(arrays)
        ]
    return arrays


def exchange(parts):
    keep, send = parts
    got = lax.ppermute(send, "gx", [(i, i ^ 1) for i in range(lax.axis_size("gx"))])
    return (keep.astype(F32) + got.astype(F32)).astype(BF)


def reduced(part, scattered):
    width = part.shape[1]
    depth = lax.axis_size("gx")
    groups = [[2 * a + b for a in range(depth // 2)] for b in range(2)]
    got = lax.all_to_all(part.reshape(16, 8, width), "gy", 0, 0, tiled=True)
    total = got.astype(F32).sum(axis=0).astype(BF)
    if scattered:
        got = lax.all_to_all(
            total.reshape(8, 1, width), "gx", 0, 0, tiled=True, axis_index_groups=groups
        )
        total = got.astype(F32).sum(axis=0).astype(BF)
        total = lax.all_to_all(
            jnp.broadcast_to(total[None], (8, 1, width)), "gx", 0, 0, tiled=True,
            axis_index_groups=groups,
        )
        return total.reshape(8, width)
    got = lax.all_to_all(
        jnp.broadcast_to(total[None], (8, 8, width)), "gx", 0, 0, tiled=True,
        axis_index_groups=groups,
    )
    return got.astype(F32).sum(axis=0).astype(BF)


def both(mine):
    other = lax.ppermute(mine, "gx", [(i, i ^ 1) for i in range(lax.axis_size("gx"))])
    first = lax.axis_index("gx") % 2 == 0
    return jnp.where(first, mine, other), jnp.where(first, other, mine)


def constants():
    w, k = np.arange(64)[:, None], np.arange(32)[None, :]
    double = np.concatenate([np.eye(64), np.eye(64)], axis=1)
    mean = np.tile((w // 2 == k).T * 0.125, (1, 4))
    stretch = np.concatenate([w == 2 * k, w == 2 * k + 1], axis=0)
    sort = np.concatenate([(w == 2 * k).T, (w == 2 * k + 1).T], axis=0)
    spread = np.concatenate([(w // 2 == k) * 0.125] * 2, axis=1)
    return [jnp.asarray(v, BF) for v in (double, mean, stretch, sort, spread)]


def flipped(weight):
    return jnp.transpose(weight[::-1, ::-1, ::-1], (0, 1, 2, 4, 3))


def shards(inputs, cotangent, w_enc, w_bot, w_up, w_dec):
    double, mean, stretch, sort, spread = constants()
    pos = jnp.stack([lax.axis_index("gx"), lax.axis_index("gy")]).astype(jnp.int32)
    k_enc = jnp.pad(w_enc.reshape(9, 192, 128), ((0, 0), (0, 64), (0, 0)))
    k_bot = w_bot.reshape(9, 384, 256)
    k_up = w_up.reshape(4, 512, 128)
    k_dec = w_dec.reshape(9, 768, 128)
    t_dec = flipped(w_dec).reshape(9, 384, 256)
    t_bot = flipped(w_bot).reshape(9, 768, 128)
    t_enc = flipped(w_enc).reshape(9, 384, 64)
    t_up = jnp.transpose(w_up, (0, 1, 2, 4, 3)).reshape(1024, 256)

    (xin,) = extend([inputs], [3])
    encoded, slope, pooled, bot_slope, bottom = call(
        encode,
        [
            ((8, 8, 64, 128), BF),
            ((6, 6, 64, 128), F32),
            ((4, 4, 32, 128), BF),
            ((128, 256), F32),
            ((2, 2, 32, 256), BF),
        ],
        [((2, 10, 10, 64, 128), BF), ((3, 4, 4, 32, 128), BF)],
        True,
        pos, xin, double, k_enc, k_bot, mean,
    )
    wide_bottom, wide_cot = extend([bottom, cotangent], [1, 1])
    decoded, lifted, dec_grad, skip, sorted_lift, bottom_grad = call(
        decode,
        [
            ((4, 4, 64, 128), BF),
            ((6, 6, 64, 128), BF),
            ((4, 4, 64, 128), BF),
            ((4, 4, 64, 128), BF),
            ((128, 1024), BF),
            ((2, 2, 32, 256), BF),
        ],
        [((3, 8, 8, 64, 256), BF), ((3, 6, 6, 64, 128), BF), ((8, 64, 128), BF)],
        False,
        wide_bottom, encoded, wide_cot, bot_slope, stretch, sort, k_up, k_dec, t_dec, t_up,
    )
    wide_grad, wide_skip = extend([bottom_grad, skip], [2, 1])
    part_dec = call(
        decode_weights,
        [((128, 3456), BF), ((128, 3456), BF)],
        [((3, 6, 6, 64, 256), BF)],
        True,
        pos, lifted, encoded, dec_grad,
    )
    part_bot = call(
        bottom_weights,
        [((128, 4480), BF), ((128, 4480), BF)],
        [((3, 4, 4, 32, 128), BF)],
        True,
        pos, sorted_lift, bottom, pooled, bottom_grad,
    )
    pool_grad, enc_grad, keep, send = call(
        encode_back,
        [
            ((2, 2, 32, 128), F32),
            ((6, 6, 64, 128), BF),
            ((128, 896), BF),
            ((128, 896), BF),
        ],
        [((3, 6, 6, 32, 256), BF), ((2, 6, 6, 64, 128), BF)],
        True,
        pos, wide_grad, wide_skip, slope, xin, double, spread, t_bot,
    )
    (input_grad,) = call(
        input_back,
        [((4, 4, 64, 64), BF)],
        [((3, 6, 6, 64, 128), BF)],
        False,
        enc_grad, t_enc,
    )
    sum_main = reduced(jnp.concatenate([exchange(part_dec), exchange(part_bot)], axis=1), True)
    sum_enc = reduced(exchange((keep, send)), False)
    one, two = both(jnp.concatenate([sum_main, sum_enc], axis=1))

    def piece(half, start, size):
        return lax.slice_in_dim(half, start, start + size, axis=1).astype(F32)

    dec = jnp.stack([piece(h, 0, 3456).reshape(8, 27, 128) for h in (one, two)], axis=2)
    grad_dec = jnp.transpose(dec.reshape(8, 27, 256), (1, 2, 0)).reshape(3, 3, 3, 256, 8)
    bot = jnp.concatenate([piece(h, 3456, 3456) for h in (one, two)], axis=0)
    grad_bot = jnp.transpose(bot, (1, 0)).reshape(3, 3, 3, 128, 16)
    up = jnp.stack([piece(h, 6912, 1024).reshape(8, 8, 128) for h in (one, two)], axis=2)
    grad_up = jnp.transpose(up.reshape(8, 8, 256), (1, 2, 0)).reshape(2, 2, 2, 256, 8)
    enc = jnp.concatenate([piece(h, 7936, 896) for h in (one, two)], axis=1)
    front = enc[:, :1152].reshape(8, 9, 2, 64)
    rear = enc[:, 1152 : 1152 + 576].reshape(8, 9, 1, 64)
    grad_enc = jnp.transpose(jnp.concatenate([front, rear], axis=2).reshape(8, 1728), (1, 0))
    grad_enc = grad_enc.reshape(3, 3, 3, 64, 8)
    return (decoded, input_grad, grad_enc, grad_bot, grad_up, grad_dec, pool_grad)


def solution(mesh):
    in_specs = (P("gx", "gy", None, None), P("gx", "gy", None, None), P(), P(), P(), P())
    out_specs = (
        P("gx", "gy", None, None),
        P("gx", "gy", None, None),
        P(None, None, None, None, "gy"),
        P(None, None, None, None, "gy"),
        P(None, None, None, None, "gy"),
        P(None, None, None, None, "gy"),
        P("gx", "gy", None, None),
    )
    return jax.shard_map(shards, mesh=mesh, in_specs=in_specs, out_specs=out_specs, check_vma=False)
```

```python
import jax
import jax.numpy as jnp
import numpy as np
from jax import lax
from jax.experimental import pallas as pl
from jax.experimental.pallas import tpu as pltpu
from jax.sharding import PartitionSpec as P

BF = jnp.bfloat16
F32 = jnp.float32
VMEM_LIMIT = 40 * 1024 * 1024


def dot(a, b):
    return jnp.dot(a, b, preferred_element_type=F32)


def call(kernel, outs, scratch, smem_first, *args):
    specs = [pl.BlockSpec(memory_space=pltpu.VMEM)] * len(args)
    if smem_first:
        specs[0] = pl.BlockSpec(memory_space=pltpu.SMEM)
    return pl.pallas_call(
        kernel,
        out_shape=[jax.ShapeDtypeStruct(shape, dtype) for shape, dtype in outs],
        in_specs=specs,
        out_specs=[pl.BlockSpec(memory_space=pltpu.VMEM)] * len(outs),
        scratch_shapes=[pltpu.VMEM(shape, dtype) for shape, dtype in scratch],
        compiler_params=pltpu.CompilerParams(vmem_limit_bytes=VMEM_LIMIT),
    )(*args)


def dot_nt(a, b):
    return lax.dot_general(a, b, (((1,), (1,)), ((), ())), preferred_element_type=F32)


def before(values, width):
    place = lax.broadcasted_iota(jnp.int32, values.shape, 0) & (width - 1)
    return jnp.where(place == 0, 0.0, pltpu.roll(values, 1, 0))


def after(values, width):
    place = lax.broadcasted_iota(jnp.int32, values.shape, 0) & (width - 1)
    return jnp.where(place == width - 1, 0.0, pltpu.roll(values, values.shape[0] - 1, 0))


def gathered(wide, width, chans):
    taps = [wide[:, k * chans : (k + 1) * chans] for k in range(3)]
    return before(taps[0], width) + taps[1] + after(taps[2], width)


def scattered(wide, width, chans):
    taps = [wide[:, k * chans : (k + 1) * chans] for k in range(3)]
    return after(taps[0], width) + taps[1] + before(taps[2], width)


def tripled(values, width):
    wide = jnp.concatenate([after(values, width), values, before(values, width)], axis=1)
    return jnp.transpose(wide).astype(BF)


def sigmoid(values):
    return 1.0 / (1.0 + jnp.exp(-values))


def slope_of(values, sigma):
    return sigma * (1.0 + values * (1.0 - sigma))


def lanes(parts):
    return jnp.concatenate(parts, axis=1)


def back_row(cells, weight, row, rows):
    width, chans = cells.shape[-2:]
    taps = [(depth, height) for depth in range(3) for height in range(3)]
    window = lanes(
        [
            cells[row + 2 - depth, 2 - height : 2 - height + rows].reshape(rows * width, chans)
            for depth, height in taps
        ]
    )
    inner = weight.shape[3]
    turned = lanes([weight[d, h].reshape(3 * inner, chans) for d, h in taps])
    return scattered(dot_nt(window, turned), width, inner)


def fill_input(store, xin, double):
    lane = lax.broadcasted_iota(jnp.int32, (640, 128), 1)

    def step(row, carry):
        twice = dot(xin[row].reshape(640, 64), double[...])
        follow = pltpu.roll(twice, 576, 0)
        store[row] = jnp.where(lane < 64, twice, follow).astype(BF).reshape(10, 64, 128)
        return carry

    lax.fori_loop(0, 10, step, 0)


def encode(pos, xin, double, w_enc, w_bot, mean, encoded, slope, pooled, bot_slope, bottom, paired, weight):
    fill_input(paired, xin, double)
    high = pos[0] * 4 - 2
    tall = pos[1] * 4 - 2
    for depth in range(3):
        for height in range(3):
            at = depth * 256 + height * 64
            weight[at : at + 64, :] = lanes([w_enc[depth, height, k] for k in range(3)])
        weight[depth * 256 + 192 : depth * 256 + 256, :] = jnp.zeros((64, 384), BF)

    def row(d, carry):
        window = lanes(
            [
                paired[d + depth, 2 * half : 2 * half + 8].reshape(512, 128)
                for depth in range(3)
                for half in range(2)
            ]
        )
        pre = gathered(dot(window, weight[...]), 64, 128)
        sigma = sigmoid(pre)
        place = lax.broadcasted_iota(jnp.int32, pre.shape, 0) // 64 + tall
        inside = (place >= 0) & (place < 64) & (d + high >= 0) & (d + high < 64)
        encoded[d] = jnp.where(inside, pre * sigma, 0.0).astype(BF).reshape(8, 64, 128)
        slope[d] = jnp.where(inside, slope_of(pre, sigma), 0.0).astype(BF).reshape(8, 64, 128)
        return carry

    lax.fori_loop(0, 8, row, 0)
    for i in range(4):
        for j in range(4):
            block = encoded[2 * i : 2 * i + 2, 2 * j : 2 * j + 2].reshape(256, 128)
            pooled[i, j] = dot(mean[...], block).astype(BF)
    window = lanes(
        [
            pooled[depth : depth + 2, height : height + 2].reshape(128, 128)
            for depth in range(3)
            for height in range(3)
        ]
    )
    rows = jnp.concatenate(
        [
            lanes([w_bot[depth, height, k] for k in range(3)])
            for depth in range(3)
            for height in range(3)
        ],
        axis=0,
    )
    pre = gathered(dot(window, rows), 32, 256)
    sigma = sigmoid(pre)
    bottom[...] = (pre * sigma).astype(BF).reshape(2, 2, 32, 256)
    bot_slope[...] = slope_of(pre, sigma)


def decode(
    bottom, encoded, cotangent, bot_slope, stretch, sort, w_up, w_dec,
    decoded, lifted, dec_grad, skip, sorted_lift, bottom_grad,
    lift_all, gstore,
):
    for i in range(4):
        wide = []
        for j in range(4):
            spread = dot(stretch[...], bottom[i, j]).astype(BF)
            wide.append(lanes([spread[:64], spread[64:]]))
        wide = jnp.concatenate(wide, axis=0)
        for a in range(2):
            for b in range(2):
                up = w_up[a, b].reshape(512, 128)
                value = dot(wide, up).astype(BF).reshape(4, 64, 128)
                for j in range(4):
                    lift_all[2 * i + a, 2 * j + b] = value[j]
    lifted[...] = lift_all[1:7, 1:7]

    def forward(d, carry):
        wide = None
        for depth in range(3):
            window = lanes(
                [
                    cells[d + depth, height : height + 6].reshape(384, 128)
                    for height in range(3)
                    for cells in (lift_all, encoded)
                ]
            )
            rows = jnp.concatenate(
                [lanes([w_dec[depth, height, k] for k in range(3)]) for height in range(3)], axis=0
            )
            part = dot(window, rows)
            wide = part if wide is None else wide + part
        pre = gathered(wide, 64, 128)
        sigma = sigmoid(pre)
        grad = (cotangent[d].reshape(384, 128).astype(F32) * slope_of(pre, sigma)).astype(BF)
        gstore[d] = grad.reshape(6, 64, 128)

        @pl.when((d >= 1) & (d <= 4))
        def _():
            decoded[d - 1] = (pre * sigma).astype(BF).reshape(6, 64, 128)[1:5]
            dec_grad[d - 1] = grad.reshape(6, 64, 128)[1:5]

        return carry

    lax.fori_loop(0, 6, forward, 0)
    pieces = [[], []]
    for d in range(4):
        back = back_row(gstore, w_dec, d, 4)
        skip[d] = back[:, 128:].astype(BF).reshape(4, 64, 128)
        lift = back[:, :128].astype(BF).reshape(4, 64, 128)
        flat = lanes([lift[h] for h in range(4)])
        pieces[d // 2].append(dot(sort[...], flat).astype(BF))
    rows = []
    for i in range(2):
        for j in range(2):
            rows.append(
                lanes(
                    [
                        pieces[i][a][32 * c : 32 * c + 32, 128 * (2 * j + b) : 128 * (2 * j + b) + 128]
                        for a in range(2)
                        for b in range(2)
                        for c in range(2)
                    ]
                )
            )
    rows = jnp.concatenate(rows, axis=0)
    sorted_lift[...] = rows
    up = lanes([w_up[a, b, c] for a in range(2) for b in range(2) for c in range(2)])
    back = dot_nt(rows, up)
    bottom_grad[...] = (back * bot_slope[...]).astype(BF).reshape(2, 2, 32, 256)


def put(first, keep, send, at, one, two):
    keep[:, at : at + 128] = jnp.where(first, one, two).astype(BF)
    send[:, at : at + 128] = jnp.where(first, two, one).astype(BF)


def decode_weights(pos, lifted, encoded, dec_grad, keep, send):
    first = pos[0] % 2 == 0
    grad = tripled(dec_grad[...].reshape(1024, 128).astype(F32), 64)
    for depth in range(3):
        for height in range(3):
            window = lanes(
                [
                    lifted[depth : depth + 4, height : height + 4].reshape(1024, 128),
                    encoded[depth + 1 : depth + 5, height + 1 : height + 5].reshape(1024, 128),
                ]
            )
            part = dot(grad, window)
            for k in range(3):
                rows = part[k * 128 : k * 128 + 128]
                at = ((depth * 3 + height) * 3 + k) * 128
                put(first, keep, send, at, rows[:, :128], rows[:, 128:])


def spread_row(row, spread):
    cells = row.reshape(4, 32, 128)
    flat = lanes([cells[h] for h in range(4)])
    upper = flat.astype(BF)
    lower = (flat - upper.astype(F32)).astype(BF)
    return dot(spread[...], jnp.concatenate([upper, lower], axis=0))


def other_weights(
    pos, sorted_lift, bottom, pooled, bottom_grad, skip, slope, xin, double, spread, w_bot,
    keep, send,
    paired, bstore, turned,
):
    first = pos[0] % 2 == 0
    grad = tripled(bottom_grad[...].reshape(128, 256).astype(F32), 32)
    for depth in range(3):
        window = lanes(
            [
                pooled[depth : depth + 2, height : height + 2].reshape(128, 128)
                for height in range(3)
            ]
        )
        part = dot(grad, window)
        for k in range(3):
            rows = part[k * 256 : k * 256 + 256].reshape(16, 2, 8, 384)
            one, two = rows[:, 0].reshape(128, 384), rows[:, 1].reshape(128, 384)
            for height in range(3):
                at = ((depth * 3 + height) * 3 + k) * 128
                cut = slice(height * 128, height * 128 + 128)
                put(first, keep, send, at, one[:, cut], two[:, cut])
    part = dot(
        jnp.transpose(sorted_lift[...].astype(F32)).astype(BF), bottom[...].reshape(128, 256)
    )
    for t in range(8):
        rows = part[t * 128 : t * 128 + 128]
        put(first, keep, send, 3456 + t * 128, rows[:, :128], rows[:, 128:])

    fill_input(paired, xin, double)
    bstore[...] = jnp.zeros((6, 6, 32, 256), BF)
    bstore[2:4, 2:4] = bottom_grad[...]
    for d in range(4):
        wide = spread_row(back_row(bstore, w_bot, d, 4), spread)
        for f in (2 * d, 2 * d + 1):
            cells = []
            for h in range(8):
                value = wide[:, h // 2 * 128 : h // 2 * 128 + 128]
                if 2 <= f < 6 and 2 <= h < 6:
                    value = value + skip[f - 2, h - 2].astype(F32)
                cells.append(value * slope[f, h].astype(F32))
            row = jnp.concatenate(cells, axis=0).astype(BF).astype(F32)
            turned[:, f * 512 : f * 512 + 512] = tripled(row, 64)

    lane = lax.broadcasted_iota(jnp.int32, (4096, 128), 1)

    def window(depth, height):
        return paired[depth : depth + 8, height : height + 8].reshape(4096, 128)

    blocks = [window(0, 0), window(1, 0), window(2, 0)]
    blocks.append(jnp.where(lane < 64, window(0, 2), window(1, 1)))
    blocks.append(jnp.where(lane < 64, window(2, 2), window(2, 1)))
    parts = []
    for n in (0, 2, 4):
        part = dot(turned[...], lanes(blocks[n : n + 2]))
        parts += [part[:, m * 128 : m * 128 + 128] for m in range(part.shape[1] // 128)]
    cut = [[part[k * 128 : k * 128 + 128] for k in range(3)] for part in parts]
    small = lax.broadcasted_iota(jnp.int32, (128, 128), 1)
    final = cut[0] + cut[1] + cut[2] + cut[3]
    final += [jnp.where(small < 64, cut[4][0], cut[4][1]), cut[4][2]]
    for n in range(7):
        put(first, keep, send, 4480 + n * 128, final[n], final[n + 7])


def encode_back(grad, skip, slope, spread, w_bot, w_enc, pool_grad, input_grad, gstore):
    for d in range(4):
        row = back_row(grad, w_bot, d, 4)
        if 1 <= d <= 2:
            pool_grad[d - 1] = row.reshape(4, 32, 128)[1:3]
        wide = spread_row(row, spread)
        for f in range(6):
            if (f + 1) // 2 != d:
                continue
            for h in range(6):
                at = (h + 1) // 2 * 128
                value = skip[f, h].astype(F32) + wide[:, at : at + 128]
                gstore[f, h] = (value * slope[f + 1, h + 1].astype(F32)).astype(BF)
    for d in range(4):
        input_grad[d] = back_row(gstore, w_enc, d, 4).astype(BF).reshape(4, 64, 64)


def swapped(low, high, axis):
    count = lax.axis_size(axis)
    even = lax.axis_index(axis) % 2 == 0
    inner = lax.ppermute(jnp.where(even, high, low), axis, [(i, i ^ 1) for i in range(count)])
    pairs = [(i, i + 1) for i in range(1, count - 1, 2)]
    pairs += [(j, i) for i, j in pairs]
    outer = lax.ppermute(jnp.where(even, low, high), axis, pairs)
    return jnp.where(even, outer, inner), jnp.where(even, inner, outer)


def ends(values, dim, width):
    size = values.shape[dim]
    low = lax.slice_in_dim(values, 0, width, axis=dim)
    high = lax.slice_in_dim(values, size - width, size, axis=dim)
    return low, high


def extend(arrays, widths):
    for axis, dim in (("gy", 1), ("gx", 0)):
        slabs = [ends(a, dim, w) for a, w in zip(arrays, widths)]
        shapes = [s[0].shape for s in slabs]
        sizes = [int(np.prod(s)) // 128 for s in shapes]
        low, high = (
            jnp.concatenate([s[e].reshape(-1, 128) for s in slabs], axis=0) for e in range(2)
        )
        low, high = swapped(low, high, axis)
        marks = np.cumsum([0] + sizes)
        arrays = [
            jnp.concatenate(
                [
                    low[marks[n] : marks[n + 1]].reshape(shapes[n]),
                    a,
                    high[marks[n] : marks[n + 1]].reshape(shapes[n]),
                ],
                axis=dim,
            )
            for n, a in enumerate(arrays)
        ]
    return arrays


def exchange(parts):
    keep, send = parts
    got = lax.ppermute(send, "gx", [(i, i ^ 1) for i in range(lax.axis_size("gx"))])
    return (keep.astype(F32) + got.astype(F32)).astype(BF)


def reduced(part):
    width = part.shape[1]
    depth = lax.axis_size("gx")
    groups = [[2 * a + b for a in range(depth // 2)] for b in range(2)]
    got = lax.all_to_all(part.reshape(16, 8, width), "gy", 0, 0, tiled=True)
    total = got.astype(F32).sum(axis=0).astype(BF)
    got = lax.all_to_all(
        total.reshape(8, 1, width), "gx", 0, 0, tiled=True, axis_index_groups=groups
    )
    total = got.astype(F32).sum(axis=0).astype(BF)
    total = lax.all_to_all(
        jnp.broadcast_to(total[None], (8, 1, width)), "gx", 0, 0, tiled=True,
        axis_index_groups=groups,
    )
    return total.reshape(8, width)


def both(mine):
    other = lax.ppermute(mine, "gx", [(i, i ^ 1) for i in range(lax.axis_size("gx"))])
    first = lax.axis_index("gx") % 2 == 0
    return jnp.where(first, mine, other), jnp.where(first, other, mine)


def constants():
    w, k = np.arange(64)[:, None], np.arange(32)[None, :]
    double = np.concatenate([np.eye(64), np.eye(64)], axis=1)
    mean = np.tile((w // 2 == k).T * 0.125, (1, 4))
    stretch = np.concatenate([w == 2 * k, w == 2 * k + 1], axis=0)
    sort = np.concatenate([(w == 2 * k).T, (w == 2 * k + 1).T], axis=0)
    spread = np.concatenate([(w // 2 == k) * 0.125] * 2, axis=1)
    return [jnp.asarray(v, BF) for v in (double, mean, stretch, sort, spread)]


def shards(inputs, cotangent, w_enc, w_bot, w_up, w_dec):
    double, mean, stretch, sort, spread = constants()
    pos = jnp.stack([lax.axis_index("gx"), lax.axis_index("gy")]).astype(jnp.int32)
    (xin,) = extend([inputs], [3])
    encoded, slope, pooled, bot_slope, bottom = call(
        encode,
        [
            ((8, 8, 64, 128), BF),
            ((8, 8, 64, 128), BF),
            ((4, 4, 32, 128), BF),
            ((128, 256), F32),
            ((2, 2, 32, 256), BF),
        ],
        [((10, 10, 64, 128), BF), ((768, 384), BF)],
        True,
        pos, xin, double, w_enc, w_bot, mean,
    )
    wide_bottom, wide_cot = extend([bottom, cotangent], [1, 1])
    decoded, lifted, dec_grad, skip, sorted_lift, bottom_grad = call(
        decode,
        [
            ((4, 4, 64, 128), BF),
            ((6, 6, 64, 128), BF),
            ((4, 4, 64, 128), BF),
            ((4, 4, 64, 128), BF),
            ((128, 1024), BF),
            ((2, 2, 32, 256), BF),
        ],
        [((8, 8, 64, 128), BF), ((6, 6, 64, 128), BF)],
        False,
        wide_bottom, encoded, wide_cot, bot_slope, stretch, sort, w_up, w_dec,
    )
    part_dec = call(
        decode_weights,
        [((128, 3456), BF), ((128, 3456), BF)],
        [],
        True,
        pos, lifted, encoded, dec_grad,
    )
    part_rest = call(
        other_weights,
        [((128, 5376), BF), ((128, 5376), BF)],
        [((10, 10, 64, 128), BF), ((6, 6, 32, 256), BF), ((384, 4096), BF)],
        True,
        pos, sorted_lift, bottom, pooled, bottom_grad, skip, slope, xin, double, spread, w_bot,
    )
    part = jnp.concatenate([exchange(part_dec), exchange(part_rest)], axis=1)
    wide_grad, wide_skip = extend([bottom_grad, skip], [2, 1])
    pool_grad, input_grad = call(
        encode_back,
        [((2, 2, 32, 128), F32), ((4, 4, 64, 64), BF)],
        [((6, 6, 64, 128), BF)],
        False,
        wide_grad, wide_skip, slope, spread, w_bot, w_enc,
    )
    one, two = both(reduced(part))

    def piece(half, start, size):
        return lax.slice_in_dim(half, start, start + size, axis=1).astype(F32)

    dec = jnp.stack([piece(h, 0, 3456).reshape(8, 27, 128) for h in (one, two)], axis=2)
    grad_dec = jnp.transpose(dec.reshape(8, 27, 256), (1, 2, 0)).reshape(3, 3, 3, 256, 8)
    bot = jnp.concatenate([piece(h, 3456, 3456) for h in (one, two)], axis=0)
    grad_bot = jnp.transpose(bot, (1, 0)).reshape(3, 3, 3, 128, 16)
    up = jnp.stack([piece(h, 6912, 1024).reshape(8, 8, 128) for h in (one, two)], axis=2)
    grad_up = jnp.transpose(up.reshape(8, 8, 256), (1, 2, 0)).reshape(2, 2, 2, 256, 8)
    enc = jnp.concatenate([piece(h, 7936, 896) for h in (one, two)], axis=1).reshape(8, 14, 2, 64)
    near = jnp.transpose(enc[:, :9].reshape(8, 3, 3, 2, 64), (0, 1, 3, 2, 4))
    far = jnp.transpose(enc[:, 9:12], (0, 2, 1, 3))
    last = jnp.stack([enc[:, 12, 0], enc[:, 12, 1], enc[:, 13, 0]], axis=1)
    far = jnp.concatenate([far, last[:, None]], axis=1)
    grad_enc = jnp.concatenate([near, far[:, :, None]], axis=2)
    grad_enc = jnp.transpose(grad_enc, (1, 2, 3, 4, 0))
    return (decoded, input_grad, grad_enc, grad_bot, grad_up, grad_dec, pool_grad)


def solution(mesh):
    in_specs = (P("gx", "gy", None, None), P("gx", "gy", None, None), P(), P(), P(), P())
    out_specs = (
        P("gx", "gy", None, None),
        P("gx", "gy", None, None),
        P(None, None, None, None, "gy"),
        P(None, None, None, None, "gy"),
        P(None, None, None, None, "gy"),
        P(None, None, None, None, "gy"),
        P("gx", "gy", None, None),
    )
    return jax.shard_map(shards, mesh=mesh, in_specs=in_specs, out_specs=out_specs, check_vma=False)
```

```python
import jax
import jax.numpy as jnp
import numpy as np
from jax import lax
from jax.experimental import pallas as pl
from jax.experimental.pallas import tpu as pltpu
from jax.sharding import PartitionSpec as P

BF = jnp.bfloat16
F32 = jnp.float32
VMEM_LIMIT = 56 * 1024 * 1024


def dot(a, b):
    return jnp.dot(a, b, preferred_element_type=F32)


def call(kernel, outs, scratch, pos, *args, behind=()):
    held = [pl.BlockSpec(memory_space=pltpu.VMEM)] * len(args)
    waits = [pl.BlockSpec(memory_space=pl.ANY)] * len(behind)

    def run(place, *refs):
        return kernel(place, *refs[: len(args)], *refs[len(args) + len(behind) :])

    return pl.pallas_call(
        run,
        out_shape=[jax.ShapeDtypeStruct(shape, dtype) for shape, dtype in outs],
        in_specs=[pl.BlockSpec(memory_space=pltpu.SMEM)] + held + waits,
        out_specs=[pl.BlockSpec(memory_space=pltpu.VMEM)] * len(outs),
        scratch_shapes=[pltpu.VMEM(shape, dtype) for shape, dtype in scratch],
        compiler_params=pltpu.CompilerParams(vmem_limit_bytes=VMEM_LIMIT),
        name=kernel.__name__,
    )(pos, *args, *behind)


def stacked(parts):
    return jnp.concatenate(parts, axis=0)


def sides(pos, axis, inner, outer):
    even = pos[axis] % 2 == 0

    def low(*at):
        return jnp.where(even, outer[at], inner[at])

    def high(*at):
        return jnp.where(even, inner[at], outer[at])

    return low, high


def give(pos, axis, inner, outer, low, high, at=slice(None)):
    even = pos[axis] % 2 == 0
    inner[at] = jnp.where(even, high, low)
    outer[at] = jnp.where(even, low, high)


def dot_nt(a, b):
    return lax.dot_general(a, b, (((1,), (1,)), ((), ())), preferred_element_type=F32)


def before(values, width):
    place = lax.broadcasted_iota(jnp.int32, values.shape, 0) & (width - 1)
    return jnp.where(place == 0, 0.0, pltpu.roll(values, 1, 0))


def after(values, width):
    place = lax.broadcasted_iota(jnp.int32, values.shape, 0) & (width - 1)
    return jnp.where(place == width - 1, 0.0, pltpu.roll(values, values.shape[0] - 1, 0))


def gathered(wide, width, chans):
    taps = [wide[:, k * chans : (k + 1) * chans] for k in range(3)]
    return before(taps[0], width) + taps[1] + after(taps[2], width)


def scattered(wide, width, chans):
    taps = [wide[:, k * chans : (k + 1) * chans] for k in range(3)]
    return after(taps[0], width) + taps[1] + before(taps[2], width)


def tripled(values, width):
    wide = jnp.concatenate([after(values, width), values, before(values, width)], axis=1)
    return jnp.transpose(wide).astype(BF)


def sigmoid(values):
    return 1.0 / (1.0 + jnp.exp(-values))


def slope_of(values, sigma):
    return sigma * (1.0 + values * (1.0 - sigma))


def lanes(parts):
    return jnp.concatenate(parts, axis=1)


def back_row(cells, weight, row, rows):
    width, chans = cells.shape[-2:]
    taps = [(depth, height) for depth in range(3) for height in range(3)]
    window = lanes(
        [
            cells[row + 2 - depth, 2 - height : 2 - height + rows].reshape(rows * width, chans)
            for depth, height in taps
        ]
    )
    inner = weight.shape[3]
    turned = lanes([weight[d, h].reshape(3 * inner, chans) for d, h in taps])
    return scattered(dot_nt(window, turned), width, inner)


def input_slabs(pos, own, g_in, g_out, s_in, s_out):
    low, high = sides(pos, 1, g_in, g_out)
    edges = []
    for d in (0, 1):
        cut = slice(d, d + 3)
        edges.append(jnp.concatenate([low(cut), own[cut], high(cut)], axis=1))
    give(pos, 0, s_in, s_out, edges[0], edges[1])


def fill_input(pos, store, own, g_in, g_out, x_in, x_out):
    low, high = sides(pos, 1, g_in, g_out)
    under, over = sides(pos, 0, x_in, x_out)
    lane = lax.broadcasted_iota(jnp.int32, (320, 128), 1)
    for d in range(10):
        if d < 3:
            line = under(d)
        elif d < 7:
            line = jnp.concatenate([low(d - 3), own[d - 3], high(d - 3)], axis=0)
        else:
            line = over(d - 7)
        wide = pltpu.roll(line.reshape(384, 128).astype(F32), 64, 1)
        odd = jnp.where(lane < 64, wide[:320], wide[64:]).astype(BF).reshape(5, 64, 128)
        for m in range(6):
            if m < 5:
                store[d, 2 * m + 1] = odd[m]
            store[d, 2 * m] = line[m]


def encode(
    pos, own, g_in, g_out, x_in, x_out, cotangent, w_enc, w_bot, mean,
    paired, encoded, slope, pooled, bot_slope, bottom, s_in, s_out,
    weight,
):
    fill_input(pos, paired, own, g_in, g_out, x_in, x_out)
    high = pos[0] * 4 - 2
    tall = pos[1] * 4 - 2
    for depth in range(3):
        for height in range(3):
            at = depth * 256 + height * 64
            weight[at : at + 64, :] = lanes([w_enc[depth, height, k] for k in range(3)])
        weight[depth * 256 + 192 : depth * 256 + 256, :] = jnp.zeros((64, 384), BF)

    def row(d, carry):
        window = lanes(
            [
                paired[d + depth, 2 * half + 1 : 2 * half + 9].reshape(512, 128)
                for depth in range(3)
                for half in range(2)
            ]
        )
        pre = gathered(dot(window, weight[...]), 64, 128)
        sigma = sigmoid(pre)
        place = lax.broadcasted_iota(jnp.int32, pre.shape, 0) // 64 + tall
        inside = (place >= 0) & (place < 64) & (d + high >= 0) & (d + high < 64)
        encoded[d] = jnp.where(inside, pre * sigma, 0.0).astype(BF).reshape(8, 64, 128)
        slope[d] = jnp.where(inside, slope_of(pre, sigma), 0.0).astype(BF).reshape(8, 64, 128)
        return carry

    lax.fori_loop(0, 8, row, 0)
    for i in range(4):
        for j in range(4):
            block = encoded[2 * i : 2 * i + 2, 2 * j : 2 * j + 2].reshape(256, 128)
            pooled[i, j] = dot(mean[...], block).astype(BF)
    window = lanes(
        [
            pooled[depth : depth + 2, height : height + 2].reshape(128, 128)
            for depth in range(3)
            for height in range(3)
        ]
    )
    rows = jnp.concatenate(
        [
            lanes([w_bot[depth, height, k] for k in range(3)])
            for depth in range(3)
            for height in range(3)
        ],
        axis=0,
    )
    pre = gathered(dot(window, rows), 32, 256)
    sigma = sigmoid(pre)
    value = (pre * sigma).astype(BF).reshape(2, 2, 32, 256)
    bottom[...] = value
    bot_slope[...] = slope_of(pre, sigma)
    edges = []
    for h, at in ((0, 0), (1, 3)):
        row = value[:, h].reshape(64, 256)
        edges.append(stacked([cotangent[:, at].reshape(256, 128), row[:, :128], row[:, 128:]]))
    give(pos, 1, s_in, s_out, edges[0], edges[1])


def bottom_slabs(pos, bottom, cotangent, g_in, g_out, s_in, s_out):
    low, high = sides(pos, 1, g_in, g_out)
    edges = []
    for d, b in ((0, 0), (3, 1)):
        cot = slice(64 * d, 64 * d + 64)
        parts = [low(cot), cotangent[d].reshape(256, 128), high(cot)]
        for half in range(2):
            cut = slice(256 + 64 * half + 32 * b, 256 + 64 * half + 32 * b + 32)
            lane = slice(128 * half, 128 * half + 128)
            parts += [low(cut), bottom[b, 0, :, lane], bottom[b, 1, :, lane], high(cut)]
        edges.append(stacked(parts))
    give(pos, 0, s_in, s_out, edges[0], edges[1])


def fill_bottom(pos, wide_bottom, wide_cot, bottom, cotangent, g_in, g_out, x_in, x_out):
    low, high = sides(pos, 1, g_in, g_out)
    for d in range(4):
        cut = slice(64 * d, 64 * d + 64)
        wide_cot[d + 1, 0] = low(cut)
        wide_cot[d + 1, 1:5] = cotangent[d]
        wide_cot[d + 1, 5] = high(cut)
    for b in range(2):
        wide_bottom[b + 1, 1:3] = bottom[b]
        for half in range(2):
            cut = slice(256 + 64 * half + 32 * b, 256 + 64 * half + 32 * b + 32)
            lane = slice(128 * half, 128 * half + 128)
            wide_bottom[b + 1, 0, :, lane] = low(cut)
            wide_bottom[b + 1, 3, :, lane] = high(cut)
    for side, d, b in zip(sides(pos, 0, x_in, x_out), (0, 5), (0, 3)):
        wide_cot[d] = side(slice(0, 384)).reshape(6, 64, 128)
        for half in range(2):
            cut = slice(384 + 128 * half, 512 + 128 * half)
            lane = slice(128 * half, 128 * half + 128)
            wide_bottom[b, :, :, lane] = side(cut).reshape(4, 32, 128)


def decode(
    pos, own_bottom, own_cot, g_in, g_out, x_in, x_out,
    encoded, bot_slope, stretch, sort, w_up, w_dec,
    decoded, lifted, dec_grad, skip, sorted_lift, bottom_grad, s_in, s_out,
    lift_all, gstore, bottom, cotangent,
):
    fill_bottom(pos, bottom, cotangent, own_bottom, own_cot, g_in, g_out, x_in, x_out)
    for i in range(4):
        wide = []
        for j in range(4):
            spread = dot(stretch[...], bottom[i, j]).astype(BF)
            wide.append(lanes([spread[:64], spread[64:]]))
        wide = jnp.concatenate(wide, axis=0)
        for a in range(2):
            for b in range(2):
                up = w_up[a, b].reshape(512, 128)
                value = dot(wide, up).astype(BF).reshape(4, 64, 128)
                for j in range(4):
                    lift_all[2 * i + a, 2 * j + b] = value[j]
    lifted[...] = lift_all[1:7, 1:7]

    def forward(d, carry):
        wide = None
        for depth in range(3):
            window = lanes(
                [
                    cells[d + depth, height : height + 6].reshape(384, 128)
                    for height in range(3)
                    for cells in (lift_all, encoded)
                ]
            )
            rows = jnp.concatenate(
                [lanes([w_dec[depth, height, k] for k in range(3)]) for height in range(3)], axis=0
            )
            part = dot(window, rows)
            wide = part if wide is None else wide + part
        pre = gathered(wide, 64, 128)
        sigma = sigmoid(pre)
        grad = (cotangent[d].reshape(384, 128).astype(F32) * slope_of(pre, sigma)).astype(BF)
        gstore[d] = grad.reshape(6, 64, 128)

        @pl.when((d >= 1) & (d <= 4))
        def _():
            decoded[d - 1] = (pre * sigma).astype(BF).reshape(6, 64, 128)[1:5]
            dec_grad[d - 1] = grad.reshape(6, 64, 128)[1:5]

        return carry

    lax.fori_loop(0, 6, forward, 0)
    pieces = [[], []]
    for d in range(4):
        back = back_row(gstore, w_dec, d, 4)
        skip[d] = back[:, 128:].astype(BF).reshape(4, 64, 128)
        lift = back[:, :128].astype(BF).reshape(4, 64, 128)
        flat = lanes([lift[h] for h in range(4)])
        pieces[d // 2].append(dot(sort[...], flat).astype(BF))
    rows = []
    for i in range(2):
        for j in range(2):
            rows.append(
                lanes(
                    [
                        pieces[i][a][32 * c : 32 * c + 32, 128 * (2 * j + b) : 128 * (2 * j + b) + 128]
                        for a in range(2)
                        for b in range(2)
                        for c in range(2)
                    ]
                )
            )
    rows = jnp.concatenate(rows, axis=0)
    sorted_lift[...] = rows
    up = lanes([w_up[a, b, c] for a in range(2) for b in range(2) for c in range(2)])
    back = dot_nt(rows, up)
    grad = (back * bot_slope[...]).astype(BF)
    bottom_grad[...] = grad.reshape(2, 2, 32, 256)
    give(pos, 1, s_in, s_out, skip[:, 0].reshape(256, 128), skip[:, 3].reshape(256, 128), slice(0, 256))
    for half in range(2):
        cut = slice(256 + 128 * half, 384 + 128 * half)
        s_in[cut] = grad[:, 128 * half : 128 * half + 128]
        s_out[cut] = grad[:, 128 * half : 128 * half + 128]


def grad_slabs(pos, grad, skip, g_in, g_out, s_in, s_out):
    low, high = sides(pos, 1, g_in, g_out)
    edges = []
    for d in (0, 3):
        cut = slice(64 * d, 64 * d + 64)
        edges.append(stacked([low(cut), skip[d].reshape(256, 128), high(cut)]))
    give(pos, 0, s_in, s_out, edges[0], edges[1], slice(0, 384))
    for half in range(2):
        lane = slice(128 * half, 128 * half + 128)
        for d in range(2):
            cut = slice(256 + 128 * half + 64 * d, 256 + 128 * half + 64 * d + 64)
            line = stacked([low(cut), grad[d, 0, :, lane], grad[d, 1, :, lane], high(cut)])
            at = 384 + 384 * half + 192 * d
            s_in[at : at + 192] = line
            s_out[at : at + 192] = line


def fill_grad(pos, wide_grad, wide_skip, grad, skip, g_in, g_out, x_in, x_out):
    low, high = sides(pos, 1, g_in, g_out)
    for d in range(4):
        cut = slice(64 * d, 64 * d + 64)
        wide_skip[d + 1, 0] = low(cut)
        wide_skip[d + 1, 1:5] = skip[d]
        wide_skip[d + 1, 5] = high(cut)
    for b in range(2):
        wide_grad[b + 2, 2:4] = grad[b]
        for half in range(2):
            cut = slice(256 + 128 * half + 64 * b, 256 + 128 * half + 64 * b + 64)
            lane = slice(128 * half, 128 * half + 128)
            wide_grad[b + 2, 0:2, :, lane] = low(cut).reshape(2, 32, 128)
            wide_grad[b + 2, 4:6, :, lane] = high(cut).reshape(2, 32, 128)
    for side, d, b in zip(sides(pos, 0, x_in, x_out), (0, 5), (0, 4)):
        wide_skip[d] = side(slice(0, 384)).reshape(6, 64, 128)
        for half in range(2):
            cut = slice(384 + 384 * half, 768 + 384 * half)
            lane = slice(128 * half, 128 * half + 128)
            wide_grad[b : b + 2, :, :, lane] = side(cut).reshape(2, 6, 32, 128)


def put(first, keep, send, at, one, two):
    keep[:, at : at + 128] = jnp.where(first, one, two).astype(BF)
    send[:, at : at + 128] = jnp.where(first, two, one).astype(BF)


def decode_weights(pos, lifted, encoded, dec_grad, keep, send):
    first = pos[0] % 2 == 0
    grad = tripled(dec_grad[...].reshape(1024, 128).astype(F32), 64)
    for depth in range(3):
        for height in range(3):
            window = lanes(
                [
                    lifted[depth : depth + 4, height : height + 4].reshape(1024, 128),
                    encoded[depth + 1 : depth + 5, height + 1 : height + 5].reshape(1024, 128),
                ]
            )
            part = dot(grad, window)
            for k in range(3):
                rows = part[k * 128 : k * 128 + 128]
                at = ((depth * 3 + height) * 3 + k) * 128
                put(first, keep, send, at, rows[:, :128], rows[:, 128:])


def spread_row(row, spread):
    cells = row.reshape(4, 32, 128)
    flat = lanes([cells[h] for h in range(4)])
    upper = flat.astype(BF)
    lower = (flat - upper.astype(F32)).astype(BF)
    return dot(spread[...], jnp.concatenate([upper, lower], axis=0))


def other_weights(
    pos, sorted_lift, bottom, pooled, bottom_grad, skip, slope, paired, spread, w_bot,
    keep, send,
    bstore, turned,
):
    first = pos[0] % 2 == 0
    grad = tripled(bottom_grad[...].reshape(128, 256).astype(F32), 32)
    for depth in range(3):
        window = lanes(
            [
                pooled[depth : depth + 2, height : height + 2].reshape(128, 128)
                for height in range(3)
            ]
        )
        part = dot(grad, window)
        for k in range(3):
            rows = part[k * 256 : k * 256 + 256].reshape(16, 2, 8, 384)
            one, two = rows[:, 0].reshape(128, 384), rows[:, 1].reshape(128, 384)
            for height in range(3):
                at = ((depth * 3 + height) * 3 + k) * 128
                cut = slice(height * 128, height * 128 + 128)
                put(first, keep, send, at, one[:, cut], two[:, cut])
    part = dot(
        jnp.transpose(sorted_lift[...].astype(F32)).astype(BF), bottom[...].reshape(128, 256)
    )
    for t in range(8):
        rows = part[t * 128 : t * 128 + 128]
        put(first, keep, send, 3456 + t * 128, rows[:, :128], rows[:, 128:])

    bstore[...] = jnp.zeros((6, 6, 32, 256), BF)
    bstore[2:4, 2:4] = bottom_grad[...]
    for d in range(4):
        wide = spread_row(back_row(bstore, w_bot, d, 4), spread)
        for f in (2 * d, 2 * d + 1):
            cells = []
            for h in range(8):
                value = wide[:, h // 2 * 128 : h // 2 * 128 + 128]
                if 2 <= f < 6 and 2 <= h < 6:
                    value = value + skip[f - 2, h - 2].astype(F32)
                cells.append(value * slope[f, h].astype(F32))
            row = jnp.concatenate(cells, axis=0).astype(BF).astype(F32)
            turned[:, f * 512 : f * 512 + 512] = tripled(row, 64)

    lane = lax.broadcasted_iota(jnp.int32, (4096, 128), 1)

    def window(depth, height):
        return paired[depth : depth + 8, height + 1 : height + 9].reshape(4096, 128)

    blocks = [window(0, 0), window(1, 0), window(2, 0)]
    blocks.append(jnp.where(lane < 64, window(0, 2), window(1, 1)))
    blocks.append(jnp.where(lane < 64, window(2, 2), window(2, 1)))
    parts = []
    for n in (0, 2, 4):
        part = dot(turned[...], lanes(blocks[n : n + 2]))
        parts += [part[:, m * 128 : m * 128 + 128] for m in range(part.shape[1] // 128)]
    cut = [[part[k * 128 : k * 128 + 128] for k in range(3)] for part in parts]
    small = lax.broadcasted_iota(jnp.int32, (128, 128), 1)
    final = cut[0] + cut[1] + cut[2] + cut[3]
    final += [jnp.where(small < 64, cut[4][0], cut[4][1]), cut[4][2]]
    for n in range(7):
        put(first, keep, send, 4480 + n * 128, final[n], final[n + 7])


def encode_back(
    pos, own_grad, own_skip, g_in, g_out, x_in, x_out, slope, spread, w_bot, w_enc,
    pool_grad, input_grad,
    gstore, grad, skip,
):
    fill_grad(pos, grad, skip, own_grad, own_skip, g_in, g_out, x_in, x_out)
    for d in range(4):
        row = back_row(grad, w_bot, d, 4)
        if 1 <= d <= 2:
            pool_grad[d - 1] = row.reshape(4, 32, 128)[1:3]
        wide = spread_row(row, spread)
        for f in range(6):
            if (f + 1) // 2 != d:
                continue
            for h in range(6):
                at = (h + 1) // 2 * 128
                value = skip[f, h].astype(F32) + wide[:, at : at + 128]
                gstore[f, h] = (value * slope[f + 1, h + 1].astype(F32)).astype(BF)
    for d in range(4):
        input_grad[d] = back_row(gstore, w_enc, d, 4).astype(BF).reshape(4, 64, 64)


def swap(inner, outer, axis):
    count = lax.axis_size(axis)
    pairs = [(i, i + 1) for i in range(1, count - 1, 2)]
    pairs += [(j, i) for i, j in pairs]
    got = lax.ppermute(inner, axis, [(i, i ^ 1) for i in range(count)])
    return got, lax.ppermute(outer, axis, pairs)


def exchange(parts):
    keep, send = parts
    got = lax.ppermute(send, "gx", [(i, i ^ 1) for i in range(lax.axis_size("gx"))])
    return (keep.astype(F32) + got.astype(F32)).astype(BF)


def reduced(part):
    width = part.shape[1]
    depth = lax.axis_size("gx")
    groups = [[2 * a + b for a in range(depth // 2)] for b in range(2)]
    got = lax.all_to_all(part.reshape(16, 8, width), "gy", 0, 0, tiled=True)
    total = got.astype(F32).sum(axis=0).astype(BF)
    got = lax.all_to_all(
        total.reshape(8, 1, width), "gx", 0, 0, tiled=True, axis_index_groups=groups
    )
    total = got.astype(F32).sum(axis=0).astype(BF)
    total = lax.all_to_all(
        jnp.broadcast_to(total[None], (8, 1, width)), "gx", 0, 0, tiled=True,
        axis_index_groups=groups,
    )
    return total.reshape(8, width)


def both(mine):
    other = lax.ppermute(mine, "gx", [(i, i ^ 1) for i in range(lax.axis_size("gx"))])
    first = lax.axis_index("gx") % 2 == 0
    return jnp.where(first, mine, other), jnp.where(first, other, mine)


def constants():
    w, k = np.arange(64)[:, None], np.arange(32)[None, :]
    mean = np.tile((w // 2 == k).T * 0.125, (1, 4))
    stretch = np.concatenate([w == 2 * k, w == 2 * k + 1], axis=0)
    sort = np.concatenate([(w == 2 * k).T, (w == 2 * k + 1).T], axis=0)
    spread = np.concatenate([(w // 2 == k) * 0.125] * 2, axis=1)
    return [jnp.asarray(v, BF) for v in (mean, stretch, sort, spread)]


def shards(inputs, cotangent, w_enc, w_bot, w_up, w_dec):
    mean, stretch, sort, spread = constants()
    pos = jnp.stack([lax.axis_index("gx"), lax.axis_index("gy")]).astype(jnp.int32)
    own = jnp.concatenate([inputs[:, 0::2], inputs[:, 1::2]], axis=3)
    near = swap(own, own, "gy")
    slabs = call(input_slabs, [((3, 6, 64, 128), BF)] * 2, [], pos, own, *near)
    near += swap(*slabs, "gx")
    paired, encoded, slope, pooled, bot_slope, bottom, *slabs = call(
        encode,
        [
            ((10, 11, 64, 128), BF),
            ((8, 8, 64, 128), BF),
            ((8, 8, 64, 128), BF),
            ((4, 4, 32, 128), BF),
            ((128, 256), F32),
            ((2, 2, 32, 256), BF),
        ]
        + [((384, 128), BF)] * 2,
        [((768, 384), BF)],
        pos, own, *near, cotangent, w_enc, w_bot, mean,
    )
    near = swap(*slabs, "gy")
    slabs = call(bottom_slabs, [((640, 128), BF)] * 2, [], pos, bottom, cotangent, *near)
    near += swap(*slabs, "gx")
    decoded, lifted, dec_grad, skip, sorted_lift, bottom_grad, *slabs = call(
        decode,
        [
            ((4, 4, 64, 128), BF),
            ((6, 6, 64, 128), BF),
            ((4, 4, 64, 128), BF),
            ((4, 4, 64, 128), BF),
            ((128, 1024), BF),
            ((2, 2, 32, 256), BF),
        ]
        + [((512, 128), BF)] * 2,
        [
            ((8, 8, 64, 128), BF),
            ((6, 6, 64, 128), BF),
            ((4, 4, 32, 256), BF),
            ((6, 6, 64, 128), BF),
        ],
        pos, bottom, cotangent, *near, encoded, bot_slope, stretch, sort, w_up, w_dec,
    )
    near = swap(*slabs, "gy")
    part_rest = call(
        other_weights,
        [((128, 5376), BF), ((128, 5376), BF)],
        [((6, 6, 32, 256), BF), ((384, 4096), BF)],
        pos, sorted_lift, bottom, pooled, bottom_grad, skip, slope, paired, spread, w_bot,
    )
    slabs = call(
        grad_slabs, [((1152, 128), BF)] * 2, [], pos, bottom_grad, skip, *near,
        behind=part_rest[:1],
    )
    near += swap(*slabs, "gx")
    part_dec = call(
        decode_weights,
        [((128, 3456), BF), ((128, 3456), BF)],
        [],
        pos, lifted, encoded, dec_grad,
        behind=slabs[:1],
    )
    part = jnp.concatenate([exchange(part_dec), exchange(part_rest)], axis=1)
    pool_grad, input_grad = call(
        encode_back,
        [((2, 2, 32, 128), F32), ((4, 4, 64, 64), BF)],
        [((6, 6, 64, 128), BF), ((6, 6, 32, 256), BF), ((6, 6, 64, 128), BF)],
        pos, bottom_grad, skip, *near, slope, spread, w_bot, w_enc,
        behind=part_dec[:1],
    )
    one, two = both(reduced(part))

    def piece(half, start, size):
        return lax.slice_in_dim(half, start, start + size, axis=1).astype(F32)

    dec = jnp.stack([piece(h, 0, 3456).reshape(8, 27, 128) for h in (one, two)], axis=2)
    grad_dec = jnp.transpose(dec.reshape(8, 27, 256), (1, 2, 0)).reshape(3, 3, 3, 256, 8)
    bot = jnp.concatenate([piece(h, 3456, 3456) for h in (one, two)], axis=0)
    grad_bot = jnp.transpose(bot, (1, 0)).reshape(3, 3, 3, 128, 16)
    up = jnp.stack([piece(h, 6912, 1024).reshape(8, 8, 128) for h in (one, two)], axis=2)
    grad_up = jnp.transpose(up.reshape(8, 8, 256), (1, 2, 0)).reshape(2, 2, 2, 256, 8)
    enc = jnp.concatenate([piece(h, 7936, 896) for h in (one, two)], axis=1).reshape(8, 14, 2, 64)
    near = jnp.transpose(enc[:, :9].reshape(8, 3, 3, 2, 64), (0, 1, 3, 2, 4))
    far = jnp.transpose(enc[:, 9:12], (0, 2, 1, 3))
    last = jnp.stack([enc[:, 12, 0], enc[:, 12, 1], enc[:, 13, 0]], axis=1)
    far = jnp.concatenate([far, last[:, None]], axis=1)
    grad_enc = jnp.concatenate([near, far[:, :, None]], axis=2)
    grad_enc = jnp.transpose(grad_enc, (1, 2, 3, 4, 0))
    return (decoded, input_grad, grad_enc, grad_bot, grad_up, grad_dec, pool_grad)


def solution(mesh):
    in_specs = (P("gx", "gy", None, None), P("gx", "gy", None, None), P(), P(), P(), P())
    out_specs = (
        P("gx", "gy", None, None),
        P("gx", "gy", None, None),
        P(None, None, None, None, "gy"),
        P(None, None, None, None, "gy"),
        P(None, None, None, None, "gy"),
        P(None, None, None, None, "gy"),
        P("gx", "gy", None, None),
    )
    return jax.shard_map(shards, mesh=mesh, in_specs=in_specs, out_specs=out_specs, check_vma=False)
```

```python
import jax
import jax.numpy as jnp
import numpy as np
from jax import lax
from jax.experimental import pallas as pl
from jax.experimental.pallas import tpu as pltpu
from jax.sharding import PartitionSpec as P

BF = jnp.bfloat16
F32 = jnp.float32
VMEM_LIMIT = 24 * 1024 * 1024


def dot(a, b):
    return jnp.dot(a, b, preferred_element_type=F32)


def call(kernel, outs, scratch, pos, *args, behind=()):
    held = [pl.BlockSpec(memory_space=pltpu.VMEM)] * len(args)
    waits = [pl.BlockSpec(memory_space=pl.ANY)] * len(behind)

    def run(place, *refs):
        return kernel(place, *refs[: len(args)], *refs[len(args) + len(behind) :])

    return pl.pallas_call(
        run,
        out_shape=[jax.ShapeDtypeStruct(shape, dtype) for shape, dtype in outs],
        in_specs=[pl.BlockSpec(memory_space=pltpu.SMEM)] + held + waits,
        out_specs=[pl.BlockSpec(memory_space=pltpu.VMEM)] * len(outs),
        scratch_shapes=[pltpu.VMEM(shape, dtype) for shape, dtype in scratch],
        compiler_params=pltpu.CompilerParams(vmem_limit_bytes=VMEM_LIMIT),
        name=kernel.__name__,
    )(pos, *args, *behind)


def stacked(parts):
    return jnp.concatenate(parts, axis=0)


def sides(pos, axis, inner, outer):
    even = pos[axis] % 2 == 0

    def low(*at):
        return jnp.where(even, outer[at], inner[at])

    def high(*at):
        return jnp.where(even, inner[at], outer[at])

    return low, high


def give(pos, axis, inner, outer, low, high, at=slice(None)):
    even = pos[axis] % 2 == 0
    inner[at] = jnp.where(even, high, low)
    outer[at] = jnp.where(even, low, high)


def dot_nt(a, b):
    return lax.dot_general(a, b, (((1,), (1,)), ((), ())), preferred_element_type=F32)


def before(values, width):
    place = lax.broadcasted_iota(jnp.int32, values.shape, 0) & (width - 1)
    return jnp.where(place == 0, 0.0, pltpu.roll(values, 1, 0))


def after(values, width):
    place = lax.broadcasted_iota(jnp.int32, values.shape, 0) & (width - 1)
    return jnp.where(place == width - 1, 0.0, pltpu.roll(values, values.shape[0] - 1, 0))


def gathered(wide, width, chans):
    taps = [wide[:, k * chans : (k + 1) * chans] for k in range(3)]
    return before(taps[0], width) + taps[1] + after(taps[2], width)


def scattered(wide, width, chans):
    taps = [wide[:, k * chans : (k + 1) * chans] for k in range(3)]
    return after(taps[0], width) + taps[1] + before(taps[2], width)


def tripled(values, width):
    wide = jnp.concatenate([after(values, width), values, before(values, width)], axis=1)
    return jnp.transpose(wide).astype(BF)


def sigmoid(values):
    return 0.5 * jnp.tanh(0.5 * values) + 0.5


def slope_of(values, sigma):
    return sigma * (1.0 + values * (1.0 - sigma))


def lanes(parts):
    return jnp.concatenate(parts, axis=1)


def back_row(cells, weight, row, rows):
    width, chans = cells.shape[-2:]
    taps = [(depth, height) for depth in range(3) for height in range(3)]
    window = lanes(
        [
            cells[row + 2 - depth, 2 - height : 2 - height + rows].reshape(rows * width, chans)
            for depth, height in taps
        ]
    )
    inner = weight.shape[3]
    turned = lanes([weight[d, h].reshape(3 * inner, chans) for d, h in taps])
    return scattered(dot_nt(window, turned), width, inner)


def input_slabs(pos, own, g_in, g_out, s_in, s_out):
    low, high = sides(pos, 1, g_in, g_out)
    edges = []
    for d in (0, 1):
        cut = slice(d, d + 3)
        edges.append(jnp.concatenate([low(cut), own[cut], high(cut)], axis=1))
    give(pos, 0, s_in, s_out, edges[0], edges[1])


def fill_input(pos, store, own, g_in, g_out, x_in, x_out):
    low, high = sides(pos, 1, g_in, g_out)
    under, over = sides(pos, 0, x_in, x_out)
    lane = lax.broadcasted_iota(jnp.int32, (320, 128), 1)
    for d in range(10):
        if d < 3:
            line = under(d)
        elif d < 7:
            line = jnp.concatenate([low(d - 3), own[d - 3], high(d - 3)], axis=0)
        else:
            line = over(d - 7)
        wide = pltpu.roll(line.reshape(384, 128).astype(F32), 64, 1)
        odd = jnp.where(lane < 64, wide[:320], wide[64:]).astype(BF).reshape(5, 64, 128)
        for m in range(6):
            if m < 5:
                store[d, 2 * m + 1] = odd[m]
            store[d, 2 * m] = line[m]


def encode(
    pos, own, g_in, g_out, x_in, x_out, cotangent, w_enc, w_bot, mean,
    paired, encoded, slope, pooled, bot_slope, bottom, s_in, s_out,
    weight,
):
    fill_input(pos, paired, own, g_in, g_out, x_in, x_out)
    high = pos[0] * 4 - 2
    tall = pos[1] * 4 - 2
    for depth in range(3):
        for height in range(3):
            at = depth * 256 + height * 64
            weight[at : at + 64, :] = lanes([w_enc[depth, height, k] for k in range(3)])
        weight[depth * 256 + 192 : depth * 256 + 256, :] = jnp.zeros((64, 384), BF)

    def row(d, carry):
        window = lanes(
            [
                paired[d + depth, 2 * half + 1 : 2 * half + 9].reshape(512, 128)
                for depth in range(3)
                for half in range(2)
            ]
        )
        pre = gathered(dot(window, weight[...]), 64, 128)
        sigma = sigmoid(pre)
        place = lax.broadcasted_iota(jnp.int32, pre.shape, 0) // 64 + tall
        inside = (place >= 0) & (place < 64) & (d + high >= 0) & (d + high < 64)
        encoded[d] = jnp.where(inside, pre * sigma, 0.0).astype(BF).reshape(8, 64, 128)
        slope[d] = jnp.where(inside, slope_of(pre, sigma), 0.0).astype(BF).reshape(8, 64, 128)
        return carry

    lax.fori_loop(0, 8, row, 0)
    for i in range(4):
        for j in range(4):
            block = encoded[2 * i : 2 * i + 2, 2 * j : 2 * j + 2].reshape(256, 128)
            pooled[i, j] = dot(mean[...], block).astype(BF)
    window = lanes(
        [
            pooled[depth : depth + 2, height : height + 2].reshape(128, 128)
            for depth in range(3)
            for height in range(3)
        ]
    )
    rows = jnp.concatenate(
        [
            lanes([w_bot[depth, height, k] for k in range(3)])
            for depth in range(3)
            for height in range(3)
        ],
        axis=0,
    )
    pre = gathered(dot(window, rows), 32, 256)
    sigma = sigmoid(pre)
    value = (pre * sigma).astype(BF).reshape(2, 2, 32, 256)
    bottom[...] = value
    bot_slope[...] = slope_of(pre, sigma)
    edges = []
    for h, at in ((0, 0), (1, 3)):
        row = value[:, h].reshape(64, 256)
        edges.append(stacked([cotangent[:, at].reshape(256, 128), row[:, :128], row[:, 128:]]))
    give(pos, 1, s_in, s_out, edges[0], edges[1])


def bottom_slabs(pos, bottom, cotangent, g_in, g_out, s_in, s_out):
    low, high = sides(pos, 1, g_in, g_out)
    edges = []
    for d, b in ((0, 0), (3, 1)):
        cot = slice(64 * d, 64 * d + 64)
        parts = [low(cot), cotangent[d].reshape(256, 128), high(cot)]
        for half in range(2):
            cut = slice(256 + 64 * half + 32 * b, 256 + 64 * half + 32 * b + 32)
            lane = slice(128 * half, 128 * half + 128)
            parts += [low(cut), bottom[b, 0, :, lane], bottom[b, 1, :, lane], high(cut)]
        edges.append(stacked(parts))
    give(pos, 0, s_in, s_out, edges[0], edges[1])


def fill_bottom(pos, wide_bottom, wide_cot, bottom, cotangent, g_in, g_out, x_in, x_out):
    low, high = sides(pos, 1, g_in, g_out)
    for d in range(4):
        cut = slice(64 * d, 64 * d + 64)
        wide_cot[d + 1, 0] = low(cut)
        wide_cot[d + 1, 1:5] = cotangent[d]
        wide_cot[d + 1, 5] = high(cut)
    for b in range(2):
        wide_bottom[b + 1, 1:3] = bottom[b]
        for half in range(2):
            cut = slice(256 + 64 * half + 32 * b, 256 + 64 * half + 32 * b + 32)
            lane = slice(128 * half, 128 * half + 128)
            wide_bottom[b + 1, 0, :, lane] = low(cut)
            wide_bottom[b + 1, 3, :, lane] = high(cut)
    for side, d, b in zip(sides(pos, 0, x_in, x_out), (0, 5), (0, 3)):
        wide_cot[d] = side(slice(0, 384)).reshape(6, 64, 128)
        for half in range(2):
            cut = slice(384 + 128 * half, 512 + 128 * half)
            lane = slice(128 * half, 128 * half + 128)
            wide_bottom[b, :, :, lane] = side(cut).reshape(4, 32, 128)


def decode(
    pos, own_bottom, own_cot, g_in, g_out, x_in, x_out,
    encoded, bot_slope, stretch, sort, w_up, w_dec,
    decoded, lifted, dec_grad, skip, sorted_lift, bottom_grad, s_in, s_out,
    lift_all, gstore, bottom, cotangent,
):
    fill_bottom(pos, bottom, cotangent, own_bottom, own_cot, g_in, g_out, x_in, x_out)
    for i in range(4):
        wide = []
        for j in range(4):
            spread = dot(stretch[...], bottom[i, j]).astype(BF)
            wide.append(lanes([spread[:64], spread[64:]]))
        wide = jnp.concatenate(wide, axis=0)
        for a in range(2):
            for b in range(2):
                up = w_up[a, b].reshape(512, 128)
                value = dot(wide, up).astype(BF).reshape(4, 64, 128)
                for j in range(4):
                    lift_all[2 * i + a, 2 * j + b] = value[j]
    lifted[...] = lift_all[1:7, 1:7]

    def forward(d, carry):
        wide = None
        for depth in range(3):
            window = lanes(
                [
                    cells[d + depth, height : height + 6].reshape(384, 128)
                    for height in range(3)
                    for cells in (lift_all, encoded)
                ]
            )
            rows = jnp.concatenate(
                [lanes([w_dec[depth, height, k] for k in range(3)]) for height in range(3)], axis=0
            )
            part = dot(window, rows)
            wide = part if wide is None else wide + part
        pre = gathered(wide, 64, 128)
        sigma = sigmoid(pre)
        grad = (cotangent[d].reshape(384, 128).astype(F32) * slope_of(pre, sigma)).astype(BF)
        gstore[d] = grad.reshape(6, 64, 128)

        @pl.when((d >= 1) & (d <= 4))
        def _():
            decoded[d - 1] = (pre * sigma).astype(BF).reshape(6, 64, 128)[1:5]
            dec_grad[d - 1] = grad.reshape(6, 64, 128)[1:5]

        return carry

    lax.fori_loop(0, 6, forward, 0)
    pieces = [[], []]
    for d in range(4):
        back = back_row(gstore, w_dec, d, 4)
        skip[d] = back[:, 128:].astype(BF).reshape(4, 64, 128)
        lift = back[:, :128].astype(BF).reshape(4, 64, 128)
        flat = lanes([lift[h] for h in range(4)])
        pieces[d // 2].append(dot(sort[...], flat).astype(BF))
    rows = []
    for i in range(2):
        for j in range(2):
            rows.append(
                lanes(
                    [
                        pieces[i][a][32 * c : 32 * c + 32, 128 * (2 * j + b) : 128 * (2 * j + b) + 128]
                        for a in range(2)
                        for b in range(2)
                        for c in range(2)
                    ]
                )
            )
    rows = jnp.concatenate(rows, axis=0)
    sorted_lift[...] = rows
    up = lanes([w_up[a, b, c] for a in range(2) for b in range(2) for c in range(2)])
    back = dot_nt(rows, up)
    grad = (back * bot_slope[...]).astype(BF)
    bottom_grad[...] = grad.reshape(2, 2, 32, 256)
    give(pos, 1, s_in, s_out, skip[:, 0].reshape(256, 128), skip[:, 3].reshape(256, 128), slice(0, 256))
    for half in range(2):
        cut = slice(256 + 128 * half, 384 + 128 * half)
        s_in[cut] = grad[:, 128 * half : 128 * half + 128]
        s_out[cut] = grad[:, 128 * half : 128 * half + 128]


def grad_slabs(pos, grad, skip, g_in, g_out, s_in, s_out):
    low, high = sides(pos, 1, g_in, g_out)
    edges = []
    for d in (0, 3):
        cut = slice(64 * d, 64 * d + 64)
        edges.append(stacked([low(cut), skip[d].reshape(256, 128), high(cut)]))
    give(pos, 0, s_in, s_out, edges[0], edges[1], slice(0, 384))
    for half in range(2):
        lane = slice(128 * half, 128 * half + 128)
        for d in range(2):
            cut = slice(256 + 128 * half + 64 * d, 256 + 128 * half + 64 * d + 64)
            line = stacked([low(cut), grad[d, 0, :, lane], grad[d, 1, :, lane], high(cut)])
            at = 384 + 384 * half + 192 * d
            s_in[at : at + 192] = line
            s_out[at : at + 192] = line


def fill_grad(pos, wide_grad, wide_skip, grad, skip, g_in, g_out, x_in, x_out):
    low, high = sides(pos, 1, g_in, g_out)
    for d in range(4):
        cut = slice(64 * d, 64 * d + 64)
        wide_skip[d + 1, 0] = low(cut)
        wide_skip[d + 1, 1:5] = skip[d]
        wide_skip[d + 1, 5] = high(cut)
    for b in range(2):
        wide_grad[b + 2, 2:4] = grad[b]
        for half in range(2):
            cut = slice(256 + 128 * half + 64 * b, 256 + 128 * half + 64 * b + 64)
            lane = slice(128 * half, 128 * half + 128)
            wide_grad[b + 2, 0:2, :, lane] = low(cut).reshape(2, 32, 128)
            wide_grad[b + 2, 4:6, :, lane] = high(cut).reshape(2, 32, 128)
    for side, d, b in zip(sides(pos, 0, x_in, x_out), (0, 5), (0, 4)):
        wide_skip[d] = side(slice(0, 384)).reshape(6, 64, 128)
        for half in range(2):
            cut = slice(384 + 384 * half, 768 + 384 * half)
            lane = slice(128 * half, 128 * half + 128)
            wide_grad[b : b + 2, :, :, lane] = side(cut).reshape(2, 6, 32, 128)


def put(first, keep, send, at, one, two):
    keep[:, at : at + 128] = jnp.where(first, one, two).astype(BF)
    send[:, at : at + 128] = jnp.where(first, two, one).astype(BF)


def decode_weights(pos, lifted, encoded, dec_grad, keep, send):
    first = pos[0] % 2 == 0
    grad = tripled(dec_grad[...].reshape(1024, 128).astype(F32), 64)
    for depth in range(3):
        for height in range(3):
            window = lanes(
                [
                    lifted[depth : depth + 4, height : height + 4].reshape(1024, 128),
                    encoded[depth + 1 : depth + 5, height + 1 : height + 5].reshape(1024, 128),
                ]
            )
            part = dot(grad, window)
            for k in range(3):
                rows = part[k * 128 : k * 128 + 128]
                at = ((depth * 3 + height) * 3 + k) * 128
                put(first, keep, send, at, rows[:, :128], rows[:, 128:])


def spread_row(row, spread):
    cells = row.reshape(4, 32, 128)
    flat = lanes([cells[h] for h in range(4)])
    upper = flat.astype(BF)
    lower = (flat - upper.astype(F32)).astype(BF)
    return dot(spread[...], jnp.concatenate([upper, lower], axis=0))


def other_weights(
    pos, sorted_lift, bottom, pooled, bottom_grad, skip, slope, paired, spread, w_bot,
    keep, send,
    bstore, turned,
):
    first = pos[0] % 2 == 0
    grad = tripled(bottom_grad[...].reshape(128, 256).astype(F32), 32)
    for depth in range(3):
        window = lanes(
            [
                pooled[depth : depth + 2, height : height + 2].reshape(128, 128)
                for height in range(3)
            ]
        )
        part = dot(grad, window)
        for k in range(3):
            rows = part[k * 256 : k * 256 + 256].reshape(16, 2, 8, 384)
            one, two = rows[:, 0].reshape(128, 384), rows[:, 1].reshape(128, 384)
            for height in range(3):
                at = ((depth * 3 + height) * 3 + k) * 128
                cut = slice(height * 128, height * 128 + 128)
                put(first, keep, send, at, one[:, cut], two[:, cut])
    part = dot(
        jnp.transpose(sorted_lift[...].astype(F32)).astype(BF), bottom[...].reshape(128, 256)
    )
    for t in range(8):
        rows = part[t * 128 : t * 128 + 128]
        put(first, keep, send, 3456 + t * 128, rows[:, :128], rows[:, 128:])

    bstore[...] = jnp.zeros((6, 6, 32, 256), BF)
    bstore[2:4, 2:4] = bottom_grad[...]
    for d in range(4):
        wide = spread_row(back_row(bstore, w_bot, d, 4), spread)
        for f in (2 * d, 2 * d + 1):
            cells = []
            for h in range(8):
                value = wide[:, h // 2 * 128 : h // 2 * 128 + 128]
                if 2 <= f < 6 and 2 <= h < 6:
                    value = value + skip[f - 2, h - 2].astype(F32)
                cells.append(value * slope[f, h].astype(F32))
            row = jnp.concatenate(cells, axis=0).astype(BF).astype(F32)
            turned[:, f * 512 : f * 512 + 512] = tripled(row, 64)

    lane = lax.broadcasted_iota(jnp.int32, (4096, 128), 1)

    def window(depth, height):
        return paired[depth : depth + 8, height + 1 : height + 9].reshape(4096, 128)

    blocks = [window(0, 0), window(1, 0), window(2, 0)]
    blocks.append(jnp.where(lane < 64, window(0, 2), window(1, 1)))
    blocks.append(jnp.where(lane < 64, window(2, 2), window(2, 1)))
    parts = []
    for n in (0, 2, 4):
        part = dot(turned[...], lanes(blocks[n : n + 2]))
        parts += [part[:, m * 128 : m * 128 + 128] for m in range(part.shape[1] // 128)]
    cut = [[part[k * 128 : k * 128 + 128] for k in range(3)] for part in parts]
    small = lax.broadcasted_iota(jnp.int32, (128, 128), 1)
    final = cut[0] + cut[1] + cut[2] + cut[3]
    final += [jnp.where(small < 64, cut[4][0], cut[4][1]), cut[4][2]]
    for n in range(7):
        put(first, keep, send, 4480 + n * 128, final[n], final[n + 7])


def encode_back(
    pos, own_grad, own_skip, g_in, g_out, x_in, x_out, slope, spread, w_bot, w_enc,
    pool_grad, input_grad,
    gstore, grad, skip,
):
    fill_grad(pos, grad, skip, own_grad, own_skip, g_in, g_out, x_in, x_out)
    for d in range(4):
        row = back_row(grad, w_bot, d, 4)
        if 1 <= d <= 2:
            pool_grad[d - 1] = row.reshape(4, 32, 128)[1:3]
        wide = spread_row(row, spread)
        for f in range(6):
            if (f + 1) // 2 != d:
                continue
            for h in range(6):
                at = (h + 1) // 2 * 128
                value = skip[f, h].astype(F32) + wide[:, at : at + 128]
                gstore[f, h] = (value * slope[f + 1, h + 1].astype(F32)).astype(BF)
    for d in range(4):
        input_grad[d] = back_row(gstore, w_enc, d, 4).astype(BF).reshape(4, 64, 64)


def swap(inner, outer, axis):
    count = lax.axis_size(axis)
    pairs = [(i, i + 1) for i in range(1, count - 1, 2)]
    pairs += [(j, i) for i, j in pairs]
    got = lax.ppermute(inner, axis, [(i, i ^ 1) for i in range(count)])
    return got, lax.ppermute(outer, axis, pairs)


def exchange(parts):
    keep, send = parts
    got = lax.ppermute(send, "gx", [(i, i ^ 1) for i in range(lax.axis_size("gx"))])
    return (keep.astype(F32) + got.astype(F32)).astype(BF)


def add_heights(pos, parts, chunks):
    for n in range(72):
        if n < 69:
            cut = slice(128 * n, 128 * n + 128)
            total = parts[0, :, cut].astype(F32)
            for j in range(1, 16):
                total = total + parts[j, :, cut].astype(F32)
        else:
            total = jnp.zeros((8, 128), F32)
        at = 128 * (n % 9)
        chunks[n // 9, :, at : at + 128] = total.astype(BF)


def add_depths(pos, parts, copies):
    total = parts[0].astype(F32)
    for j in range(1, 8):
        total = total + parts[j].astype(F32)
    total = total.astype(BF)
    for j in range(8):
        copies[j] = total


def finish(pos, mine, other, grad_enc, grad_bot, grad_up, grad_dec):
    first = pos[0] % 2 == 0

    def block(n):
        cut = slice(128 * (n % 9), 128 * (n % 9) + 128)
        left, right = mine[n // 9, :, cut].astype(F32), other[n // 9, :, cut].astype(F32)
        return jnp.where(first, left, right), jnp.where(first, right, left)

    for t in range(27):
        grad_dec[t, :, :128], grad_dec[t, :, 128:] = block(t)
        grad_bot[t, :8], grad_bot[t, 8:] = block(27 + t)
    for t in range(8):
        grad_up[t, :, :128], grad_up[t, :, 128:] = block(54 + t)
    pairs = [block(62 + n) for n in range(7)]
    pieces = [p[0] for p in pairs] + [p[1] for p in pairs]

    def tap(depth, height, k):
        return (depth * 3 + height) * 3 + k

    for k in range(3):
        for depth in range(3):
            piece = pieces[depth * 3 + k]
            grad_enc[tap(depth, 0, k)] = piece[:, :64]
            grad_enc[tap(depth, 1, k)] = piece[:, 64:]
        grad_enc[tap(0, 2, k)] = pieces[9 + k][:, :64]
        grad_enc[tap(1, 2, k)] = pieces[9 + k][:, 64:]
    grad_enc[tap(2, 2, 0)] = pieces[12][:, :64]
    grad_enc[tap(2, 2, 1)] = pieces[12][:, 64:]
    grad_enc[tap(2, 2, 2)] = pieces[13][:, :64]


def reduced(pos, part, behind):
    groups = [[2 * a + b for a in range(8)] for b in range(2)]
    got = lax.all_to_all(part.reshape(16, 8, 8832), "gy", 0, 0, tiled=True)
    (chunks,) = call(add_heights, [((8, 8, 1152), BF)], [], pos, got, behind=behind)
    got = lax.all_to_all(chunks, "gx", 0, 0, tiled=True, axis_index_groups=groups)
    (copies,) = call(add_depths, [((8, 8, 1152), BF)], [], pos, got)
    return lax.all_to_all(copies, "gx", 0, 0, tiled=True, axis_index_groups=groups)


def constants():
    w, k = np.arange(64)[:, None], np.arange(32)[None, :]
    mean = np.tile((w // 2 == k).T * 0.125, (1, 4))
    stretch = np.concatenate([w == 2 * k, w == 2 * k + 1], axis=0)
    sort = np.concatenate([(w == 2 * k).T, (w == 2 * k + 1).T], axis=0)
    spread = np.concatenate([(w // 2 == k) * 0.125] * 2, axis=1)
    return [jnp.asarray(v, BF) for v in (mean, stretch, sort, spread)]


def shards(inputs, cotangent, w_enc, w_bot, w_up, w_dec):
    mean, stretch, sort, spread = constants()
    pos = jnp.stack([lax.axis_index("gx"), lax.axis_index("gy")]).astype(jnp.int32)
    own = jnp.concatenate([inputs[:, 0::2], inputs[:, 1::2]], axis=3)
    near = swap(own, own, "gy")
    slabs = call(input_slabs, [((3, 6, 64, 128), BF)] * 2, [], pos, own, *near)
    near += swap(*slabs, "gx")
    paired, encoded, slope, pooled, bot_slope, bottom, *slabs = call(
        encode,
        [
            ((10, 11, 64, 128), BF),
            ((8, 8, 64, 128), BF),
            ((8, 8, 64, 128), BF),
            ((4, 4, 32, 128), BF),
            ((128, 256), F32),
            ((2, 2, 32, 256), BF),
        ]
        + [((384, 128), BF)] * 2,
        [((768, 384), BF)],
        pos, own, *near, cotangent, w_enc, w_bot, mean,
    )
    near = swap(*slabs, "gy")
    slabs = call(bottom_slabs, [((640, 128), BF)] * 2, [], pos, bottom, cotangent, *near)
    near += swap(*slabs, "gx")
    decoded, lifted, dec_grad, skip, sorted_lift, bottom_grad, *slabs = call(
        decode,
        [
            ((4, 4, 64, 128), BF),
            ((6, 6, 64, 128), BF),
            ((4, 4, 64, 128), BF),
            ((4, 4, 64, 128), BF),
            ((128, 1024), BF),
            ((2, 2, 32, 256), BF),
        ]
        + [((512, 128), BF)] * 2,
        [
            ((8, 8, 64, 128), BF),
            ((6, 6, 64, 128), BF),
            ((4, 4, 32, 256), BF),
            ((6, 6, 64, 128), BF),
        ],
        pos, bottom, cotangent, *near, encoded, bot_slope, stretch, sort, w_up, w_dec,
    )
    near = swap(*slabs, "gy")
    part_rest = call(
        other_weights,
        [((128, 5376), BF), ((128, 5376), BF)],
        [((6, 6, 32, 256), BF), ((384, 4096), BF)],
        pos, sorted_lift, bottom, pooled, bottom_grad, skip, slope, paired, spread, w_bot,
    )
    slabs = call(
        grad_slabs, [((1152, 128), BF)] * 2, [], pos, bottom_grad, skip, *near,
        behind=part_rest[:1],
    )
    near += swap(*slabs, "gx")
    part_dec = call(
        decode_weights,
        [((128, 3456), BF), ((128, 3456), BF)],
        [],
        pos, lifted, encoded, dec_grad,
        behind=slabs[:1],
    )
    part = jnp.concatenate([exchange(part_dec), exchange(part_rest)], axis=1)
    pool_grad, input_grad = call(
        encode_back,
        [((2, 2, 32, 128), F32), ((4, 4, 64, 64), BF)],
        [((6, 6, 64, 128), BF), ((6, 6, 32, 256), BF), ((6, 6, 64, 128), BF)],
        pos, bottom_grad, skip, *near, slope, spread, w_bot, w_enc,
        behind=part_dec[:1],
    )
    mine = reduced(pos, part, (input_grad,))
    other = lax.ppermute(mine, "gx", [(i, i ^ 1) for i in range(lax.axis_size("gx"))])
    grads = call(
        finish,
        [((27, 8, 64), F32), ((27, 16, 128), F32), ((8, 8, 256), F32), ((27, 8, 256), F32)],
        [],
        pos, mine, other,
    )
    grad_enc, grad_bot, grad_up, grad_dec = (
        jnp.transpose(grad, (0, 2, 1)).reshape(*shape, grad.shape[2], grad.shape[1])
        for grad, shape in zip(grads, ((3, 3, 3), (3, 3, 3), (2, 2, 2), (3, 3, 3)))
    )
    return (decoded, input_grad, grad_enc, grad_bot, grad_up, grad_dec, pool_grad)


def solution(mesh):
    in_specs = (P("gx", "gy", None, None), P("gx", "gy", None, None), P(), P(), P(), P())
    out_specs = (
        P("gx", "gy", None, None),
        P("gx", "gy", None, None),
        P(None, None, None, None, "gy"),
        P(None, None, None, None, "gy"),
        P(None, None, None, None, "gy"),
        P(None, None, None, None, "gy"),
        P("gx", "gy", None, None),
    )
    return jax.shard_map(shards, mesh=mesh, in_specs=in_specs, out_specs=out_specs, check_vma=False)
```

```python
import jax
import jax.numpy as jnp
import numpy as np
from jax import lax
from jax.experimental import pallas as pl
from jax.experimental.pallas import tpu as pltpu
from jax.sharding import PartitionSpec as P

BF = jnp.bfloat16
F32 = jnp.float32
VMEM_LIMIT = 24 * 1024 * 1024


def dot(a, b):
    return jnp.dot(a, b, preferred_element_type=F32)


def call(kernel, outs, scratch, pos, *args, far=(), behind=()):
    held = [pl.BlockSpec(memory_space=pltpu.VMEM)] * len(args)
    waits = [pl.BlockSpec(memory_space=pltpu.HBM)] * len(far)
    waits += [pl.BlockSpec(memory_space=pl.ANY)] * len(behind)
    count = len(args)

    def run(place, *refs):
        own = refs[count + len(waits) :]
        copies = []
        for n in range(len(far)):
            room = own[len(own) - 1 - len(far) + n]
            copies.append(pltpu.make_async_copy(refs[count + n], room, own[-1].at[n]))
            copies[-1].start()

        def fetched(n):
            copies[n].wait()
            return own[len(own) - 1 - len(far) + n]

        extra = (fetched,) if far else ()
        kept = own[: len(own) - 1 - len(far)] if far else own
        return kernel(place, *extra, *refs[:count], *kept)

    rooms = [pltpu.VMEM(shape, dtype) for shape, dtype in scratch]
    if far:
        rooms += [pltpu.VMEM(a.shape, a.dtype) for a in far]
        rooms.append(pltpu.SemaphoreType.DMA((len(far),)))
    return pl.pallas_call(
        run,
        out_shape=[jax.ShapeDtypeStruct(shape, dtype) for shape, dtype in outs],
        in_specs=[pl.BlockSpec(memory_space=pltpu.SMEM)] + held + waits,
        out_specs=[pl.BlockSpec(memory_space=pltpu.VMEM)] * len(outs),
        scratch_shapes=rooms,
        compiler_params=pltpu.CompilerParams(vmem_limit_bytes=VMEM_LIMIT),
        name=kernel.__name__,
    )(pos, *args, *far, *behind)


def stacked(parts):
    return jnp.concatenate(parts, axis=0)


def sides(pos, axis, inner, outer):
    even = pos[axis] % 2 == 0
    within = (pos[axis] > 0) & (pos[axis] < 15)

    def far_side(at):
        value = outer[at]
        return jnp.where(within, value, jnp.zeros_like(value))

    def low(*at):
        return jnp.where(even, far_side(at), inner[at])

    def high(*at):
        return jnp.where(even, inner[at], far_side(at))

    return low, high


def give(pos, axis, inner, outer, low, high, at=slice(None)):
    even = pos[axis] % 2 == 0
    inner[at] = jnp.where(even, high, low)
    outer[at] = jnp.where(even, low, high)


def dot_nt(a, b):
    return lax.dot_general(a, b, (((1,), (1,)), ((), ())), preferred_element_type=F32)


def before(values, width):
    place = lax.broadcasted_iota(jnp.int32, values.shape, 0) & (width - 1)
    return jnp.where(place == 0, 0.0, pltpu.roll(values, 1, 0))


def after(values, width):
    place = lax.broadcasted_iota(jnp.int32, values.shape, 0) & (width - 1)
    return jnp.where(place == width - 1, 0.0, pltpu.roll(values, values.shape[0] - 1, 0))


def gathered(wide, width, chans):
    taps = [wide[:, k * chans : (k + 1) * chans] for k in range(3)]
    return before(taps[0], width) + taps[1] + after(taps[2], width)


def scattered(wide, width, chans):
    taps = [wide[:, k * chans : (k + 1) * chans] for k in range(3)]
    return after(taps[0], width) + taps[1] + before(taps[2], width)


def tripled(values, width):
    wide = jnp.concatenate([after(values, width), values, before(values, width)], axis=1)
    return jnp.transpose(wide).astype(BF)


def sigmoid(values):
    return 0.5 * jnp.tanh(0.5 * values) + 0.5


def slope_of(values, sigma):
    return sigma * (1.0 + values * (1.0 - sigma))


def lanes(parts):
    return jnp.concatenate(parts, axis=1)


def back_row(cells, weight, row, rows):
    width, chans = cells.shape[-2:]
    taps = [(depth, height) for depth in range(3) for height in range(3)]
    window = lanes(
        [
            cells[row + 2 - depth, 2 - height : 2 - height + rows].reshape(rows * width, chans)
            for depth, height in taps
        ]
    )
    inner = weight.shape[3]
    turned = lanes([weight[d, h].reshape(3 * inner, chans) for d, h in taps])
    return scattered(dot_nt(window, turned), width, inner)


def input_slabs(pos, own, g_in, g_out, s_in, s_out):
    low, high = sides(pos, 1, g_in, g_out)
    edges = []
    for d in (0, 1):
        cut = slice(d, d + 3)
        edges.append(jnp.concatenate([low(cut), own[cut], high(cut)], axis=1))
    give(pos, 0, s_in, s_out, edges[0], edges[1])


def fill_input(pos, store, own, g_in, g_out, x_in, x_out):
    low, high = sides(pos, 1, g_in, g_out)
    under, over = sides(pos, 0, x_in, x_out)
    lane = lax.broadcasted_iota(jnp.int32, (320, 128), 1)
    for d in range(10):
        if d < 3:
            line = under(d)
        elif d < 7:
            line = jnp.concatenate([low(d - 3), own[d - 3], high(d - 3)], axis=0)
        else:
            line = over(d - 7)
        wide = pltpu.roll(line.reshape(384, 128).astype(F32), 64, 1)
        odd = jnp.where(lane < 64, wide[:320], wide[64:]).astype(BF).reshape(5, 64, 128)
        for m in range(6):
            if m < 5:
                store[d, 2 * m + 1] = odd[m]
            store[d, 2 * m] = line[m]


def encode(
    pos, fetched, own, g_in, g_out, x_in, x_out, cotangent, mean,
    paired, encoded, slope, pooled, bot_slope, bottom, s_in, s_out,
    weight,
):
    fill_input(pos, paired, own, g_in, g_out, x_in, x_out)
    high = pos[0] * 4 - 2
    tall = pos[1] * 4 - 2
    w_enc = fetched(0)
    for depth in range(3):
        for height in range(3):
            at = depth * 256 + height * 64
            weight[at : at + 64, :] = lanes([w_enc[depth, height, k] for k in range(3)])
        weight[depth * 256 + 192 : depth * 256 + 256, :] = jnp.zeros((64, 384), BF)

    place = lax.broadcasted_iota(jnp.int32, (512, 128), 0) // 64 + tall
    across = (place >= 0) & (place < 64)
    for d in range(8):
        window = lanes(
            [
                paired[d + depth, 2 * half + 1 : 2 * half + 9].reshape(512, 128)
                for depth in range(3)
                for half in range(2)
            ]
        )
        pre = gathered(dot(window, weight[...]), 64, 128)
        sigma = sigmoid(pre)
        inside = across & (d + high >= 0) & (d + high < 64)
        encoded[d] = jnp.where(inside, pre * sigma, 0.0).astype(BF).reshape(8, 64, 128)
        slope[d] = jnp.where(inside, slope_of(pre, sigma), 0.0).astype(BF).reshape(8, 64, 128)
    for i in range(4):
        for j in range(4):
            block = encoded[2 * i : 2 * i + 2, 2 * j : 2 * j + 2].reshape(256, 128)
            pooled[i, j] = dot(mean[...], block).astype(BF)
    window = lanes(
        [
            pooled[depth : depth + 2, height : height + 2].reshape(128, 128)
            for depth in range(3)
            for height in range(3)
        ]
    )
    w_bot = fetched(1)
    rows = jnp.concatenate(
        [
            lanes([w_bot[depth, height, k] for k in range(3)])
            for depth in range(3)
            for height in range(3)
        ],
        axis=0,
    )
    pre = gathered(dot(window, rows), 32, 256)
    sigma = sigmoid(pre)
    value = (pre * sigma).astype(BF).reshape(2, 2, 32, 256)
    bottom[...] = value
    bot_slope[...] = slope_of(pre, sigma)
    edges = []
    for h, at in ((0, 0), (1, 3)):
        row = value[:, h].reshape(64, 256)
        edges.append(stacked([cotangent[:, at].reshape(256, 128), row[:, :128], row[:, 128:]]))
    give(pos, 1, s_in, s_out, edges[0], edges[1])


def bottom_slabs(pos, bottom, cotangent, g_in, g_out, s_in, s_out):
    low, high = sides(pos, 1, g_in, g_out)
    edges = []
    for d, b in ((0, 0), (3, 1)):
        cot = slice(64 * d, 64 * d + 64)
        parts = [low(cot), cotangent[d].reshape(256, 128), high(cot)]
        for half in range(2):
            cut = slice(256 + 64 * half + 32 * b, 256 + 64 * half + 32 * b + 32)
            lane = slice(128 * half, 128 * half + 128)
            parts += [low(cut), bottom[b, 0, :, lane], bottom[b, 1, :, lane], high(cut)]
        edges.append(stacked(parts))
    give(pos, 0, s_in, s_out, edges[0], edges[1])


def fill_bottom(pos, wide_bottom, wide_cot, bottom, cotangent, g_in, g_out, x_in, x_out):
    low, high = sides(pos, 1, g_in, g_out)
    for d in range(4):
        cut = slice(64 * d, 64 * d + 64)
        wide_cot[d + 1, 0] = low(cut)
        wide_cot[d + 1, 1:5] = cotangent[d]
        wide_cot[d + 1, 5] = high(cut)
    for b in range(2):
        wide_bottom[b + 1, 1:3] = bottom[b]
        for half in range(2):
            cut = slice(256 + 64 * half + 32 * b, 256 + 64 * half + 32 * b + 32)
            lane = slice(128 * half, 128 * half + 128)
            wide_bottom[b + 1, 0, :, lane] = low(cut)
            wide_bottom[b + 1, 3, :, lane] = high(cut)
    for side, d, b in zip(sides(pos, 0, x_in, x_out), (0, 5), (0, 3)):
        wide_cot[d] = side(slice(0, 384)).reshape(6, 64, 128)
        for half in range(2):
            cut = slice(384 + 128 * half, 512 + 128 * half)
            lane = slice(128 * half, 128 * half + 128)
            wide_bottom[b, :, :, lane] = side(cut).reshape(4, 32, 128)


def decode(
    pos, fetched, own_bottom, own_cot, g_in, g_out, x_in, x_out,
    encoded, bot_slope, stretch, sort,
    decoded, lifted, dec_grad, skip, sorted_lift, bottom_grad, s_in, s_out,
    lift_all, gstore, bottom, cotangent,
):
    fill_bottom(pos, bottom, cotangent, own_bottom, own_cot, g_in, g_out, x_in, x_out)
    w_up = fetched(0)
    for i in range(4):
        wide = []
        for j in range(4):
            spread = dot(stretch[...], bottom[i, j]).astype(BF)
            wide.append(lanes([spread[:64], spread[64:]]))
        wide = jnp.concatenate(wide, axis=0)
        for a in range(2):
            for b in range(2):
                up = w_up[a, b].reshape(512, 128)
                value = dot(wide, up).astype(BF).reshape(4, 64, 128)
                for j in range(4):
                    lift_all[2 * i + a, 2 * j + b] = value[j]
    lifted[...] = lift_all[1:7, 1:7]

    w_dec = fetched(1)
    for d in range(6):
        wide = None
        for depth in range(3):
            window = lanes(
                [
                    cells[d + depth, height : height + 6].reshape(384, 128)
                    for height in range(3)
                    for cells in (lift_all, encoded)
                ]
            )
            rows = stacked([lanes([w_dec[depth, height, k] for k in range(3)]) for height in range(3)])
            part = dot(window, rows)
            wide = part if wide is None else wide + part
        pre = gathered(wide, 64, 128)
        sigma = sigmoid(pre)
        grad = (cotangent[d].reshape(384, 128).astype(F32) * slope_of(pre, sigma)).astype(BF)
        gstore[d] = grad.reshape(6, 64, 128)
        if 1 <= d <= 4:
            decoded[d - 1] = (pre * sigma).astype(BF).reshape(6, 64, 128)[1:5]
            dec_grad[d - 1] = grad.reshape(6, 64, 128)[1:5]
    pieces = [[], []]
    for d in range(4):
        back = back_row(gstore, w_dec, d, 4)
        skip[d] = back[:, 128:].astype(BF).reshape(4, 64, 128)
        lift = back[:, :128].astype(BF).reshape(4, 64, 128)
        flat = lanes([lift[h] for h in range(4)])
        pieces[d // 2].append(dot(sort[...], flat).astype(BF))
    rows = []
    for i in range(2):
        for j in range(2):
            rows.append(
                lanes(
                    [
                        pieces[i][a][32 * c : 32 * c + 32, 128 * (2 * j + b) : 128 * (2 * j + b) + 128]
                        for a in range(2)
                        for b in range(2)
                        for c in range(2)
                    ]
                )
            )
    rows = jnp.concatenate(rows, axis=0)
    sorted_lift[...] = rows
    up = lanes([w_up[a, b, c] for a in range(2) for b in range(2) for c in range(2)])
    back = dot_nt(rows, up)
    grad = (back * bot_slope[...]).astype(BF)
    bottom_grad[...] = grad.reshape(2, 2, 32, 256)
    give(pos, 1, s_in, s_out, skip[:, 0].reshape(256, 128), skip[:, 3].reshape(256, 128), slice(0, 256))
    for half in range(2):
        cut = slice(256 + 128 * half, 384 + 128 * half)
        s_in[cut] = grad[:, 128 * half : 128 * half + 128]
        s_out[cut] = grad[:, 128 * half : 128 * half + 128]


def grad_slabs(pos, grad, skip, g_in, g_out, s_in, s_out):
    low, high = sides(pos, 1, g_in, g_out)
    edges = []
    for d in (0, 3):
        cut = slice(64 * d, 64 * d + 64)
        edges.append(stacked([low(cut), skip[d].reshape(256, 128), high(cut)]))
    give(pos, 0, s_in, s_out, edges[0], edges[1], slice(0, 384))
    for half in range(2):
        lane = slice(128 * half, 128 * half + 128)
        for d in range(2):
            cut = slice(256 + 128 * half + 64 * d, 256 + 128 * half + 64 * d + 64)
            line = stacked([low(cut), grad[d, 0, :, lane], grad[d, 1, :, lane], high(cut)])
            at = 384 + 384 * half + 192 * d
            s_in[at : at + 192] = line
            s_out[at : at + 192] = line


def fill_grad(pos, wide_grad, wide_skip, grad, skip, g_in, g_out, x_in, x_out):
    low, high = sides(pos, 1, g_in, g_out)
    for d in range(4):
        cut = slice(64 * d, 64 * d + 64)
        wide_skip[d + 1, 0] = low(cut)
        wide_skip[d + 1, 1:5] = skip[d]
        wide_skip[d + 1, 5] = high(cut)
    for b in range(2):
        wide_grad[b + 2, 2:4] = grad[b]
        for half in range(2):
            cut = slice(256 + 128 * half + 64 * b, 256 + 128 * half + 64 * b + 64)
            lane = slice(128 * half, 128 * half + 128)
            wide_grad[b + 2, 0:2, :, lane] = low(cut).reshape(2, 32, 128)
            wide_grad[b + 2, 4:6, :, lane] = high(cut).reshape(2, 32, 128)
    for side, d, b in zip(sides(pos, 0, x_in, x_out), (0, 5), (0, 4)):
        wide_skip[d] = side(slice(0, 384)).reshape(6, 64, 128)
        for half in range(2):
            cut = slice(384 + 384 * half, 768 + 384 * half)
            lane = slice(128 * half, 128 * half + 128)
            wide_grad[b : b + 2, :, :, lane] = side(cut).reshape(2, 6, 32, 128)


def put(first, keep, send, at, one, two):
    keep[:, at : at + 128] = jnp.where(first, one, two).astype(BF)
    send[:, at : at + 128] = jnp.where(first, two, one).astype(BF)


def decode_weights(pos, lifted, encoded, dec_grad, keep, send):
    first = pos[0] % 2 == 0
    grad = tripled(dec_grad[...].reshape(1024, 128).astype(F32), 64)
    for depth in range(3):
        for height in range(3):
            window = lanes(
                [
                    lifted[depth : depth + 4, height : height + 4].reshape(1024, 128),
                    encoded[depth + 1 : depth + 5, height + 1 : height + 5].reshape(1024, 128),
                ]
            )
            part = dot(grad, window)
            for k in range(3):
                rows = part[k * 128 : k * 128 + 128]
                at = ((depth * 3 + height) * 3 + k) * 128
                put(first, keep, send, at, rows[:, :128], rows[:, 128:])


def spread_row(row, spread):
    cells = row.reshape(4, 32, 128)
    flat = lanes([cells[h] for h in range(4)])
    upper = flat.astype(BF)
    lower = (flat - upper.astype(F32)).astype(BF)
    return dot(spread[...], jnp.concatenate([upper, lower], axis=0))


def other_weights(
    pos, fetched, sorted_lift, bottom, pooled, bottom_grad, skip, slope, paired, spread,
    keep, send,
    bstore, turned,
):
    first = pos[0] % 2 == 0
    grad = tripled(bottom_grad[...].reshape(128, 256).astype(F32), 32)
    for depth in range(3):
        window = lanes(
            [
                pooled[depth : depth + 2, height : height + 2].reshape(128, 128)
                for height in range(3)
            ]
        )
        part = dot(grad, window)
        for k in range(3):
            rows = part[k * 256 : k * 256 + 256].reshape(16, 2, 8, 384)
            one, two = rows[:, 0].reshape(128, 384), rows[:, 1].reshape(128, 384)
            for height in range(3):
                at = ((depth * 3 + height) * 3 + k) * 128
                cut = slice(height * 128, height * 128 + 128)
                put(first, keep, send, at, one[:, cut], two[:, cut])
    part = dot(
        jnp.transpose(sorted_lift[...].astype(F32)).astype(BF), bottom[...].reshape(128, 256)
    )
    for t in range(8):
        rows = part[t * 128 : t * 128 + 128]
        put(first, keep, send, 3456 + t * 128, rows[:, :128], rows[:, 128:])

    bstore[...] = jnp.zeros((6, 6, 32, 256), BF)
    bstore[2:4, 2:4] = bottom_grad[...]
    w_bot = fetched(0)
    for d in range(4):
        wide = spread_row(back_row(bstore, w_bot, d, 4), spread)
        for f in (2 * d, 2 * d + 1):
            cells = []
            for h in range(8):
                value = wide[:, h // 2 * 128 : h // 2 * 128 + 128]
                if 2 <= f < 6 and 2 <= h < 6:
                    value = value + skip[f - 2, h - 2].astype(F32)
                cells.append(value * slope[f, h].astype(F32))
            row = jnp.concatenate(cells, axis=0).astype(BF).astype(F32)
            turned[:, f * 512 : f * 512 + 512] = tripled(row, 64)

    lane = lax.broadcasted_iota(jnp.int32, (4096, 128), 1)

    def window(depth, height):
        return paired[depth : depth + 8, height + 1 : height + 9].reshape(4096, 128)

    blocks = [window(0, 0), window(1, 0), window(2, 0)]
    blocks.append(jnp.where(lane < 64, window(0, 2), window(1, 1)))
    blocks.append(jnp.where(lane < 64, window(2, 2), window(2, 1)))
    parts = []
    for n in (0, 2, 4):
        part = dot(turned[...], lanes(blocks[n : n + 2]))
        parts += [part[:, m * 128 : m * 128 + 128] for m in range(part.shape[1] // 128)]
    cut = [[part[k * 128 : k * 128 + 128] for k in range(3)] for part in parts]
    small = lax.broadcasted_iota(jnp.int32, (128, 128), 1)
    final = cut[0] + cut[1] + cut[2] + cut[3]
    final += [jnp.where(small < 64, cut[4][0], cut[4][1]), cut[4][2]]
    for n in range(7):
        put(first, keep, send, 4480 + n * 128, final[n], final[n + 7])


def encode_back(
    pos, fetched, own_grad, own_skip, g_in, g_out, x_in, x_out, slope, spread,
    pool_grad, input_grad, done,
    gstore, grad, skip,
):
    done[...] = jnp.zeros((8, 128), F32)
    fill_grad(pos, grad, skip, own_grad, own_skip, g_in, g_out, x_in, x_out)
    w_bot = fetched(0)
    for d in range(4):
        row = back_row(grad, w_bot, d, 4)
        if 1 <= d <= 2:
            pool_grad[d - 1] = row.reshape(4, 32, 128)[1:3]
        wide = spread_row(row, spread)
        for f in range(6):
            if (f + 1) // 2 != d:
                continue
            for h in range(6):
                at = (h + 1) // 2 * 128
                value = skip[f, h].astype(F32) + wide[:, at : at + 128]
                gstore[f, h] = (value * slope[f + 1, h + 1].astype(F32)).astype(BF)
    w_enc = fetched(1)
    for d in range(4):
        input_grad[d] = back_row(gstore, w_enc, d, 4).astype(BF).reshape(4, 64, 64)


def swap(inner, outer, axis):
    count = lax.axis_size(axis)
    pairs = [(i, (i + 1) % count) for i in range(1, count, 2)]
    pairs += [(j, i) for i, j in pairs]
    got = lax.ppermute(inner, axis, [(i, i ^ 1) for i in range(count)])
    return got, lax.ppermute(outer, axis, pairs)


def add_cores(pos, keep, got, total):
    total[...] = (keep[...].astype(F32) + got[...].astype(F32)).astype(BF)


def add_heights(pos, dec, rest, chunks):
    for n in range(72):
        if n < 69:
            parts, at = (dec, 128 * n) if n < 27 else (rest, 128 * (n - 27))
            cut = slice(at, at + 128)
            total = parts[0, :, cut].astype(F32)
            for j in range(1, 16):
                total = total + parts[j, :, cut].astype(F32)
        else:
            total = jnp.zeros((8, 128), F32)
        at = 128 * (n % 9)
        chunks[n // 9, :, at : at + 128] = total.astype(BF)


def add_depths(pos, parts, copies):
    total = parts[0].astype(F32)
    for j in range(1, 8):
        total = total + parts[j].astype(F32)
    total = total.astype(BF)
    for j in range(8):
        copies[j] = total


def finish(pos, mine, other, grad_enc, grad_bot, grad_up, grad_dec):
    first = pos[0] % 2 == 0

    def block(n):
        cut = slice(128 * (n % 9), 128 * (n % 9) + 128)
        left, right = mine[n // 9, :, cut].astype(F32), other[n // 9, :, cut].astype(F32)
        return jnp.where(first, left, right), jnp.where(first, right, left)

    for t in range(27):
        grad_dec[t, :, :128], grad_dec[t, :, 128:] = block(t)
        grad_bot[t, :8], grad_bot[t, 8:] = block(27 + t)
    for t in range(8):
        grad_up[t, :, :128], grad_up[t, :, 128:] = block(54 + t)
    pairs = [block(62 + n) for n in range(7)]
    pieces = [p[0] for p in pairs] + [p[1] for p in pairs]

    def tap(depth, height, k):
        return (depth * 3 + height) * 3 + k

    for k in range(3):
        for depth in range(3):
            piece = pieces[depth * 3 + k]
            grad_enc[tap(depth, 0, k)] = piece[:, :64]
            grad_enc[tap(depth, 1, k)] = piece[:, 64:]
        grad_enc[tap(0, 2, k)] = pieces[9 + k][:, :64]
        grad_enc[tap(1, 2, k)] = pieces[9 + k][:, 64:]
    grad_enc[tap(2, 2, 0)] = pieces[12][:, :64]
    grad_enc[tap(2, 2, 1)] = pieces[12][:, 64:]
    grad_enc[tap(2, 2, 2)] = pieces[13][:, :64]


def other_core(values):
    return lax.ppermute(values, "gx", [(i, i ^ 1) for i in range(lax.axis_size("gx"))])


def to_owners(part):
    return lax.all_to_all(part.reshape(16, 8, part.shape[1]), "gy", 0, 0, tiled=True)


def over_depths(pos, chunks):
    groups = [[2 * a + b for a in range(8)] for b in range(2)]
    got = lax.all_to_all(chunks, "gx", 0, 0, tiled=True, axis_index_groups=groups)
    (copies,) = call(add_depths, [((8, 8, 1152), BF)], [], pos, got)
    return lax.all_to_all(copies, "gx", 0, 0, tiled=True, axis_index_groups=groups)


def constants():
    w, k = np.arange(64)[:, None], np.arange(32)[None, :]
    mean = np.tile((w // 2 == k).T * 0.125, (1, 4))
    stretch = np.concatenate([w == 2 * k, w == 2 * k + 1], axis=0)
    sort = np.concatenate([(w == 2 * k).T, (w == 2 * k + 1).T], axis=0)
    spread = np.concatenate([(w // 2 == k) * 0.125] * 2, axis=1)
    return [jnp.asarray(v, BF) for v in (mean, stretch, sort, spread)]


def shards(inputs, cotangent, w_enc, w_bot, w_up, w_dec):
    mean, stretch, sort, spread = constants()
    pos = jnp.stack([lax.axis_index("gx"), lax.axis_index("gy")]).astype(jnp.int32)
    own = jnp.concatenate([inputs[:, 0::2], inputs[:, 1::2]], axis=3)
    near = swap(own, own, "gy")
    slabs = call(input_slabs, [((3, 6, 64, 128), BF)] * 2, [], pos, own, *near)
    near += swap(*slabs, "gx")
    paired, encoded, slope, pooled, bot_slope, bottom, *slabs = call(
        encode,
        [
            ((10, 11, 64, 128), BF),
            ((8, 8, 64, 128), BF),
            ((8, 8, 64, 128), BF),
            ((4, 4, 32, 128), BF),
            ((128, 256), F32),
            ((2, 2, 32, 256), BF),
        ]
        + [((384, 128), BF)] * 2,
        [((768, 384), BF)],
        pos, own, *near, cotangent, mean, far=(w_enc, w_bot),
    )
    near = swap(*slabs, "gy")
    slabs = call(bottom_slabs, [((640, 128), BF)] * 2, [], pos, bottom, cotangent, *near)
    near += swap(*slabs, "gx")
    decoded, lifted, dec_grad, skip, sorted_lift, bottom_grad, *slabs = call(
        decode,
        [
            ((4, 4, 64, 128), BF),
            ((6, 6, 64, 128), BF),
            ((4, 4, 64, 128), BF),
            ((4, 4, 64, 128), BF),
            ((128, 1024), BF),
            ((2, 2, 32, 256), BF),
        ]
        + [((512, 128), BF)] * 2,
        [
            ((8, 8, 64, 128), BF),
            ((6, 6, 64, 128), BF),
            ((4, 4, 32, 256), BF),
            ((6, 6, 64, 128), BF),
        ],
        pos, bottom, cotangent, *near, encoded, bot_slope, stretch, sort, far=(w_up, w_dec),
    )
    near = swap(*slabs, "gy")
    keep, send = call(
        decode_weights,
        [((128, 3456), BF), ((128, 3456), BF)],
        [],
        pos, lifted, encoded, dec_grad,
    )
    (part_dec,) = call(
        add_cores, [((128, 3456), BF)], [], pos, keep, other_core(send), behind=near
    )
    keep, send = call(
        other_weights,
        [((128, 5376), BF), ((128, 5376), BF)],
        [((6, 6, 32, 256), BF), ((384, 4096), BF)],
        pos, sorted_lift, bottom, pooled, bottom_grad, skip, slope, paired, spread,
        far=(w_bot,), behind=(part_dec,),
    )
    part_dec = to_owners(part_dec)
    (part_rest,) = call(add_cores, [((128, 5376), BF)], [], pos, keep, other_core(send))
    slabs = call(
        grad_slabs, [((1152, 128), BF)] * 2, [], pos, bottom_grad, skip, *near,
        behind=(part_rest,),
    )
    part_rest = to_owners(part_rest)
    near += swap(*slabs, "gx")
    pool_grad, input_grad, done = call(
        encode_back,
        [((2, 2, 32, 128), F32), ((4, 4, 64, 64), BF), ((8, 128), F32)],
        [((6, 6, 64, 128), BF), ((6, 6, 32, 256), BF), ((6, 6, 64, 128), BF)],
        pos, bottom_grad, skip, *near, slope, spread,
        far=(w_bot, w_enc),
    )
    (chunks,) = call(add_heights, [((8, 8, 1152), BF)], [], pos, part_dec, part_rest, behind=(done,))
    mine = over_depths(pos, chunks)
    other = other_core(mine)
    grads = call(
        finish,
        [((27, 8, 64), F32), ((27, 16, 128), F32), ((8, 8, 256), F32), ((27, 8, 256), F32)],
        [],
        pos, mine, other,
    )
    grad_enc, grad_bot, grad_up, grad_dec = (
        jnp.transpose(grad, (0, 2, 1)).reshape(*shape, grad.shape[2], grad.shape[1])
        for grad, shape in zip(grads, ((3, 3, 3), (3, 3, 3), (2, 2, 2), (3, 3, 3)))
    )
    return (decoded, input_grad, grad_enc, grad_bot, grad_up, grad_dec, pool_grad)


def solution(mesh):
    in_specs = (P("gx", "gy", None, None), P("gx", "gy", None, None), P(), P(), P(), P())
    out_specs = (
        P("gx", "gy", None, None),
        P("gx", "gy", None, None),
        P(None, None, None, None, "gy"),
        P(None, None, None, None, "gy"),
        P(None, None, None, None, "gy"),
        P(None, None, None, None, "gy"),
        P("gx", "gy", None, None),
    )
    return jax.shard_map(shards, mesh=mesh, in_specs=in_specs, out_specs=out_specs, check_vma=False)
```

```python
import jax
import jax.numpy as jnp
import numpy as np
from jax import lax
from jax.experimental import pallas as pl
from jax.experimental.pallas import tpu as pltpu
from jax.sharding import PartitionSpec as P

BF = jnp.bfloat16
F32 = jnp.float32
VMEM_LIMIT = 24 * 1024 * 1024


def dot(a, b):
    return jnp.dot(a, b, preferred_element_type=F32)


def call(kernel, outs, scratch, pos, *args, far=(), behind=(), us=1):
    held = [pl.BlockSpec(memory_space=pltpu.VMEM)] * len(args)
    waits = [pl.BlockSpec(memory_space=pltpu.HBM)] * len(far)
    waits += [pl.BlockSpec(memory_space=pl.ANY)] * len(behind)
    count = len(args)

    def run(place, *refs):
        own = refs[count + len(waits) :]
        copies = []
        for n in range(len(far)):
            room = own[len(own) - 1 - len(far) + n]
            copies.append(pltpu.make_async_copy(refs[count + n], room, own[-1].at[n]))
            copies[-1].start()

        def fetched(n):
            copies[n].wait()
            return own[len(own) - 1 - len(far) + n]

        extra = (fetched,) if far else ()
        kept = own[: len(own) - 1 - len(far)] if far else own
        return kernel(place, *extra, *refs[:count], *kept)

    rooms = [pltpu.VMEM(shape, dtype) for shape, dtype in scratch]
    if far:
        rooms += [pltpu.VMEM(a.shape, a.dtype) for a in far]
        rooms.append(pltpu.SemaphoreType.DMA((len(far),)))
    return pl.pallas_call(
        run,
        out_shape=[jax.ShapeDtypeStruct(shape, dtype) for shape, dtype in outs],
        in_specs=[pl.BlockSpec(memory_space=pltpu.SMEM)] + held + waits,
        out_specs=[pl.BlockSpec(memory_space=pltpu.VMEM)] * len(outs),
        scratch_shapes=rooms,
        compiler_params=pltpu.CompilerParams(vmem_limit_bytes=VMEM_LIMIT),
        cost_estimate=pl.CostEstimate(
            flops=us * 10**9, transcendentals=0, bytes_accessed=us * 3 * 10**6
        ),
        name=kernel.__name__,
    )(pos, *args, *far, *behind)


def stacked(parts):
    return jnp.concatenate(parts, axis=0)


def sides(pos, axis, inner, outer):
    even = pos[axis] % 2 == 0
    within = (pos[axis] > 0) & (pos[axis] < 15)

    def far_side(at):
        value = outer[at]
        return jnp.where(within, value, jnp.zeros_like(value))

    def low(*at):
        return jnp.where(even, far_side(at), inner[at])

    def high(*at):
        return jnp.where(even, inner[at], far_side(at))

    return low, high


def give(pos, axis, inner, outer, low, high, at=slice(None)):
    even = pos[axis] % 2 == 0
    inner[at] = jnp.where(even, high, low)
    outer[at] = jnp.where(even, low, high)


def dot_nt(a, b):
    return lax.dot_general(a, b, (((1,), (1,)), ((), ())), preferred_element_type=F32)


def before(values, width):
    place = lax.broadcasted_iota(jnp.int32, values.shape, 0) & (width - 1)
    return jnp.where(place == 0, 0.0, pltpu.roll(values, 1, 0))


def after(values, width):
    place = lax.broadcasted_iota(jnp.int32, values.shape, 0) & (width - 1)
    return jnp.where(place == width - 1, 0.0, pltpu.roll(values, values.shape[0] - 1, 0))


def gathered(wide, width, chans):
    taps = [wide[:, k * chans : (k + 1) * chans] for k in range(3)]
    return before(taps[0], width) + taps[1] + after(taps[2], width)


def scattered(wide, width, chans):
    taps = [wide[:, k * chans : (k + 1) * chans] for k in range(3)]
    return after(taps[0], width) + taps[1] + before(taps[2], width)


def tripled(values, width):
    wide = jnp.concatenate([after(values, width), values, before(values, width)], axis=1)
    return jnp.transpose(wide).astype(BF)


def sigmoid(values):
    return 0.5 * jnp.tanh(0.5 * values) + 0.5


def slope_of(values, sigma):
    return sigma * (1.0 + values * (1.0 - sigma))


def lanes(parts):
    return jnp.concatenate(parts, axis=1)


def back_row(cells, weight, row, rows):
    width, chans = cells.shape[-2:]
    taps = [(depth, height) for depth in range(3) for height in range(3)]
    window = lanes(
        [
            cells[row + 2 - depth, 2 - height : 2 - height + rows].reshape(rows * width, chans)
            for depth, height in taps
        ]
    )
    inner = weight.shape[3]
    turned = lanes([weight[d, h].reshape(3 * inner, chans) for d, h in taps])
    return scattered(dot_nt(window, turned), width, inner)


def input_slabs(pos, own, g_in, g_out, s_in, s_out):
    low, high = sides(pos, 1, g_in, g_out)
    edges = []
    for d in (0, 1):
        cut = slice(d, d + 3)
        edges.append(jnp.concatenate([low(cut), own[cut], high(cut)], axis=1))
    give(pos, 0, s_in, s_out, edges[0], edges[1])


def fill_input(pos, store, own, g_in, g_out, x_in, x_out):
    low, high = sides(pos, 1, g_in, g_out)
    under, over = sides(pos, 0, x_in, x_out)
    lane = lax.broadcasted_iota(jnp.int32, (320, 128), 1)
    for d in range(10):
        if d < 3:
            line = under(d)
        elif d < 7:
            line = jnp.concatenate([low(d - 3), own[d - 3], high(d - 3)], axis=0)
        else:
            line = over(d - 7)
        wide = pltpu.roll(line.reshape(384, 128).astype(F32), 64, 1)
        odd = jnp.where(lane < 64, wide[:320], wide[64:]).astype(BF).reshape(5, 64, 128)
        for m in range(6):
            if m < 5:
                store[d, 2 * m + 1] = odd[m]
            store[d, 2 * m] = line[m]


def encode(
    pos, fetched, own, g_in, g_out, x_in, x_out, cotangent, mean,
    paired, encoded, slope, pooled, bot_slope, bottom, s_in, s_out,
    weight,
):
    fill_input(pos, paired, own, g_in, g_out, x_in, x_out)
    high = pos[0] * 4 - 2
    tall = pos[1] * 4 - 2
    w_enc = fetched(0)
    for depth in range(3):
        for height in range(3):
            at = depth * 256 + height * 64
            weight[at : at + 64, :] = lanes([w_enc[depth, height, k] for k in range(3)])
        weight[depth * 256 + 192 : depth * 256 + 256, :] = jnp.zeros((64, 384), BF)

    place = lax.broadcasted_iota(jnp.int32, (512, 128), 0) // 64 + tall
    across = (place >= 0) & (place < 64)
    for d in range(8):
        window = lanes(
            [
                paired[d + depth, 2 * half + 1 : 2 * half + 9].reshape(512, 128)
                for depth in range(3)
                for half in range(2)
            ]
        )
        pre = gathered(dot(window, weight[...]), 64, 128)
        sigma = sigmoid(pre)
        inside = across & (d + high >= 0) & (d + high < 64)
        encoded[d] = jnp.where(inside, pre * sigma, 0.0).astype(BF).reshape(8, 64, 128)
        slope[d] = jnp.where(inside, slope_of(pre, sigma), 0.0).astype(BF).reshape(8, 64, 128)
    for i in range(4):
        for j in range(4):
            block = encoded[2 * i : 2 * i + 2, 2 * j : 2 * j + 2].reshape(256, 128)
            pooled[i, j] = dot(mean[...], block).astype(BF)
    window = lanes(
        [
            pooled[depth : depth + 2, height : height + 2].reshape(128, 128)
            for depth in range(3)
            for height in range(3)
        ]
    )
    w_bot = fetched(1)
    rows = jnp.concatenate(
        [
            lanes([w_bot[depth, height, k] for k in range(3)])
            for depth in range(3)
            for height in range(3)
        ],
        axis=0,
    )
    pre = gathered(dot(window, rows), 32, 256)
    sigma = sigmoid(pre)
    value = (pre * sigma).astype(BF).reshape(2, 2, 32, 256)
    bottom[...] = value
    bot_slope[...] = slope_of(pre, sigma)
    edges = []
    for h, at in ((0, 0), (1, 3)):
        row = value[:, h].reshape(64, 256)
        edges.append(stacked([cotangent[:, at].reshape(256, 128), row[:, :128], row[:, 128:]]))
    give(pos, 1, s_in, s_out, edges[0], edges[1])


def bottom_slabs(pos, bottom, cotangent, g_in, g_out, s_in, s_out):
    low, high = sides(pos, 1, g_in, g_out)
    edges = []
    for d, b in ((0, 0), (3, 1)):
        cot = slice(64 * d, 64 * d + 64)
        parts = [low(cot), cotangent[d].reshape(256, 128), high(cot)]
        for half in range(2):
            cut = slice(256 + 64 * half + 32 * b, 256 + 64 * half + 32 * b + 32)
            lane = slice(128 * half, 128 * half + 128)
            parts += [low(cut), bottom[b, 0, :, lane], bottom[b, 1, :, lane], high(cut)]
        edges.append(stacked(parts))
    give(pos, 0, s_in, s_out, edges[0], edges[1])


def fill_bottom(pos, wide_bottom, wide_cot, bottom, cotangent, g_in, g_out, x_in, x_out):
    low, high = sides(pos, 1, g_in, g_out)
    for d in range(4):
        cut = slice(64 * d, 64 * d + 64)
        wide_cot[d + 1, 0] = low(cut)
        wide_cot[d + 1, 1:5] = cotangent[d]
        wide_cot[d + 1, 5] = high(cut)
    for b in range(2):
        wide_bottom[b + 1, 1:3] = bottom[b]
        for half in range(2):
            cut = slice(256 + 64 * half + 32 * b, 256 + 64 * half + 32 * b + 32)
            lane = slice(128 * half, 128 * half + 128)
            wide_bottom[b + 1, 0, :, lane] = low(cut)
            wide_bottom[b + 1, 3, :, lane] = high(cut)
    for side, d, b in zip(sides(pos, 0, x_in, x_out), (0, 5), (0, 3)):
        wide_cot[d] = side(slice(0, 384)).reshape(6, 64, 128)
        for half in range(2):
            cut = slice(384 + 128 * half, 512 + 128 * half)
            lane = slice(128 * half, 128 * half + 128)
            wide_bottom[b, :, :, lane] = side(cut).reshape(4, 32, 128)


def decode(
    pos, fetched, own_bottom, own_cot, g_in, g_out, x_in, x_out,
    encoded, bot_slope, stretch, sort,
    decoded, lifted, dec_grad, skip, sorted_lift, bottom_grad,
    lift_all, gstore, bottom, cotangent,
):
    fill_bottom(pos, bottom, cotangent, own_bottom, own_cot, g_in, g_out, x_in, x_out)
    w_up = fetched(0)
    for i in range(4):
        wide = []
        for j in range(4):
            spread = dot(stretch[...], bottom[i, j]).astype(BF)
            wide.append(lanes([spread[:64], spread[64:]]))
        wide = jnp.concatenate(wide, axis=0)
        for a in range(2):
            for b in range(2):
                up = w_up[a, b].reshape(512, 128)
                value = dot(wide, up).astype(BF).reshape(4, 64, 128)
                for j in range(4):
                    lift_all[2 * i + a, 2 * j + b] = value[j]
    lifted[...] = lift_all[1:7, 1:7]

    w_dec = fetched(1)
    for d in range(6):
        wide = None
        for depth in range(3):
            window = lanes(
                [
                    cells[d + depth, height : height + 6].reshape(384, 128)
                    for height in range(3)
                    for cells in (lift_all, encoded)
                ]
            )
            rows = stacked([lanes([w_dec[depth, height, k] for k in range(3)]) for height in range(3)])
            part = dot(window, rows)
            wide = part if wide is None else wide + part
        pre = gathered(wide, 64, 128)
        sigma = sigmoid(pre)
        grad = (cotangent[d].reshape(384, 128).astype(F32) * slope_of(pre, sigma)).astype(BF)
        gstore[d] = grad.reshape(6, 64, 128)
        if 1 <= d <= 4:
            decoded[d - 1] = (pre * sigma).astype(BF).reshape(6, 64, 128)[1:5]
            dec_grad[d - 1] = grad.reshape(6, 64, 128)[1:5]
    pieces = [[], []]
    for d in range(4):
        back = back_row(gstore, w_dec, d, 4)
        skip[d] = back[:, 128:].astype(BF).reshape(4, 64, 128)
        lift = back[:, :128].astype(BF).reshape(4, 64, 128)
        flat = lanes([lift[h] for h in range(4)])
        pieces[d // 2].append(dot(sort[...], flat).astype(BF))
    rows = []
    for i in range(2):
        for j in range(2):
            rows.append(
                lanes(
                    [
                        pieces[i][a][32 * c : 32 * c + 32, 128 * (2 * j + b) : 128 * (2 * j + b) + 128]
                        for a in range(2)
                        for b in range(2)
                        for c in range(2)
                    ]
                )
            )
    rows = jnp.concatenate(rows, axis=0)
    sorted_lift[...] = rows
    up = lanes([w_up[a, b, c] for a in range(2) for b in range(2) for c in range(2)])
    back = dot_nt(rows, up)
    grad = (back * bot_slope[...]).astype(BF)
    bottom_grad[...] = grad.reshape(2, 2, 32, 256)


def grad_edges(pos, grad, skip, s_in, s_out):
    give(pos, 1, s_in, s_out, skip[:, 0].reshape(256, 128), skip[:, 3].reshape(256, 128), slice(0, 256))
    flat = grad[...].reshape(128, 256)
    for half in range(2):
        cut = slice(256 + 128 * half, 384 + 128 * half)
        s_in[cut] = flat[:, 128 * half : 128 * half + 128]
        s_out[cut] = flat[:, 128 * half : 128 * half + 128]


def grad_slabs(pos, grad, skip, g_in, g_out, s_in, s_out):
    low, high = sides(pos, 1, g_in, g_out)
    edges = []
    for d in (0, 3):
        cut = slice(64 * d, 64 * d + 64)
        edges.append(stacked([low(cut), skip[d].reshape(256, 128), high(cut)]))
    give(pos, 0, s_in, s_out, edges[0], edges[1], slice(0, 384))
    for half in range(2):
        lane = slice(128 * half, 128 * half + 128)
        for d in range(2):
            cut = slice(256 + 128 * half + 64 * d, 256 + 128 * half + 64 * d + 64)
            line = stacked([low(cut), grad[d, 0, :, lane], grad[d, 1, :, lane], high(cut)])
            at = 384 + 384 * half + 192 * d
            s_in[at : at + 192] = line
            s_out[at : at + 192] = line


def fill_grad(pos, wide_grad, wide_skip, grad, skip, g_in, g_out, x_in, x_out):
    low, high = sides(pos, 1, g_in, g_out)
    for d in range(4):
        cut = slice(64 * d, 64 * d + 64)
        wide_skip[d + 1, 0] = low(cut)
        wide_skip[d + 1, 1:5] = skip[d]
        wide_skip[d + 1, 5] = high(cut)
    for b in range(2):
        wide_grad[b + 2, 2:4] = grad[b]
        for half in range(2):
            cut = slice(256 + 128 * half + 64 * b, 256 + 128 * half + 64 * b + 64)
            lane = slice(128 * half, 128 * half + 128)
            wide_grad[b + 2, 0:2, :, lane] = low(cut).reshape(2, 32, 128)
            wide_grad[b + 2, 4:6, :, lane] = high(cut).reshape(2, 32, 128)
    for side, d, b in zip(sides(pos, 0, x_in, x_out), (0, 5), (0, 4)):
        wide_skip[d] = side(slice(0, 384)).reshape(6, 64, 128)
        for half in range(2):
            cut = slice(384 + 384 * half, 768 + 384 * half)
            lane = slice(128 * half, 128 * half + 128)
            wide_grad[b : b + 2, :, :, lane] = side(cut).reshape(2, 6, 32, 128)


def put(first, keep, send, at, one, two):
    keep[:, at : at + 128] = jnp.where(first, one, two).astype(BF)
    send[:, at : at + 128] = jnp.where(first, two, one).astype(BF)


def decode_weights(pos, lifted, encoded, dec_grad, keep, send):
    first = pos[0] % 2 == 0
    grad = tripled(dec_grad[...].reshape(1024, 128).astype(F32), 64)
    for depth in range(3):
        for height in range(3):
            window = lanes(
                [
                    lifted[depth : depth + 4, height : height + 4].reshape(1024, 128),
                    encoded[depth + 1 : depth + 5, height + 1 : height + 5].reshape(1024, 128),
                ]
            )
            part = dot(grad, window)
            for k in range(3):
                rows = part[k * 128 : k * 128 + 128]
                at = ((depth * 3 + height) * 3 + k) * 128
                put(first, keep, send, at, rows[:, :128], rows[:, 128:])


def spread_row(row, spread):
    cells = row.reshape(4, 32, 128)
    flat = lanes([cells[h] for h in range(4)])
    upper = flat.astype(BF)
    lower = (flat - upper.astype(F32)).astype(BF)
    return dot(spread[...], jnp.concatenate([upper, lower], axis=0))


def bottom_weights(
    pos, sorted_lift, bottom, pooled, bottom_grad,
    keep, send,
):
    first = pos[0] % 2 == 0
    grad = tripled(bottom_grad[...].reshape(128, 256).astype(F32), 32)
    for depth in range(3):
        window = lanes(
            [
                pooled[depth : depth + 2, height : height + 2].reshape(128, 128)
                for height in range(3)
            ]
        )
        part = dot(grad, window)
        for k in range(3):
            rows = part[k * 256 : k * 256 + 256].reshape(16, 2, 8, 384)
            one, two = rows[:, 0].reshape(128, 384), rows[:, 1].reshape(128, 384)
            for height in range(3):
                at = ((depth * 3 + height) * 3 + k) * 128
                cut = slice(height * 128, height * 128 + 128)
                put(first, keep, send, at, one[:, cut], two[:, cut])
    part = dot(
        jnp.transpose(sorted_lift[...].astype(F32)).astype(BF), bottom[...].reshape(128, 256)
    )
    for t in range(8):
        rows = part[t * 128 : t * 128 + 128]
        put(first, keep, send, 3456 + t * 128, rows[:, :128], rows[:, 128:])


def encode_weights(
    pos, fetched, bottom_grad, skip, slope, paired, spread,
    keep, send,
    bstore, turned,
):
    first = pos[0] % 2 == 0
    bstore[...] = jnp.zeros((6, 6, 32, 256), BF)
    bstore[2:4, 2:4] = bottom_grad[...]
    w_bot = fetched(0)
    for d in range(4):
        wide = spread_row(back_row(bstore, w_bot, d, 4), spread)
        for f in (2 * d, 2 * d + 1):
            cells = []
            for h in range(8):
                value = wide[:, h // 2 * 128 : h // 2 * 128 + 128]
                if 2 <= f < 6 and 2 <= h < 6:
                    value = value + skip[f - 2, h - 2].astype(F32)
                cells.append(value * slope[f, h].astype(F32))
            row = jnp.concatenate(cells, axis=0).astype(BF).astype(F32)
            turned[:, f * 512 : f * 512 + 512] = tripled(row, 64)

    lane = lax.broadcasted_iota(jnp.int32, (4096, 128), 1)

    def window(depth, height):
        return paired[depth : depth + 8, height + 1 : height + 9].reshape(4096, 128)

    blocks = [window(0, 0), window(1, 0), window(2, 0)]
    blocks.append(jnp.where(lane < 64, window(0, 2), window(1, 1)))
    blocks.append(jnp.where(lane < 64, window(2, 2), window(2, 1)))
    parts = []
    for n in (0, 2, 4):
        part = dot(turned[...], lanes(blocks[n : n + 2]))
        parts += [part[:, m * 128 : m * 128 + 128] for m in range(part.shape[1] // 128)]
    cut = [[part[k * 128 : k * 128 + 128] for k in range(3)] for part in parts]
    small = lax.broadcasted_iota(jnp.int32, (128, 128), 1)
    final = cut[0] + cut[1] + cut[2] + cut[3]
    final += [jnp.where(small < 64, cut[4][0], cut[4][1]), cut[4][2]]
    for n in range(7):
        put(first, keep, send, n * 128, final[n], final[n + 7])


def encode_back(
    pos, fetched, own_grad, own_skip, g_in, g_out, x_in, x_out, slope, spread,
    pool_grad, input_grad, done,
    gstore, grad, skip,
):
    done[...] = jnp.zeros((8, 128), F32)
    fill_grad(pos, grad, skip, own_grad, own_skip, g_in, g_out, x_in, x_out)
    w_bot = fetched(0)
    for d in range(4):
        row = back_row(grad, w_bot, d, 4)
        if 1 <= d <= 2:
            pool_grad[d - 1] = row.reshape(4, 32, 128)[1:3]
        wide = spread_row(row, spread)
        for f in range(6):
            if (f + 1) // 2 != d:
                continue
            for h in range(6):
                at = (h + 1) // 2 * 128
                value = skip[f, h].astype(F32) + wide[:, at : at + 128]
                gstore[f, h] = (value * slope[f + 1, h + 1].astype(F32)).astype(BF)
    w_enc = fetched(1)
    for d in range(4):
        input_grad[d] = back_row(gstore, w_enc, d, 4).astype(BF).reshape(4, 64, 64)


def swap(inner, outer, axis):
    count = lax.axis_size(axis)
    pairs = [(i, (i + 1) % count) for i in range(1, count, 2)]
    pairs += [(j, i) for i, j in pairs]
    got = lax.ppermute(inner, axis, [(i, i ^ 1) for i in range(count)])
    return got, lax.ppermute(outer, axis, pairs)


def add_cores(pos, *refs):
    total = refs[-1]
    at = 0
    for keep, got in zip(refs[0:-1:2], refs[1:-1:2]):
        width = keep.shape[1]
        total[:, at : at + width] = (keep[...].astype(F32) + got[...].astype(F32)).astype(BF)
        at += width


def add_heights(pos, parts, chunks):
    filled = parts.shape[2] // 128
    for n in range(9 * chunks.shape[0]):
        if n < filled:
            cut = slice(128 * n, 128 * n + 128)
            total = parts[0, :, cut].astype(F32)
            for j in range(1, 16):
                total = total + parts[j, :, cut].astype(F32)
        else:
            total = jnp.zeros((8, 128), F32)
        at = 128 * (n % 9)
        chunks[n // 9, :, at : at + 128] = total.astype(BF)


def add_rest(pos, parts, chunks, every):
    every[0:3] = chunks[...]
    add_heights(pos, parts, every.at[3:8])


def add_depths(pos, parts, copies):
    total = parts[0].astype(F32)
    for j in range(1, 8):
        total = total + parts[j].astype(F32)
    total = total.astype(BF)
    for j in range(8):
        copies[j] = total


def finish(pos, mine, other, grad_enc, grad_bot, grad_up, grad_dec):
    first = pos[0] % 2 == 0

    def block(n):
        cut = slice(128 * (n % 9), 128 * (n % 9) + 128)
        left, right = mine[n // 9, :, cut].astype(F32), other[n // 9, :, cut].astype(F32)
        return jnp.where(first, left, right), jnp.where(first, right, left)

    for t in range(27):
        grad_dec[t, :, :128], grad_dec[t, :, 128:] = block(t)
        grad_bot[t, :8], grad_bot[t, 8:] = block(27 + t)
    for t in range(8):
        grad_up[t, :, :128], grad_up[t, :, 128:] = block(54 + t)
    pairs = [block(62 + n) for n in range(7)]
    pieces = [p[0] for p in pairs] + [p[1] for p in pairs]

    def tap(depth, height, k):
        return (depth * 3 + height) * 3 + k

    for k in range(3):
        for depth in range(3):
            piece = pieces[depth * 3 + k]
            grad_enc[tap(depth, 0, k)] = piece[:, :64]
            grad_enc[tap(depth, 1, k)] = piece[:, 64:]
        grad_enc[tap(0, 2, k)] = pieces[9 + k][:, :64]
        grad_enc[tap(1, 2, k)] = pieces[9 + k][:, 64:]
    grad_enc[tap(2, 2, 0)] = pieces[12][:, :64]
    grad_enc[tap(2, 2, 1)] = pieces[12][:, 64:]
    grad_enc[tap(2, 2, 2)] = pieces[13][:, :64]


def other_core(values):
    return lax.ppermute(values, "gx", [(i, i ^ 1) for i in range(lax.axis_size("gx"))])


def to_owners(part):
    return lax.all_to_all(part.reshape(16, 8, part.shape[1]), "gy", 0, 0, tiled=True)


def over_depths(pos, chunks):
    groups = [[2 * a + b for a in range(8)] for b in range(2)]
    got = lax.all_to_all(chunks, "gx", 0, 0, tiled=True, axis_index_groups=groups)
    (copies,) = call(add_depths, [((8, 8, 1152), BF)], [], pos, got)
    return lax.all_to_all(copies, "gx", 0, 0, tiled=True, axis_index_groups=groups)


def constants():
    w, k = np.arange(64)[:, None], np.arange(32)[None, :]
    mean = np.tile((w // 2 == k).T * 0.125, (1, 4))
    stretch = np.concatenate([w == 2 * k, w == 2 * k + 1], axis=0)
    sort = np.concatenate([(w == 2 * k).T, (w == 2 * k + 1).T], axis=0)
    spread = np.concatenate([(w // 2 == k) * 0.125] * 2, axis=1)
    return [jnp.asarray(v, BF) for v in (mean, stretch, sort, spread)]


def shards(inputs, cotangent, w_enc, w_bot, w_up, w_dec):
    mean, stretch, sort, spread = constants()
    pos = jnp.stack([lax.axis_index("gx"), lax.axis_index("gy")]).astype(jnp.int32)
    own = jnp.concatenate([inputs[:, 0::2], inputs[:, 1::2]], axis=3)
    near = swap(own, own, "gy")
    slabs = call(input_slabs, [((3, 6, 64, 128), BF)] * 2, [], pos, own, *near)
    near += swap(*slabs, "gx")
    paired, encoded, slope, pooled, bot_slope, bottom, *slabs = call(
        encode,
        [
            ((10, 11, 64, 128), BF),
            ((8, 8, 64, 128), BF),
            ((8, 8, 64, 128), BF),
            ((4, 4, 32, 128), BF),
            ((128, 256), F32),
            ((2, 2, 32, 256), BF),
        ]
        + [((384, 128), BF)] * 2,
        [((768, 384), BF)],
        pos, own, *near, cotangent, mean, far=(w_enc, w_bot),
        us=6,
    )
    near = swap(*slabs, "gy")
    slabs = call(bottom_slabs, [((640, 128), BF)] * 2, [], pos, bottom, cotangent, *near)
    near += swap(*slabs, "gx")
    decoded, lifted, dec_grad, skip, sorted_lift, bottom_grad = call(
        decode,
        [
            ((4, 4, 64, 128), BF),
            ((6, 6, 64, 128), BF),
            ((4, 4, 64, 128), BF),
            ((4, 4, 64, 128), BF),
            ((128, 1024), BF),
            ((2, 2, 32, 256), BF),
        ],
        [
            ((8, 8, 64, 128), BF),
            ((6, 6, 64, 128), BF),
            ((4, 4, 32, 256), BF),
            ((6, 6, 64, 128), BF),
        ],
        pos, bottom, cotangent, *near, encoded, bot_slope, stretch, sort, far=(w_up, w_dec),
        us=13,
    )
    keep, send = call(
        decode_weights,
        [((128, 3456), BF)] * 2,
        [],
        pos, lifted, encoded, dec_grad,
        us=3,
    )
    (part_dec,) = call(add_cores, [((128, 3456), BF)], [], pos, keep, other_core(send))
    keep, send = call(
        encode_weights,
        [((128, 896), BF)] * 2,
        [((6, 6, 32, 256), BF), ((384, 4096), BF)],
        pos, bottom_grad, skip, slope, paired, spread,
        far=(w_bot,), behind=(part_dec,),
        us=6,
    )
    part_dec = to_owners(part_dec)
    part_enc = [keep, other_core(send)]
    slabs = call(
        grad_edges, [((512, 128), BF)] * 2, [], pos, bottom_grad, skip,
        behind=(part_dec, keep),
    )
    near = swap(*slabs, "gy")
    keep, send = call(
        bottom_weights,
        [((128, 4480), BF)] * 2,
        [],
        pos, sorted_lift, bottom, pooled, bottom_grad,
        behind=slabs[:1],
        us=3,
    )
    (part_rest,) = call(
        add_cores, [((128, 5376), BF)], [], pos, keep, other_core(send), *part_enc, behind=near
    )
    slabs = call(
        grad_slabs, [((1152, 128), BF)] * 2, [], pos, bottom_grad, skip, *near,
        behind=(part_rest,),
    )
    part_rest = to_owners(part_rest)
    (chunks,) = call(add_heights, [((3, 8, 1152), BF)], [], pos, part_dec, behind=slabs[:1])
    near += swap(*slabs, "gx")
    pool_grad, input_grad, done = call(
        encode_back,
        [((2, 2, 32, 128), F32), ((4, 4, 64, 64), BF), ((8, 128), F32)],
        [((6, 6, 64, 128), BF), ((6, 6, 32, 256), BF), ((6, 6, 64, 128), BF)],
        pos, bottom_grad, skip, *near, slope, spread,
        far=(w_bot, w_enc),
        us=5,
    )
    (chunks,) = call(
        add_rest, [((8, 8, 1152), BF)], [], pos, part_rest, chunks, behind=(done,)
    )
    mine = over_depths(pos, chunks)
    other = other_core(mine)
    grads = call(
        finish,
        [((27, 8, 64), F32), ((27, 16, 128), F32), ((8, 8, 256), F32), ((27, 8, 256), F32)],
        [],
        pos, mine, other,
    )
    grad_enc, grad_bot, grad_up, grad_dec = (
        jnp.transpose(grad, (0, 2, 1)).reshape(*shape, grad.shape[2], grad.shape[1])
        for grad, shape in zip(grads, ((3, 3, 3), (3, 3, 3), (2, 2, 2), (3, 3, 3)))
    )
    return (decoded, input_grad, grad_enc, grad_bot, grad_up, grad_dec, pool_grad)


def solution(mesh):
    in_specs = (P("gx", "gy", None, None), P("gx", "gy", None, None), P(), P(), P(), P())
    out_specs = (
        P("gx", "gy", None, None),
        P("gx", "gy", None, None),
        P(None, None, None, None, "gy"),
        P(None, None, None, None, "gy"),
        P(None, None, None, None, "gy"),
        P(None, None, None, None, "gy"),
        P("gx", "gy", None, None),
    )
    return jax.shard_map(shards, mesh=mesh, in_specs=in_specs, out_specs=out_specs, check_vma=False)
```

```python
import jax
import jax.numpy as jnp
import numpy as np
from jax import lax
from jax.experimental import pallas as pl
from jax.experimental.pallas import tpu as pltpu
from jax.sharding import PartitionSpec as P

BF = jnp.bfloat16
F32 = jnp.float32
VMEM_LIMIT = 24 * 1024 * 1024


def dot(a, b):
    return jnp.dot(a, b, preferred_element_type=F32)


def call(kernel, outs, scratch, pos, *args, far=(), behind=(), us=1):
    held = [pl.BlockSpec(memory_space=pltpu.VMEM)] * len(args)
    waits = [pl.BlockSpec(memory_space=pltpu.HBM)] * len(far)
    waits += [pl.BlockSpec(memory_space=pl.ANY)] * len(behind)
    count = len(args)

    def run(place, *refs):
        own = refs[count + len(waits) :]
        copies = []
        for n in range(len(far)):
            room = own[len(own) - 1 - len(far) + n]
            copies.append(pltpu.make_async_copy(refs[count + n], room, own[-1].at[n]))
            copies[-1].start()

        def fetched(n):
            copies[n].wait()
            return own[len(own) - 1 - len(far) + n]

        extra = (fetched,) if far else ()
        kept = own[: len(own) - 1 - len(far)] if far else own
        return kernel(place, *extra, *refs[:count], *kept)

    rooms = [pltpu.VMEM(shape, dtype) for shape, dtype in scratch]
    if far:
        rooms += [pltpu.VMEM(a.shape, a.dtype) for a in far]
        rooms.append(pltpu.SemaphoreType.DMA((len(far),)))
    return pl.pallas_call(
        run,
        out_shape=[jax.ShapeDtypeStruct(shape, dtype) for shape, dtype in outs],
        in_specs=[pl.BlockSpec(memory_space=pltpu.SMEM)] + held + waits,
        out_specs=[pl.BlockSpec(memory_space=pltpu.VMEM)] * len(outs),
        scratch_shapes=rooms,
        compiler_params=pltpu.CompilerParams(vmem_limit_bytes=VMEM_LIMIT),
        cost_estimate=pl.CostEstimate(
            flops=us * 10**9, transcendentals=0, bytes_accessed=us * 3 * 10**6
        ),
        name=kernel.__name__,
    )(pos, *args, *far, *behind)


def stacked(parts):
    return jnp.concatenate(parts, axis=0)


def sides(pos, axis, inner, outer):
    even = pos[axis] % 2 == 0
    within = (pos[axis] > 0) & (pos[axis] < 15)

    def far_side(at):
        value = outer[at]
        return jnp.where(within, value, jnp.zeros_like(value))

    def low(*at):
        return jnp.where(even, far_side(at), inner[at])

    def high(*at):
        return jnp.where(even, inner[at], far_side(at))

    return low, high


def give(pos, axis, inner, outer, low, high, at=slice(None)):
    even = pos[axis] % 2 == 0
    inner[at] = jnp.where(even, high, low)
    outer[at] = jnp.where(even, low, high)


def dot_nt(a, b):
    return lax.dot_general(a, b, (((1,), (1,)), ((), ())), preferred_element_type=F32)


def before(values, width):
    place = lax.broadcasted_iota(jnp.int32, values.shape, 0) & (width - 1)
    return jnp.where(place == 0, 0.0, pltpu.roll(values, 1, 0))


def after(values, width):
    place = lax.broadcasted_iota(jnp.int32, values.shape, 0) & (width - 1)
    return jnp.where(place == width - 1, 0.0, pltpu.roll(values, values.shape[0] - 1, 0))


def gathered(wide, width, chans):
    taps = [wide[:, k * chans : (k + 1) * chans] for k in range(3)]
    return before(taps[0], width) + taps[1] + after(taps[2], width)


def scattered(wide, width, chans):
    taps = [wide[:, k * chans : (k + 1) * chans] for k in range(3)]
    return after(taps[0], width) + taps[1] + before(taps[2], width)


def tripled(values, width):
    wide = jnp.concatenate([after(values, width), values, before(values, width)], axis=1)
    return jnp.transpose(wide).astype(BF)


def sigmoid(values):
    return 0.5 * jnp.tanh(0.5 * values) + 0.5


def slope_of(values, sigma):
    return sigma * (1.0 + values * (1.0 - sigma))


def lanes(parts):
    return jnp.concatenate(parts, axis=1)


def back_row(cells, weight, row, rows):
    width, chans = cells.shape[-2:]
    taps = [(depth, height) for depth in range(3) for height in range(3)]
    window = lanes(
        [
            cells[row + 2 - depth, 2 - height : 2 - height + rows].reshape(rows * width, chans)
            for depth, height in taps
        ]
    )
    inner = weight.shape[3]
    turned = lanes([weight[d, h].reshape(3 * inner, chans) for d, h in taps])
    return scattered(dot_nt(window, turned), width, inner)


def input_slabs(pos, own, g_in, g_out, s_in, s_out):
    low, high = sides(pos, 1, g_in, g_out)
    edges = []
    for d in (0, 1):
        cut = slice(d, d + 3)
        edges.append(jnp.concatenate([low(cut), own[cut], high(cut)], axis=1))
    give(pos, 0, s_in, s_out, edges[0], edges[1])


def fill_input(pos, store, own, g_in, g_out, x_in, x_out):
    low, high = sides(pos, 1, g_in, g_out)
    under, over = sides(pos, 0, x_in, x_out)
    lane = lax.broadcasted_iota(jnp.int32, (320, 128), 1)
    for d in range(10):
        if d < 3:
            line = under(d)
        elif d < 7:
            line = jnp.concatenate([low(d - 3), own[d - 3], high(d - 3)], axis=0)
        else:
            line = over(d - 7)
        wide = pltpu.roll(line.reshape(384, 128).astype(F32), 64, 1)
        odd = jnp.where(lane < 64, wide[:320], wide[64:]).astype(BF).reshape(5, 64, 128)
        for m in range(6):
            if m < 5:
                store[d, 2 * m + 1] = odd[m]
            store[d, 2 * m] = line[m]


def encode(
    pos, fetched, own, g_in, g_out, x_in, x_out, cotangent, mean,
    paired, encoded, slope, pooled, bot_slope, bottom, s_in, s_out,
    weight,
):
    fill_input(pos, paired, own, g_in, g_out, x_in, x_out)
    high = pos[0] * 4 - 2
    tall = pos[1] * 4 - 2
    w_enc = fetched(0)
    for depth in range(3):
        for height in range(3):
            at = depth * 256 + height * 64
            weight[at : at + 64, :] = lanes([w_enc[depth, height, k] for k in range(3)])
        weight[depth * 256 + 192 : depth * 256 + 256, :] = jnp.zeros((64, 384), BF)

    place = lax.broadcasted_iota(jnp.int32, (512, 128), 0) // 64 + tall
    across = (place >= 0) & (place < 64)
    for d in range(8):
        window = lanes(
            [
                paired[d + depth, 2 * half + 1 : 2 * half + 9].reshape(512, 128)
                for depth in range(3)
                for half in range(2)
            ]
        )
        pre = gathered(dot(window, weight[...]), 64, 128)
        sigma = sigmoid(pre)
        inside = across & (d + high >= 0) & (d + high < 64)
        encoded[d] = jnp.where(inside, pre * sigma, 0.0).astype(BF).reshape(8, 64, 128)
        slope[d] = jnp.where(inside, slope_of(pre, sigma), 0.0).astype(BF).reshape(8, 64, 128)
    for i in range(4):
        for j in range(4):
            block = encoded[2 * i : 2 * i + 2, 2 * j : 2 * j + 2].reshape(256, 128)
            pooled[i, j] = dot(mean[...], block).astype(BF)
    window = lanes(
        [
            pooled[depth : depth + 2, height : height + 2].reshape(128, 128)
            for depth in range(3)
            for height in range(3)
        ]
    )
    w_bot = fetched(1)
    rows = jnp.concatenate(
        [
            lanes([w_bot[depth, height, k] for k in range(3)])
            for depth in range(3)
            for height in range(3)
        ],
        axis=0,
    )
    pre = gathered(dot(window, rows), 32, 256)
    sigma = sigmoid(pre)
    value = (pre * sigma).astype(BF).reshape(2, 2, 32, 256)
    bottom[...] = value
    bot_slope[...] = slope_of(pre, sigma)
    edges = []
    for h, at in ((0, 0), (1, 3)):
        row = value[:, h].reshape(64, 256)
        edges.append(stacked([cotangent[:, at].reshape(256, 128), row[:, :128], row[:, 128:]]))
    give(pos, 1, s_in, s_out, edges[0], edges[1])


def bottom_slabs(pos, bottom, cotangent, g_in, g_out, s_in, s_out):
    low, high = sides(pos, 1, g_in, g_out)
    edges = []
    for d, b in ((0, 0), (3, 1)):
        cot = slice(64 * d, 64 * d + 64)
        parts = [low(cot), cotangent[d].reshape(256, 128), high(cot)]
        for half in range(2):
            cut = slice(256 + 64 * half + 32 * b, 256 + 64 * half + 32 * b + 32)
            lane = slice(128 * half, 128 * half + 128)
            parts += [low(cut), bottom[b, 0, :, lane], bottom[b, 1, :, lane], high(cut)]
        edges.append(stacked(parts))
    give(pos, 0, s_in, s_out, edges[0], edges[1])


def fill_bottom(pos, wide_bottom, wide_cot, bottom, cotangent, g_in, g_out, x_in, x_out):
    low, high = sides(pos, 1, g_in, g_out)
    for d in range(4):
        cut = slice(64 * d, 64 * d + 64)
        wide_cot[d + 1, 0] = low(cut)
        wide_cot[d + 1, 1:5] = cotangent[d]
        wide_cot[d + 1, 5] = high(cut)
    for b in range(2):
        wide_bottom[b + 1, 1:3] = bottom[b]
        for half in range(2):
            cut = slice(256 + 64 * half + 32 * b, 256 + 64 * half + 32 * b + 32)
            lane = slice(128 * half, 128 * half + 128)
            wide_bottom[b + 1, 0, :, lane] = low(cut)
            wide_bottom[b + 1, 3, :, lane] = high(cut)
    for side, d, b in zip(sides(pos, 0, x_in, x_out), (0, 5), (0, 3)):
        wide_cot[d] = side(slice(0, 384)).reshape(6, 64, 128)
        for half in range(2):
            cut = slice(384 + 128 * half, 512 + 128 * half)
            lane = slice(128 * half, 128 * half + 128)
            wide_bottom[b, :, :, lane] = side(cut).reshape(4, 32, 128)


def decode(
    pos, fetched, own_bottom, own_cot, g_in, g_out, x_in, x_out,
    encoded, bot_slope, stretch, sort,
    decoded, lifted, dec_grad, skip, sorted_lift, bottom_grad,
    lift_all, gstore, bottom, cotangent,
):
    fill_bottom(pos, bottom, cotangent, own_bottom, own_cot, g_in, g_out, x_in, x_out)
    w_up = fetched(0)
    for i in range(4):
        wide = []
        for j in range(4):
            spread = dot(stretch[...], bottom[i, j]).astype(BF)
            wide.append(lanes([spread[:64], spread[64:]]))
        wide = jnp.concatenate(wide, axis=0)
        for a in range(2):
            for b in range(2):
                up = w_up[a, b].reshape(512, 128)
                value = dot(wide, up).astype(BF).reshape(4, 64, 128)
                for j in range(4):
                    lift_all[2 * i + a, 2 * j + b] = value[j]
    lifted[...] = lift_all[1:7, 1:7]

    w_dec = fetched(1)
    for d in range(6):
        wide = None
        for depth in range(3):
            window = lanes(
                [
                    cells[d + depth, height : height + 6].reshape(384, 128)
                    for height in range(3)
                    for cells in (lift_all, encoded)
                ]
            )
            rows = stacked([lanes([w_dec[depth, height, k] for k in range(3)]) for height in range(3)])
            part = dot(window, rows)
            wide = part if wide is None else wide + part
        pre = gathered(wide, 64, 128)
        sigma = sigmoid(pre)
        grad = (cotangent[d].reshape(384, 128).astype(F32) * slope_of(pre, sigma)).astype(BF)
        gstore[d] = grad.reshape(6, 64, 128)
        if 1 <= d <= 4:
            decoded[d - 1] = (pre * sigma).astype(BF).reshape(6, 64, 128)[1:5]
            dec_grad[d - 1] = grad.reshape(6, 64, 128)[1:5]
    pieces = [[], []]
    for d in range(4):
        back = back_row(gstore, w_dec, d, 4)
        skip[d] = back[:, 128:].astype(BF).reshape(4, 64, 128)
        lift = back[:, :128].astype(BF).reshape(4, 64, 128)
        flat = lanes([lift[h] for h in range(4)])
        pieces[d // 2].append(dot(sort[...], flat).astype(BF))
    rows = []
    for i in range(2):
        for j in range(2):
            rows.append(
                lanes(
                    [
                        pieces[i][a][32 * c : 32 * c + 32, 128 * (2 * j + b) : 128 * (2 * j + b) + 128]
                        for a in range(2)
                        for b in range(2)
                        for c in range(2)
                    ]
                )
            )
    rows = jnp.concatenate(rows, axis=0)
    sorted_lift[...] = rows
    up = lanes([w_up[a, b, c] for a in range(2) for b in range(2) for c in range(2)])
    back = dot_nt(rows, up)
    grad = (back * bot_slope[...]).astype(BF)
    bottom_grad[...] = grad.reshape(2, 2, 32, 256)


def grad_edges(pos, grad, skip, s_in, s_out):
    give(pos, 1, s_in, s_out, skip[:, 0].reshape(256, 128), skip[:, 3].reshape(256, 128), slice(0, 256))
    flat = grad[...].reshape(128, 256)
    for half in range(2):
        cut = slice(256 + 128 * half, 384 + 128 * half)
        s_in[cut] = flat[:, 128 * half : 128 * half + 128]
        s_out[cut] = flat[:, 128 * half : 128 * half + 128]


def grad_slabs(pos, grad, skip, g_in, g_out, s_in, s_out):
    low, high = sides(pos, 1, g_in, g_out)
    edges = []
    for d in (0, 3):
        cut = slice(64 * d, 64 * d + 64)
        edges.append(stacked([low(cut), skip[d].reshape(256, 128), high(cut)]))
    give(pos, 0, s_in, s_out, edges[0], edges[1], slice(0, 384))
    for half in range(2):
        lane = slice(128 * half, 128 * half + 128)
        for d in range(2):
            cut = slice(256 + 128 * half + 64 * d, 256 + 128 * half + 64 * d + 64)
            line = stacked([low(cut), grad[d, 0, :, lane], grad[d, 1, :, lane], high(cut)])
            at = 384 + 384 * half + 192 * d
            s_in[at : at + 192] = line
            s_out[at : at + 192] = line


def fill_grad(pos, wide_grad, wide_skip, grad, skip, g_in, g_out, x_in, x_out):
    low, high = sides(pos, 1, g_in, g_out)
    for d in range(4):
        cut = slice(64 * d, 64 * d + 64)
        wide_skip[d + 1, 0] = low(cut)
        wide_skip[d + 1, 1:5] = skip[d]
        wide_skip[d + 1, 5] = high(cut)
    for b in range(2):
        wide_grad[b + 2, 2:4] = grad[b]
        for half in range(2):
            cut = slice(256 + 128 * half + 64 * b, 256 + 128 * half + 64 * b + 64)
            lane = slice(128 * half, 128 * half + 128)
            wide_grad[b + 2, 0:2, :, lane] = low(cut).reshape(2, 32, 128)
            wide_grad[b + 2, 4:6, :, lane] = high(cut).reshape(2, 32, 128)
    for side, d, b in zip(sides(pos, 0, x_in, x_out), (0, 5), (0, 4)):
        wide_skip[d] = side(slice(0, 384)).reshape(6, 64, 128)
        for half in range(2):
            cut = slice(384 + 384 * half, 768 + 384 * half)
            lane = slice(128 * half, 128 * half + 128)
            wide_grad[b : b + 2, :, :, lane] = side(cut).reshape(2, 6, 32, 128)


def put(first, keep, send, at, one, two):
    keep[:, at : at + 128] = jnp.where(first, one, two).astype(BF)
    send[:, at : at + 128] = jnp.where(first, two, one).astype(BF)


def decode_weights(pos, lifted, encoded, dec_grad, keep, send):
    first = pos[0] % 2 == 0
    grad = tripled(dec_grad[...].reshape(1024, 128).astype(F32), 64)
    for depth in range(3):
        for height in range(3):
            window = lanes(
                [
                    lifted[depth : depth + 4, height : height + 4].reshape(1024, 128),
                    encoded[depth + 1 : depth + 5, height + 1 : height + 5].reshape(1024, 128),
                ]
            )
            part = dot(grad, window)
            for k in range(3):
                rows = part[k * 128 : k * 128 + 128]
                at = ((depth * 3 + height) * 3 + k) * 128
                put(first, keep, send, at, rows[:, :128], rows[:, 128:])


def spread_row(row, spread):
    cells = row.reshape(4, 32, 128)
    flat = lanes([cells[h] for h in range(4)])
    upper = flat.astype(BF)
    lower = (flat - upper.astype(F32)).astype(BF)
    return dot(spread[...], jnp.concatenate([upper, lower], axis=0))


def bottom_weights(
    pos, sorted_lift, bottom, pooled, bottom_grad,
    keep, send,
):
    first = pos[0] % 2 == 0
    grad = tripled(bottom_grad[...].reshape(128, 256).astype(F32), 32)
    for depth in range(3):
        window = lanes(
            [
                pooled[depth : depth + 2, height : height + 2].reshape(128, 128)
                for height in range(3)
            ]
        )
        part = dot(grad, window)
        for k in range(3):
            rows = part[k * 256 : k * 256 + 256].reshape(16, 2, 8, 384)
            one, two = rows[:, 0].reshape(128, 384), rows[:, 1].reshape(128, 384)
            for height in range(3):
                at = ((depth * 3 + height) * 3 + k) * 128
                cut = slice(height * 128, height * 128 + 128)
                put(first, keep, send, at, one[:, cut], two[:, cut])
    part = dot(
        jnp.transpose(sorted_lift[...].astype(F32)).astype(BF), bottom[...].reshape(128, 256)
    )
    for t in range(8):
        rows = part[t * 128 : t * 128 + 128]
        put(first, keep, send, 3456 + t * 128, rows[:, :128], rows[:, 128:])


def encode_weights(
    pos, fetched, bottom_grad, skip, slope, paired, spread,
    keep, send,
    bstore, turned,
):
    first = pos[0] % 2 == 0
    bstore[...] = jnp.zeros((6, 6, 32, 256), BF)
    bstore[2:4, 2:4] = bottom_grad[...]
    w_bot = fetched(0)
    for d in range(4):
        wide = spread_row(back_row(bstore, w_bot, d, 4), spread)
        for f in (2 * d, 2 * d + 1):
            cells = []
            for h in range(8):
                value = wide[:, h // 2 * 128 : h // 2 * 128 + 128]
                if 2 <= f < 6 and 2 <= h < 6:
                    value = value + skip[f - 2, h - 2].astype(F32)
                cells.append(value * slope[f, h].astype(F32))
            row = jnp.concatenate(cells, axis=0).astype(BF).astype(F32)
            turned[:, f * 512 : f * 512 + 512] = tripled(row, 64)

    lane = lax.broadcasted_iota(jnp.int32, (4096, 128), 1)

    def window(depth, height):
        return paired[depth : depth + 8, height + 1 : height + 9].reshape(4096, 128)

    blocks = [window(0, 0), window(1, 0), window(2, 0)]
    blocks.append(jnp.where(lane < 64, window(0, 2), window(1, 1)))
    blocks.append(jnp.where(lane < 64, window(2, 2), window(2, 1)))
    parts = []
    for n in (0, 2, 4):
        part = dot(turned[...], lanes(blocks[n : n + 2]))
        parts += [part[:, m * 128 : m * 128 + 128] for m in range(part.shape[1] // 128)]
    cut = [[part[k * 128 : k * 128 + 128] for k in range(3)] for part in parts]
    small = lax.broadcasted_iota(jnp.int32, (128, 128), 1)
    final = cut[0] + cut[1] + cut[2] + cut[3]
    final += [jnp.where(small < 64, cut[4][0], cut[4][1]), cut[4][2]]
    for n in range(7):
        put(first, keep, send, n * 128, final[n], final[n + 7])


def encode_back(
    pos, fetched, own_grad, own_skip, g_in, g_out, x_in, x_out, slope, spread,
    pool_grad, input_grad, done,
    gstore, grad, skip,
):
    done[...] = jnp.zeros((8, 128), F32)
    fill_grad(pos, grad, skip, own_grad, own_skip, g_in, g_out, x_in, x_out)
    w_bot = fetched(0)
    for d in range(4):
        row = back_row(grad, w_bot, d, 4)
        if 1 <= d <= 2:
            pool_grad[d - 1] = row.reshape(4, 32, 128)[1:3]
        wide = spread_row(row, spread)
        for f in range(6):
            if (f + 1) // 2 != d:
                continue
            for h in range(6):
                at = (h + 1) // 2 * 128
                value = skip[f, h].astype(F32) + wide[:, at : at + 128]
                gstore[f, h] = (value * slope[f + 1, h + 1].astype(F32)).astype(BF)
    w_enc = fetched(1)
    for d in range(4):
        input_grad[d] = back_row(gstore, w_enc, d, 4).astype(BF).reshape(4, 64, 64)


def swap(inner, outer, axis):
    count = lax.axis_size(axis)
    pairs = [(i, (i + 1) % count) for i in range(1, count, 2)]
    pairs += [(j, i) for i, j in pairs]
    got = lax.ppermute(inner, axis, [(i, i ^ 1) for i in range(count)])
    return got, lax.ppermute(outer, axis, pairs)


def add_cores(pos, *refs):
    total = refs[-1]
    at = 0
    for keep, got in zip(refs[0:-1:2], refs[1:-1:2]):
        width = keep.shape[1]
        total[:, at : at + width] = (keep[...].astype(F32) + got[...].astype(F32)).astype(BF)
        at += width


def add_heights(pos, parts, chunks):
    filled = parts.shape[2] // 128
    for n in range(64):
        if n < filled:
            cut = slice(128 * n, 128 * n + 128)
            total = parts[0, :, cut].astype(F32)
            for j in range(1, 16):
                total = total + parts[j, :, cut].astype(F32)
        else:
            total = jnp.zeros((8, 128), F32)
        at = 128 * (n % 8)
        chunks[n // 8, :, at : at + 128] = total.astype(BF)


def added(parts):
    total = parts[0].astype(F32)
    for j in range(1, parts.shape[0]):
        total = total + parts[j].astype(F32)
    return total


def add_depths(pos, chunks, parts, copies):
    total = added(chunks).astype(BF)
    rest = added(parts).astype(BF)
    for j in range(8):
        copies[j, :, :1024] = total
        copies[j, :, 1024:] = rest


def finish(pos, mine, other, grad_enc, grad_bot, grad_up, grad_dec):
    first = pos[0] % 2 == 0

    def halves(left, right):
        return jnp.where(first, left, right), jnp.where(first, right, left)

    def block(n):
        cut = slice(128 * (n % 8), 128 * (n % 8) + 128)
        return halves(mine[n // 8, :, cut].astype(F32), other[n // 8, :, cut].astype(F32))

    for t in range(27):
        grad_dec[t, :, :128], grad_dec[t, :, 128:] = block(t)
        grad_bot[t, :8], grad_bot[t, 8:] = block(27 + t)
    for t in range(8):
        grad_up[t, :, :128], grad_up[t, :, 128:] = block(54 + t)
    pairs = []
    for n in range(7):
        cut = slice(1024 + 128 * n, 1152 + 128 * n)
        pairs.append(halves(added(mine.at[:, :, cut]), added(other.at[:, :, cut])))
    pieces = [p[0] for p in pairs] + [p[1] for p in pairs]

    def tap(depth, height, k):
        return (depth * 3 + height) * 3 + k

    for k in range(3):
        for depth in range(3):
            piece = pieces[depth * 3 + k]
            grad_enc[tap(depth, 0, k)] = piece[:, :64]
            grad_enc[tap(depth, 1, k)] = piece[:, 64:]
        grad_enc[tap(0, 2, k)] = pieces[9 + k][:, :64]
        grad_enc[tap(1, 2, k)] = pieces[9 + k][:, 64:]
    grad_enc[tap(2, 2, 0)] = pieces[12][:, :64]
    grad_enc[tap(2, 2, 1)] = pieces[12][:, 64:]
    grad_enc[tap(2, 2, 2)] = pieces[13][:, :64]


def other_core(values):
    return lax.ppermute(values, "gx", [(i, i ^ 1) for i in range(lax.axis_size("gx"))])


def to_owners(part):
    return lax.all_to_all(part.reshape(16, 8, part.shape[1]), "gy", 0, 0, tiled=True)


def over_chips(chunks):
    groups = [[2 * a + b for a in range(8)] for b in range(2)]
    return lax.all_to_all(chunks, "gx", 0, 0, tiled=True, axis_index_groups=groups)


def constants():
    w, k = np.arange(64)[:, None], np.arange(32)[None, :]
    mean = np.tile((w // 2 == k).T * 0.125, (1, 4))
    stretch = np.concatenate([w == 2 * k, w == 2 * k + 1], axis=0)
    sort = np.concatenate([(w == 2 * k).T, (w == 2 * k + 1).T], axis=0)
    spread = np.concatenate([(w // 2 == k) * 0.125] * 2, axis=1)
    return [jnp.asarray(v, BF) for v in (mean, stretch, sort, spread)]


def shards(inputs, cotangent, w_enc, w_bot, w_up, w_dec):
    mean, stretch, sort, spread = constants()
    pos = jnp.stack([lax.axis_index("gx"), lax.axis_index("gy")]).astype(jnp.int32)
    own = jnp.concatenate([inputs[:, 0::2], inputs[:, 1::2]], axis=3)
    near = swap(own, own, "gy")
    slabs = call(input_slabs, [((3, 6, 64, 128), BF)] * 2, [], pos, own, *near)
    near += swap(*slabs, "gx")
    paired, encoded, slope, pooled, bot_slope, bottom, *slabs = call(
        encode,
        [
            ((10, 11, 64, 128), BF),
            ((8, 8, 64, 128), BF),
            ((8, 8, 64, 128), BF),
            ((4, 4, 32, 128), BF),
            ((128, 256), F32),
            ((2, 2, 32, 256), BF),
        ]
        + [((384, 128), BF)] * 2,
        [((768, 384), BF)],
        pos, own, *near, cotangent, mean, far=(w_enc, w_bot),
        us=6,
    )
    near = swap(*slabs, "gy")
    slabs = call(bottom_slabs, [((640, 128), BF)] * 2, [], pos, bottom, cotangent, *near)
    near += swap(*slabs, "gx")
    decoded, lifted, dec_grad, skip, sorted_lift, bottom_grad = call(
        decode,
        [
            ((4, 4, 64, 128), BF),
            ((6, 6, 64, 128), BF),
            ((4, 4, 64, 128), BF),
            ((4, 4, 64, 128), BF),
            ((128, 1024), BF),
            ((2, 2, 32, 256), BF),
        ],
        [
            ((8, 8, 64, 128), BF),
            ((6, 6, 64, 128), BF),
            ((4, 4, 32, 256), BF),
            ((6, 6, 64, 128), BF),
        ],
        pos, bottom, cotangent, *near, encoded, bot_slope, stretch, sort, far=(w_up, w_dec),
        us=13,
    )
    slabs = call(grad_edges, [((512, 128), BF)] * 2, [], pos, bottom_grad, skip)
    near = swap(*slabs, "gy")
    keep, send = call(
        decode_weights,
        [((128, 3456), BF)] * 2,
        [],
        pos, lifted, encoded, dec_grad,
        behind=slabs[:1],
        us=3,
    )
    part_dec = [keep, other_core(send)]
    keep, send = call(
        bottom_weights,
        [((128, 4480), BF)] * 2,
        [],
        pos, sorted_lift, bottom, pooled, bottom_grad,
        us=2,
    )
    (part_main,) = call(
        add_cores, [((128, 7936), BF)], [], pos, *part_dec, keep, other_core(send), behind=near
    )
    keep, send = call(
        encode_weights,
        [((128, 896), BF)] * 2,
        [((6, 6, 32, 256), BF), ((384, 4096), BF)],
        pos, bottom_grad, skip, slope, paired, spread,
        far=(w_bot,), behind=(part_main,),
        us=6,
    )
    part_enc = [keep, other_core(send)]
    slabs = call(
        grad_slabs, [((1152, 128), BF)] * 2, [], pos, bottom_grad, skip, *near,
        behind=(part_main,),
    )
    part_main = to_owners(part_main)
    near += swap(*slabs, "gx")
    pool_grad, input_grad, done = call(
        encode_back,
        [((2, 2, 32, 128), F32), ((4, 4, 64, 64), BF), ((8, 128), F32)],
        [((6, 6, 64, 128), BF), ((6, 6, 32, 256), BF), ((6, 6, 64, 128), BF)],
        pos, bottom_grad, skip, *near, slope, spread,
        far=(w_bot, w_enc),
        us=5,
    )
    (part_enc,) = call(add_cores, [((128, 896), BF)], [], pos, *part_enc, behind=(done,))
    (chunks,) = call(
        add_heights, [((8, 8, 1024), BF)], [], pos, part_main, behind=(done,), us=2
    )
    chunks = over_chips(chunks)
    part_enc = to_owners(part_enc)
    (copies,) = call(add_depths, [((8, 8, 1920), BF)], [], pos, chunks, part_enc)
    mine = over_chips(copies)
    other = other_core(mine)
    grads = call(
        finish,
        [((27, 8, 64), F32), ((27, 16, 128), F32), ((8, 8, 256), F32), ((27, 8, 256), F32)],
        [],
        pos, mine, other,
    )
    grad_enc, grad_bot, grad_up, grad_dec = (
        jnp.transpose(grad, (0, 2, 1)).reshape(*shape, grad.shape[2], grad.shape[1])
        for grad, shape in zip(grads, ((3, 3, 3), (3, 3, 3), (2, 2, 2), (3, 3, 3)))
    )
    return (decoded, input_grad, grad_enc, grad_bot, grad_up, grad_dec, pool_grad)


def solution(mesh):
    in_specs = (P("gx", "gy", None, None), P("gx", "gy", None, None), P(), P(), P(), P())
    out_specs = (
        P("gx", "gy", None, None),
        P("gx", "gy", None, None),
        P(None, None, None, None, "gy"),
        P(None, None, None, None, "gy"),
        P(None, None, None, None, "gy"),
        P(None, None, None, None, "gy"),
        P("gx", "gy", None, None),
    )
    return jax.shard_map(shards, mesh=mesh, in_specs=in_specs, out_specs=out_specs, check_vma=False)
```

```python
import jax
import jax.numpy as jnp
import numpy as np
from jax import lax
from jax.experimental import pallas as pl
from jax.experimental.pallas import tpu as pltpu
from jax.sharding import PartitionSpec as P

BF = jnp.bfloat16
F32 = jnp.float32
VMEM_LIMIT = 24 * 1024 * 1024


def dot(a, b):
    return jnp.dot(a, b, preferred_element_type=F32)


def call(kernel, outs, scratch, pos, *args, far=(), behind=(), us=1):
    held = [pl.BlockSpec(memory_space=pltpu.VMEM)] * len(args)
    waits = [pl.BlockSpec(memory_space=pltpu.HBM)] * len(far)
    waits += [pl.BlockSpec(memory_space=pl.ANY)] * len(behind)
    count = len(args)

    def run(place, *refs):
        own = refs[count + len(waits) :]
        copies = []
        for n in range(len(far)):
            room = own[len(own) - 1 - len(far) + n]
            copies.append(pltpu.make_async_copy(refs[count + n], room, own[-1].at[n]))
            copies[-1].start()

        def fetched(n):
            copies[n].wait()
            return own[len(own) - 1 - len(far) + n]

        extra = (fetched,) if far else ()
        kept = own[: len(own) - 1 - len(far)] if far else own
        return kernel(place, *extra, *refs[:count], *kept)

    rooms = [pltpu.VMEM(shape, dtype) for shape, dtype in scratch]
    if far:
        rooms += [pltpu.VMEM(a.shape, a.dtype) for a in far]
        rooms.append(pltpu.SemaphoreType.DMA((len(far),)))
    return pl.pallas_call(
        run,
        out_shape=[jax.ShapeDtypeStruct(shape, dtype) for shape, dtype in outs],
        in_specs=[pl.BlockSpec(memory_space=pltpu.SMEM)] + held + waits,
        out_specs=[pl.BlockSpec(memory_space=pltpu.VMEM)] * len(outs),
        scratch_shapes=rooms,
        compiler_params=pltpu.CompilerParams(vmem_limit_bytes=VMEM_LIMIT),
        cost_estimate=pl.CostEstimate(
            flops=us * 10**9, transcendentals=0, bytes_accessed=us * 3 * 10**6
        ),
        name=kernel.__name__,
    )(pos, *args, *far, *behind)


def stacked(parts):
    return jnp.concatenate(parts, axis=0)


def sides(pos, axis, inner, outer):
    even = pos[axis] % 2 == 0
    within = (pos[axis] > 0) & (pos[axis] < 15)

    def far_side(at):
        value = outer[at]
        return jnp.where(within, value, jnp.zeros_like(value))

    def low(*at):
        return jnp.where(even, far_side(at), inner[at])

    def high(*at):
        return jnp.where(even, inner[at], far_side(at))

    return low, high


def give(pos, axis, inner, outer, low, high, at=slice(None)):
    even = pos[axis] % 2 == 0
    inner[at] = jnp.where(even, high, low)
    outer[at] = jnp.where(even, low, high)


def dot_nt(a, b):
    return lax.dot_general(a, b, (((1,), (1,)), ((), ())), preferred_element_type=F32)


def before(values, width):
    place = lax.broadcasted_iota(jnp.int32, values.shape, 0) & (width - 1)
    return jnp.where(place == 0, 0.0, pltpu.roll(values, 1, 0))


def after(values, width):
    place = lax.broadcasted_iota(jnp.int32, values.shape, 0) & (width - 1)
    return jnp.where(place == width - 1, 0.0, pltpu.roll(values, values.shape[0] - 1, 0))


def gathered(wide, width, chans):
    taps = [wide[:, k * chans : (k + 1) * chans] for k in range(3)]
    return before(taps[0], width) + taps[1] + after(taps[2], width)


def scattered(wide, width, chans):
    taps = [wide[:, k * chans : (k + 1) * chans] for k in range(3)]
    return after(taps[0], width) + taps[1] + before(taps[2], width)


def tripled(values, width):
    wide = jnp.concatenate([after(values, width), values, before(values, width)], axis=1)
    return jnp.transpose(wide).astype(BF)


def sigmoid(values):
    return 0.5 * jnp.tanh(0.5 * values) + 0.5


def slope_of(values, sigma):
    return sigma * (1.0 + values * (1.0 - sigma))


def lanes(parts):
    return jnp.concatenate(parts, axis=1)


def transposed(cells, weight):
    depths, rows, width, chans = cells.shape
    depths, rows = depths - 2, rows - 2
    taps = [(depth, height) for depth in range(3) for height in range(3)]
    window = lanes(
        [
            cells[2 - d : 2 - d + depths, 2 - h : 2 - h + rows].reshape(depths * rows * width, chans)
            for d, h in taps
        ]
    )
    inner = weight.shape[3]
    turned = lanes([weight[d, h].reshape(3 * inner, chans) for d, h in taps])
    return scattered(dot_nt(window, turned), width, inner)


def input_slabs(pos, own, g_in, g_out, s_in, s_out):
    low, high = sides(pos, 1, g_in, g_out)
    edges = []
    for d in (0, 1):
        cut = slice(d, d + 3)
        edges.append(jnp.concatenate([low(cut), own[cut], high(cut)], axis=1))
    give(pos, 0, s_in, s_out, edges[0], edges[1])


def fill_input(pos, store, own, g_in, g_out, x_in, x_out):
    low, high = sides(pos, 1, g_in, g_out)
    under, over = sides(pos, 0, x_in, x_out)
    lane = lax.broadcasted_iota(jnp.int32, (320, 128), 1)
    for d in range(10):
        if d < 3:
            line = under(d)
        elif d < 7:
            line = jnp.concatenate([low(d - 3), own[d - 3], high(d - 3)], axis=0)
        else:
            line = over(d - 7)
        wide = pltpu.roll(line.reshape(384, 128).astype(F32), 64, 1)
        odd = jnp.where(lane < 64, wide[:320], wide[64:]).astype(BF).reshape(5, 64, 128)
        for m in range(6):
            if m < 5:
                store[d, 2 * m + 1] = odd[m]
            store[d, 2 * m] = line[m]


def encode(
    pos, fetched, own, g_in, g_out, x_in, x_out, cotangent, mean,
    paired, encoded, slope, pooled, bot_slope, bottom, s_in, s_out,
    weight,
):
    fill_input(pos, paired, own, g_in, g_out, x_in, x_out)
    high = pos[0] * 4 - 2
    tall = pos[1] * 4 - 2
    w_enc = fetched(0)
    for depth in range(3):
        for height in range(3):
            at = depth * 256 + height * 64
            weight[at : at + 64, :] = lanes([w_enc[depth, height, k] for k in range(3)])
        weight[depth * 256 + 192 : depth * 256 + 256, :] = jnp.zeros((64, 384), BF)

    place = lax.broadcasted_iota(jnp.int32, (512, 128), 0) // 64 + tall
    across = (place >= 0) & (place < 64)
    for d in range(8):
        window = lanes(
            [
                paired[d + depth, 2 * half + 1 : 2 * half + 9].reshape(512, 128)
                for depth in range(3)
                for half in range(2)
            ]
        )
        pre = gathered(dot(window, weight[...]), 64, 128)
        sigma = sigmoid(pre)
        inside = across & (d + high >= 0) & (d + high < 64)
        encoded[d] = jnp.where(inside, pre * sigma, 0.0).astype(BF).reshape(8, 64, 128)
        slope[d] = jnp.where(inside, slope_of(pre, sigma), 0.0).astype(BF).reshape(8, 64, 128)
    for i in range(4):
        for j in range(4):
            block = encoded[2 * i : 2 * i + 2, 2 * j : 2 * j + 2].reshape(256, 128)
            pooled[i, j] = dot(mean[...], block).astype(BF)
    window = lanes(
        [
            pooled[depth : depth + 2, height : height + 2].reshape(128, 128)
            for depth in range(3)
            for height in range(3)
        ]
    )
    w_bot = fetched(1)
    rows = jnp.concatenate(
        [
            lanes([w_bot[depth, height, k] for k in range(3)])
            for depth in range(3)
            for height in range(3)
        ],
        axis=0,
    )
    pre = gathered(dot(window, rows), 32, 256)
    sigma = sigmoid(pre)
    value = (pre * sigma).astype(BF).reshape(2, 2, 32, 256)
    bottom[...] = value
    bot_slope[...] = slope_of(pre, sigma)
    edges = []
    for h, at in ((0, 0), (1, 3)):
        row = value[:, h].reshape(64, 256)
        edges.append(stacked([cotangent[:, at].reshape(256, 128), row[:, :128], row[:, 128:]]))
    give(pos, 1, s_in, s_out, edges[0], edges[1])


def bottom_slabs(pos, bottom, cotangent, g_in, g_out, s_in, s_out):
    low, high = sides(pos, 1, g_in, g_out)
    edges = []
    for d, b in ((0, 0), (3, 1)):
        cot = slice(64 * d, 64 * d + 64)
        parts = [low(cot), cotangent[d].reshape(256, 128), high(cot)]
        for half in range(2):
            cut = slice(256 + 64 * half + 32 * b, 256 + 64 * half + 32 * b + 32)
            lane = slice(128 * half, 128 * half + 128)
            parts += [low(cut), bottom[b, 0, :, lane], bottom[b, 1, :, lane], high(cut)]
        edges.append(stacked(parts))
    give(pos, 0, s_in, s_out, edges[0], edges[1])


def fill_bottom(pos, wide_bottom, wide_cot, bottom, cotangent, g_in, g_out, x_in, x_out):
    low, high = sides(pos, 1, g_in, g_out)
    for d in range(4):
        cut = slice(64 * d, 64 * d + 64)
        wide_cot[d + 1, 0] = low(cut)
        wide_cot[d + 1, 1:5] = cotangent[d]
        wide_cot[d + 1, 5] = high(cut)
    for b in range(2):
        wide_bottom[b + 1, 1:3] = bottom[b]
        for half in range(2):
            cut = slice(256 + 64 * half + 32 * b, 256 + 64 * half + 32 * b + 32)
            lane = slice(128 * half, 128 * half + 128)
            wide_bottom[b + 1, 0, :, lane] = low(cut)
            wide_bottom[b + 1, 3, :, lane] = high(cut)
    for side, d, b in zip(sides(pos, 0, x_in, x_out), (0, 5), (0, 3)):
        wide_cot[d] = side(slice(0, 384)).reshape(6, 64, 128)
        for half in range(2):
            cut = slice(384 + 128 * half, 512 + 128 * half)
            lane = slice(128 * half, 128 * half + 128)
            wide_bottom[b, :, :, lane] = side(cut).reshape(4, 32, 128)


def decode(
    pos, fetched, own_bottom, own_cot, g_in, g_out, x_in, x_out,
    encoded, bot_slope, stretch, sort,
    decoded, lifted, dec_grad, skip, sorted_lift, bottom_grad, s_in, s_out,
    lift_all, gstore, bottom, cotangent,
):
    fill_bottom(pos, bottom, cotangent, own_bottom, own_cot, g_in, g_out, x_in, x_out)
    w_up = fetched(0)
    for i in range(4):
        wide = []
        for j in range(4):
            spread = dot(stretch[...], bottom[i, j]).astype(BF)
            wide.append(lanes([spread[:64], spread[64:]]))
        wide = jnp.concatenate(wide, axis=0)
        for a in range(2):
            for b in range(2):
                up = w_up[a, b].reshape(512, 128)
                value = dot(wide, up).astype(BF).reshape(4, 64, 128)
                for j in range(4):
                    lift_all[2 * i + a, 2 * j + b] = value[j]
    lifted[...] = lift_all[1:7, 1:7]

    w_dec = fetched(1)
    for d in range(0, 6, 2):
        wide = None
        for depth in range(3):
            window = lanes(
                [
                    cells[d + depth : d + depth + 2, height : height + 6].reshape(768, 128)
                    for height in range(3)
                    for cells in (lift_all, encoded)
                ]
            )
            rows = stacked([lanes([w_dec[depth, height, k] for k in range(3)]) for height in range(3)])
            part = dot(window, rows)
            wide = part if wide is None else wide + part
        pre = gathered(wide, 64, 128)
        sigma = sigmoid(pre)
        cot = cotangent[d : d + 2].reshape(768, 128).astype(F32)
        grad = (cot * slope_of(pre, sigma)).astype(BF).reshape(2, 6, 64, 128)
        value = (pre * sigma).astype(BF).reshape(2, 6, 64, 128)
        gstore[d : d + 2] = grad
        for n in range(2):
            if 1 <= d + n <= 4:
                decoded[d + n - 1] = value[n, 1:5]
                dec_grad[d + n - 1] = grad[n, 1:5]
    pieces = [[], []]
    back_all = transposed(gstore, w_dec)
    for d in range(4):
        back = back_all[256 * d : 256 * d + 256]
        skip[d] = back[:, 128:].astype(BF).reshape(4, 64, 128)
        lift = back[:, :128].astype(BF).reshape(4, 64, 128)
        flat = lanes([lift[h] for h in range(4)])
        pieces[d // 2].append(dot(sort[...], flat).astype(BF))
    rows = []
    for i in range(2):
        for j in range(2):
            rows.append(
                lanes(
                    [
                        pieces[i][a][32 * c : 32 * c + 32, 128 * (2 * j + b) : 128 * (2 * j + b) + 128]
                        for a in range(2)
                        for b in range(2)
                        for c in range(2)
                    ]
                )
            )
    rows = jnp.concatenate(rows, axis=0)
    sorted_lift[...] = rows
    up = lanes([w_up[a, b, c] for a in range(2) for b in range(2) for c in range(2)])
    back = dot_nt(rows, up)
    grad = (back * bot_slope[...]).astype(BF)
    bottom_grad[...] = grad.reshape(2, 2, 32, 256)
    give(pos, 1, s_in, s_out, skip[:, 0].reshape(256, 128), skip[:, 3].reshape(256, 128), slice(0, 256))
    for half in range(2):
        cut = slice(256 + 128 * half, 384 + 128 * half)
        s_in[cut] = grad[:, 128 * half : 128 * half + 128]
        s_out[cut] = grad[:, 128 * half : 128 * half + 128]


def grad_slabs(pos, grad, skip, g_in, g_out, s_in, s_out):
    low, high = sides(pos, 1, g_in, g_out)
    edges = []
    for d in (0, 3):
        cut = slice(64 * d, 64 * d + 64)
        edges.append(stacked([low(cut), skip[d].reshape(256, 128), high(cut)]))
    give(pos, 0, s_in, s_out, edges[0], edges[1], slice(0, 384))
    for half in range(2):
        lane = slice(128 * half, 128 * half + 128)
        for d in range(2):
            cut = slice(256 + 128 * half + 64 * d, 256 + 128 * half + 64 * d + 64)
            line = stacked([low(cut), grad[d, 0, :, lane], grad[d, 1, :, lane], high(cut)])
            at = 384 + 384 * half + 192 * d
            s_in[at : at + 192] = line
            s_out[at : at + 192] = line


def fill_grad(pos, wide_grad, wide_skip, grad, skip, g_in, g_out, x_in, x_out):
    low, high = sides(pos, 1, g_in, g_out)
    for d in range(4):
        cut = slice(64 * d, 64 * d + 64)
        wide_skip[d + 1, 0] = low(cut)
        wide_skip[d + 1, 1:5] = skip[d]
        wide_skip[d + 1, 5] = high(cut)
    for b in range(2):
        wide_grad[b + 2, 2:4] = grad[b]
        for half in range(2):
            cut = slice(256 + 128 * half + 64 * b, 256 + 128 * half + 64 * b + 64)
            lane = slice(128 * half, 128 * half + 128)
            wide_grad[b + 2, 0:2, :, lane] = low(cut).reshape(2, 32, 128)
            wide_grad[b + 2, 4:6, :, lane] = high(cut).reshape(2, 32, 128)
    for side, d, b in zip(sides(pos, 0, x_in, x_out), (0, 5), (0, 4)):
        wide_skip[d] = side(slice(0, 384)).reshape(6, 64, 128)
        for half in range(2):
            cut = slice(384 + 384 * half, 768 + 384 * half)
            lane = slice(128 * half, 128 * half + 128)
            wide_grad[b : b + 2, :, :, lane] = side(cut).reshape(2, 6, 32, 128)


def put(first, keep, send, at, one, two):
    keep[:, at : at + 128] = jnp.where(first, one, two).astype(BF)
    send[:, at : at + 128] = jnp.where(first, two, one).astype(BF)


def decode_weights(pos, lifted, encoded, dec_grad, keep, send):
    first = pos[0] % 2 == 0
    grad = tripled(dec_grad[...].reshape(1024, 128).astype(F32), 64)
    for depth in range(3):
        for height in range(3):
            window = lanes(
                [
                    lifted[depth : depth + 4, height : height + 4].reshape(1024, 128),
                    encoded[depth + 1 : depth + 5, height + 1 : height + 5].reshape(1024, 128),
                ]
            )
            part = dot(grad, window)
            for k in range(3):
                rows = part[k * 128 : k * 128 + 128]
                at = ((depth * 3 + height) * 3 + k) * 128
                put(first, keep, send, at, rows[:, :128], rows[:, 128:])


def spread_row(row, spread):
    cells = row.reshape(4, 32, 128)
    flat = lanes([cells[h] for h in range(4)])
    upper = flat.astype(BF)
    lower = (flat - upper.astype(F32)).astype(BF)
    return dot(spread[...], jnp.concatenate([upper, lower], axis=0))


def bottom_weights(
    pos, sorted_lift, bottom, pooled, bottom_grad,
    keep, send,
):
    first = pos[0] % 2 == 0
    grad = tripled(bottom_grad[...].reshape(128, 256).astype(F32), 32)
    for depth in range(3):
        window = lanes(
            [
                pooled[depth : depth + 2, height : height + 2].reshape(128, 128)
                for height in range(3)
            ]
        )
        part = dot(grad, window)
        for k in range(3):
            rows = part[k * 256 : k * 256 + 256].reshape(16, 2, 8, 384)
            one, two = rows[:, 0].reshape(128, 384), rows[:, 1].reshape(128, 384)
            for height in range(3):
                at = ((depth * 3 + height) * 3 + k) * 128
                cut = slice(height * 128, height * 128 + 128)
                put(first, keep, send, at, one[:, cut], two[:, cut])
    part = dot(
        jnp.transpose(sorted_lift[...].astype(F32)).astype(BF), bottom[...].reshape(128, 256)
    )
    for t in range(8):
        rows = part[t * 128 : t * 128 + 128]
        put(first, keep, send, 3456 + t * 128, rows[:, :128], rows[:, 128:])


def encode_weights(
    pos, fetched, bottom_grad, skip, slope, paired, spread,
    keep, send,
    bstore, turned,
):
    first = pos[0] % 2 == 0
    bstore[...] = jnp.zeros((6, 6, 32, 256), BF)
    bstore[2:4, 2:4] = bottom_grad[...]
    w_bot = fetched(0)
    back = transposed(bstore, w_bot)
    for d in range(4):
        wide = spread_row(back[128 * d : 128 * d + 128], spread)
        for f in (2 * d, 2 * d + 1):
            cells = []
            for h in range(8):
                value = wide[:, h // 2 * 128 : h // 2 * 128 + 128]
                if 2 <= f < 6 and 2 <= h < 6:
                    value = value + skip[f - 2, h - 2].astype(F32)
                cells.append(value * slope[f, h].astype(F32))
            row = jnp.concatenate(cells, axis=0).astype(BF).astype(F32)
            turned[:, f * 512 : f * 512 + 512] = tripled(row, 64)

    lane = lax.broadcasted_iota(jnp.int32, (4096, 128), 1)

    def window(depth, height):
        return paired[depth : depth + 8, height + 1 : height + 9].reshape(4096, 128)

    blocks = [window(0, 0), window(1, 0), window(2, 0)]
    blocks.append(jnp.where(lane < 64, window(0, 2), window(1, 1)))
    blocks.append(jnp.where(lane < 64, window(2, 2), window(2, 1)))
    parts = []
    for n in (0, 2, 4):
        part = dot(turned[...], lanes(blocks[n : n + 2]))
        parts += [part[:, m * 128 : m * 128 + 128] for m in range(part.shape[1] // 128)]
    cut = [[part[k * 128 : k * 128 + 128] for k in range(3)] for part in parts]
    small = lax.broadcasted_iota(jnp.int32, (128, 128), 1)
    final = cut[0] + cut[1] + cut[2] + cut[3]
    final += [jnp.where(small < 64, cut[4][0], cut[4][1]), cut[4][2]]
    for n in range(7):
        put(first, keep, send, n * 128, final[n], final[n + 7])


def encode_back(
    pos, fetched, own_grad, own_skip, g_in, g_out, x_in, x_out, slope, spread,
    pool_grad, input_grad, done,
    gstore, grad, skip,
):
    done[...] = jnp.zeros((8, 128), F32)
    fill_grad(pos, grad, skip, own_grad, own_skip, g_in, g_out, x_in, x_out)
    w_bot = fetched(0)
    back = transposed(grad, w_bot)
    for d in range(4):
        row = back[128 * d : 128 * d + 128]
        if 1 <= d <= 2:
            pool_grad[d - 1] = row.reshape(4, 32, 128)[1:3]
        wide = spread_row(row, spread)
        for f in range(6):
            if (f + 1) // 2 != d:
                continue
            for h in range(6):
                at = (h + 1) // 2 * 128
                value = skip[f, h].astype(F32) + wide[:, at : at + 128]
                gstore[f, h] = (value * slope[f + 1, h + 1].astype(F32)).astype(BF)
    w_enc = fetched(1)
    input_grad[...] = transposed(gstore, w_enc).astype(BF).reshape(4, 4, 64, 64)


def swap(inner, outer, axis):
    count = lax.axis_size(axis)
    pairs = [(i, (i + 1) % count) for i in range(1, count, 2)]
    pairs += [(j, i) for i, j in pairs]
    got = lax.ppermute(inner, axis, [(i, i ^ 1) for i in range(count)])
    return got, lax.ppermute(outer, axis, pairs)


def add_cores(pos, *refs):
    total = refs[-1]
    at = 0
    for keep, got in zip(refs[0:-1:2], refs[1:-1:2]):
        width = keep.shape[1]
        total[:, at : at + width] = (keep[...].astype(F32) + got[...].astype(F32)).astype(BF)
        at += width


def add_heights(pos, parts, chunks):
    filled = parts.shape[2] // 128
    for n in range(9 * chunks.shape[0]):
        if n < filled:
            cut = slice(128 * n, 128 * n + 128)
            total = parts[0, :, cut].astype(F32)
            for j in range(1, 16):
                total = total + parts[j, :, cut].astype(F32)
        else:
            total = jnp.zeros((8, 128), F32)
        at = 128 * (n % 9)
        chunks[n // 9, :, at : at + 128] = total.astype(BF)


def add_depths(pos, parts, copies):
    total = parts[0].astype(F32)
    for j in range(1, 8):
        total = total + parts[j].astype(F32)
    total = total.astype(BF)
    for j in range(8):
        copies[j] = total


def finish(pos, mine, other, grad_enc, grad_bot, grad_up, grad_dec):
    first = pos[0] % 2 == 0

    def block(n):
        cut = slice(128 * (n % 9), 128 * (n % 9) + 128)
        left, right = mine[n // 9, :, cut].astype(F32), other[n // 9, :, cut].astype(F32)
        return jnp.where(first, left, right), jnp.where(first, right, left)

    for t in range(27):
        grad_dec[t, :, :128], grad_dec[t, :, 128:] = block(t)
        grad_bot[t, :8], grad_bot[t, 8:] = block(27 + t)
    for t in range(8):
        grad_up[t, :, :128], grad_up[t, :, 128:] = block(54 + t)
    pairs = [block(62 + n) for n in range(7)]
    pieces = [p[0] for p in pairs] + [p[1] for p in pairs]

    def tap(depth, height, k):
        return (depth * 3 + height) * 3 + k

    for k in range(3):
        for depth in range(3):
            piece = pieces[depth * 3 + k]
            grad_enc[tap(depth, 0, k)] = piece[:, :64]
            grad_enc[tap(depth, 1, k)] = piece[:, 64:]
        grad_enc[tap(0, 2, k)] = pieces[9 + k][:, :64]
        grad_enc[tap(1, 2, k)] = pieces[9 + k][:, 64:]
    grad_enc[tap(2, 2, 0)] = pieces[12][:, :64]
    grad_enc[tap(2, 2, 1)] = pieces[12][:, 64:]
    grad_enc[tap(2, 2, 2)] = pieces[13][:, :64]


def other_core(values):
    return lax.ppermute(values, "gx", [(i, i ^ 1) for i in range(lax.axis_size("gx"))])


def to_owners(part):
    return lax.all_to_all(part.reshape(16, 8, part.shape[1]), "gy", 0, 0, tiled=True)


def over_depths(pos, chunks):
    groups = [[2 * a + b for a in range(8)] for b in range(2)]
    got = lax.all_to_all(chunks, "gx", 0, 0, tiled=True, axis_index_groups=groups)
    (copies,) = call(add_depths, [((8, 8, 1152), BF)], [], pos, got)
    return lax.all_to_all(copies, "gx", 0, 0, tiled=True, axis_index_groups=groups)


def constants():
    w, k = np.arange(64)[:, None], np.arange(32)[None, :]
    mean = np.tile((w // 2 == k).T * 0.125, (1, 4))
    stretch = np.concatenate([w == 2 * k, w == 2 * k + 1], axis=0)
    sort = np.concatenate([(w == 2 * k).T, (w == 2 * k + 1).T], axis=0)
    spread = np.concatenate([(w // 2 == k) * 0.125] * 2, axis=1)
    return [jnp.asarray(v, BF) for v in (mean, stretch, sort, spread)]


def shards(inputs, cotangent, w_enc, w_bot, w_up, w_dec):
    mean, stretch, sort, spread = constants()
    pos = jnp.stack([lax.axis_index("gx"), lax.axis_index("gy")]).astype(jnp.int32)
    own = jnp.concatenate([inputs[:, 0::2], inputs[:, 1::2]], axis=3)
    near = swap(own, own, "gy")
    slabs = call(input_slabs, [((3, 6, 64, 128), BF)] * 2, [], pos, own, *near)
    near += swap(*slabs, "gx")
    paired, encoded, slope, pooled, bot_slope, bottom, *slabs = call(
        encode,
        [
            ((10, 11, 64, 128), BF),
            ((8, 8, 64, 128), BF),
            ((8, 8, 64, 128), BF),
            ((4, 4, 32, 128), BF),
            ((128, 256), F32),
            ((2, 2, 32, 256), BF),
        ]
        + [((384, 128), BF)] * 2,
        [((768, 384), BF)],
        pos, own, *near, cotangent, mean, far=(w_enc, w_bot),
        us=6,
    )
    near = swap(*slabs, "gy")
    slabs = call(bottom_slabs, [((640, 128), BF)] * 2, [], pos, bottom, cotangent, *near)
    near += swap(*slabs, "gx")
    decoded, lifted, dec_grad, skip, sorted_lift, bottom_grad, *slabs = call(
        decode,
        [
            ((4, 4, 64, 128), BF),
            ((6, 6, 64, 128), BF),
            ((4, 4, 64, 128), BF),
            ((4, 4, 64, 128), BF),
            ((128, 1024), BF),
            ((2, 2, 32, 256), BF),
        ]
        + [((512, 128), BF)] * 2,
        [
            ((8, 8, 64, 128), BF),
            ((6, 6, 64, 128), BF),
            ((4, 4, 32, 256), BF),
            ((6, 6, 64, 128), BF),
        ],
        pos, bottom, cotangent, *near, encoded, bot_slope, stretch, sort, far=(w_up, w_dec),
        us=13,
    )
    near = swap(*slabs, "gy")
    keep_enc, send_enc = call(
        encode_weights,
        [((128, 896), BF)] * 2,
        [((6, 6, 32, 256), BF), ((384, 4096), BF)],
        pos, bottom_grad, skip, slope, paired, spread,
        far=(w_bot,),
        us=6,
    )
    keep_bot, send_bot = call(
        bottom_weights,
        [((128, 4480), BF)] * 2,
        [],
        pos, sorted_lift, bottom, pooled, bottom_grad,
        us=2,
    )
    slabs = call(
        grad_slabs, [((1152, 128), BF)] * 2, [], pos, bottom_grad, skip, *near,
        behind=(keep_enc, keep_bot),
    )
    keep, send = call(
        decode_weights,
        [((128, 3456), BF)] * 2,
        [],
        pos, lifted, encoded, dec_grad,
        behind=slabs[:1],
        us=3,
    )
    (part,) = call(
        add_cores, [((128, 8832), BF)], [],
        pos, keep, other_core(send), keep_bot, other_core(send_bot), keep_enc, other_core(send_enc),
    )
    near += swap(*slabs, "gx")
    pool_grad, input_grad, done = call(
        encode_back,
        [((2, 2, 32, 128), F32), ((4, 4, 64, 64), BF), ((8, 128), F32)],
        [((6, 6, 64, 128), BF), ((6, 6, 32, 256), BF), ((6, 6, 64, 128), BF)],
        pos, bottom_grad, skip, *near, slope, spread,
        far=(w_bot, w_enc), behind=(part,),
        us=5,
    )
    (chunks,) = call(
        add_heights, [((8, 8, 1152), BF)], [], pos, to_owners(part), behind=(done,), us=2
    )
    mine = over_depths(pos, chunks)
    other = other_core(mine)
    grads = call(
        finish,
        [((27, 8, 64), F32), ((27, 16, 128), F32), ((8, 8, 256), F32), ((27, 8, 256), F32)],
        [],
        pos, mine, other,
    )
    grad_enc, grad_bot, grad_up, grad_dec = (
        jnp.transpose(grad, (0, 2, 1)).reshape(*shape, grad.shape[2], grad.shape[1])
        for grad, shape in zip(grads, ((3, 3, 3), (3, 3, 3), (2, 2, 2), (3, 3, 3)))
    )
    return (decoded, input_grad, grad_enc, grad_bot, grad_up, grad_dec, pool_grad)


def solution(mesh):
    in_specs = (P("gx", "gy", None, None), P("gx", "gy", None, None), P(), P(), P(), P())
    out_specs = (
        P("gx", "gy", None, None),
        P("gx", "gy", None, None),
        P(None, None, None, None, "gy"),
        P(None, None, None, None, "gy"),
        P(None, None, None, None, "gy"),
        P(None, None, None, None, "gy"),
        P("gx", "gy", None, None),
    )
    return jax.shard_map(shards, mesh=mesh, in_specs=in_specs, out_specs=out_specs, check_vma=False)
```

```python
import jax
import jax.numpy as jnp
import numpy as np
from jax import lax
from jax.experimental import pallas as pl
from jax.experimental.pallas import tpu as pltpu
from jax.sharding import PartitionSpec as P

BF = jnp.bfloat16
F32 = jnp.float32
VMEM_LIMIT = 24 * 1024 * 1024


def dot(a, b):
    return jnp.dot(a, b, preferred_element_type=F32)


def call(kernel, outs, scratch, pos, *args, far=(), behind=(), us=1):
    held = [pl.BlockSpec(memory_space=pltpu.VMEM)] * len(args)
    waits = [pl.BlockSpec(memory_space=pltpu.HBM)] * len(far)
    waits += [pl.BlockSpec(memory_space=pl.ANY)] * len(behind)
    count = len(args)

    def run(place, *refs):
        own = refs[count + len(waits) :]
        copies = []
        for n in range(len(far)):
            room = own[len(own) - 1 - len(far) + n]
            copies.append(pltpu.make_async_copy(refs[count + n], room, own[-1].at[n]))
            copies[-1].start()

        def fetched(n):
            copies[n].wait()
            return own[len(own) - 1 - len(far) + n]

        extra = (fetched,) if far else ()
        kept = own[: len(own) - 1 - len(far)] if far else own
        return kernel(place, *extra, *refs[:count], *kept)

    rooms = [pltpu.VMEM(shape, dtype) for shape, dtype in scratch]
    if far:
        rooms += [pltpu.VMEM(a.shape, a.dtype) for a in far]
        rooms.append(pltpu.SemaphoreType.DMA((len(far),)))
    return pl.pallas_call(
        run,
        out_shape=[jax.ShapeDtypeStruct(shape, dtype) for shape, dtype in outs],
        in_specs=[pl.BlockSpec(memory_space=pltpu.SMEM)] + held + waits,
        out_specs=[pl.BlockSpec(memory_space=pltpu.VMEM)] * len(outs),
        scratch_shapes=rooms,
        compiler_params=pltpu.CompilerParams(vmem_limit_bytes=VMEM_LIMIT),
        cost_estimate=pl.CostEstimate(
            flops=us * 10**9, transcendentals=0, bytes_accessed=us * 3 * 10**6
        ),
        name=kernel.__name__,
    )(pos, *args, *far, *behind)


def stacked(parts):
    return jnp.concatenate(parts, axis=0)


def sides(pos, axis, inner, outer):
    even = pos[axis] % 2 == 0
    within = (pos[axis] > 0) & (pos[axis] < 15)

    def far_side(at):
        value = outer[at]
        return jnp.where(within, value, jnp.zeros_like(value))

    def low(*at):
        return jnp.where(even, far_side(at), inner[at])

    def high(*at):
        return jnp.where(even, inner[at], far_side(at))

    return low, high


def give(pos, axis, inner, outer, low, high, at=slice(None)):
    even = pos[axis] % 2 == 0
    inner[at] = jnp.where(even, high, low)
    outer[at] = jnp.where(even, low, high)


def dot_nt(a, b):
    return lax.dot_general(a, b, (((1,), (1,)), ((), ())), preferred_element_type=F32)


def before(values, width):
    place = lax.broadcasted_iota(jnp.int32, values.shape, 0) & (width - 1)
    return jnp.where(place == 0, 0.0, pltpu.roll(values, 1, 0))


def after(values, width):
    place = lax.broadcasted_iota(jnp.int32, values.shape, 0) & (width - 1)
    return jnp.where(place == width - 1, 0.0, pltpu.roll(values, values.shape[0] - 1, 0))


def gathered(wide, width, chans):
    taps = [wide[:, k * chans : (k + 1) * chans] for k in range(3)]
    return before(taps[0], width) + taps[1] + after(taps[2], width)


def scattered(wide, width, chans):
    taps = [wide[:, k * chans : (k + 1) * chans] for k in range(3)]
    return after(taps[0], width) + taps[1] + before(taps[2], width)


def tripled(values, width):
    wide = jnp.concatenate([after(values, width), values, before(values, width)], axis=1)
    return jnp.transpose(wide).astype(BF)


def sigmoid(values):
    return 0.5 * jnp.tanh(0.5 * values) + 0.5


def slope_of(values, sigma):
    return sigma * (1.0 + values * (1.0 - sigma))


def lanes(parts):
    return jnp.concatenate(parts, axis=1)


def transposed(cells, weight):
    depths, rows, width, chans = cells.shape
    depths, rows = depths - 2, rows - 2
    taps = [(depth, height) for depth in range(3) for height in range(3)]
    window = lanes(
        [
            cells[2 - d : 2 - d + depths, 2 - h : 2 - h + rows].reshape(depths * rows * width, chans)
            for d, h in taps
        ]
    )
    inner = weight.shape[3]
    turned = lanes([weight[d, h].reshape(3 * inner, chans) for d, h in taps])
    return scattered(dot_nt(window, turned), width, inner)


def input_slabs(pos, own, g_in, g_out, s_in, s_out):
    low, high = sides(pos, 1, g_in, g_out)
    edges = []
    for d in (0, 1):
        cut = slice(d, d + 3)
        edges.append(jnp.concatenate([low(cut), own[cut], high(cut)], axis=1))
    give(pos, 0, s_in, s_out, edges[0], edges[1])


def fill_input(pos, store, own, g_in, g_out, x_in, x_out):
    low, high = sides(pos, 1, g_in, g_out)
    under, over = sides(pos, 0, x_in, x_out)
    lane = lax.broadcasted_iota(jnp.int32, (320, 128), 1)
    for d in range(10):
        if d < 3:
            line = under(d)
        elif d < 7:
            line = jnp.concatenate([low(d - 3), own[d - 3], high(d - 3)], axis=0)
        else:
            line = over(d - 7)
        wide = pltpu.roll(line.reshape(384, 128).astype(F32), 64, 1)
        odd = jnp.where(lane < 64, wide[:320], wide[64:]).astype(BF).reshape(5, 64, 128)
        for m in range(6):
            if m < 5:
                store[d, 2 * m + 1] = odd[m]
            store[d, 2 * m] = line[m]


def encode(
    pos, fetched, own, g_in, g_out, x_in, x_out, cotangent, mean,
    paired, encoded, slope, pooled, bot_slope, bottom, s_in, s_out,
    weight,
):
    fill_input(pos, paired, own, g_in, g_out, x_in, x_out)
    high = pos[0] * 4 - 2
    tall = pos[1] * 4 - 2
    w_enc = fetched(0)
    for depth in range(3):
        for height in range(3):
            at = depth * 256 + height * 64
            weight[at : at + 64, :] = lanes([w_enc[depth, height, k] for k in range(3)])
        weight[depth * 256 + 192 : depth * 256 + 256, :] = jnp.zeros((64, 384), BF)

    place = lax.broadcasted_iota(jnp.int32, (512, 128), 0) // 64 + tall
    across = (place >= 0) & (place < 64)
    for d in range(8):
        window = lanes(
            [
                paired[d + depth, 2 * half + 1 : 2 * half + 9].reshape(512, 128)
                for depth in range(3)
                for half in range(2)
            ]
        )
        pre = gathered(dot(window, weight[...]), 64, 128)
        sigma = sigmoid(pre)
        inside = across & (d + high >= 0) & (d + high < 64)
        encoded[d] = jnp.where(inside, pre * sigma, 0.0).astype(BF).reshape(8, 64, 128)
        slope[d] = jnp.where(inside, slope_of(pre, sigma), 0.0).astype(BF).reshape(8, 64, 128)
    for i in range(4):
        line = lanes(
            [encoded[2 * i : 2 * i + 2, 2 * j : 2 * j + 2].reshape(256, 128) for j in range(4)]
        )
        value = dot(mean[...], line).astype(BF)
        for j in range(4):
            pooled[i, j] = value[:, 128 * j : 128 * j + 128]
    window = lanes(
        [
            pooled[depth : depth + 2, height : height + 2].reshape(128, 128)
            for depth in range(3)
            for height in range(3)
        ]
    )
    w_bot = fetched(1)
    rows = jnp.concatenate(
        [
            lanes([w_bot[depth, height, k] for k in range(3)])
            for depth in range(3)
            for height in range(3)
        ],
        axis=0,
    )
    pre = gathered(dot(window, rows), 32, 256)
    sigma = sigmoid(pre)
    value = (pre * sigma).astype(BF).reshape(2, 2, 32, 256)
    bottom[...] = value
    bot_slope[...] = slope_of(pre, sigma)
    edges = []
    for h, at in ((0, 0), (1, 3)):
        row = value[:, h].reshape(64, 256)
        edges.append(stacked([cotangent[:, at].reshape(256, 128), row[:, :128], row[:, 128:]]))
    give(pos, 1, s_in, s_out, edges[0], edges[1])


def bottom_slabs(pos, bottom, cotangent, g_in, g_out, s_in, s_out):
    low, high = sides(pos, 1, g_in, g_out)
    edges = []
    for d, b in ((0, 0), (3, 1)):
        cot = slice(64 * d, 64 * d + 64)
        parts = [low(cot), cotangent[d].reshape(256, 128), high(cot)]
        for half in range(2):
            cut = slice(256 + 64 * half + 32 * b, 256 + 64 * half + 32 * b + 32)
            lane = slice(128 * half, 128 * half + 128)
            parts += [low(cut), bottom[b, 0, :, lane], bottom[b, 1, :, lane], high(cut)]
        edges.append(stacked(parts))
    give(pos, 0, s_in, s_out, edges[0], edges[1])


def fill_bottom(pos, wide_bottom, wide_cot, bottom, cotangent, g_in, g_out, x_in, x_out):
    low, high = sides(pos, 1, g_in, g_out)
    for d in range(4):
        cut = slice(64 * d, 64 * d + 64)
        wide_cot[d + 1, 0] = low(cut)
        wide_cot[d + 1, 1:5] = cotangent[d]
        wide_cot[d + 1, 5] = high(cut)
    for b in range(2):
        wide_bottom[b + 1, 1:3] = bottom[b]
        for half in range(2):
            cut = slice(256 + 64 * half + 32 * b, 256 + 64 * half + 32 * b + 32)
            lane = slice(128 * half, 128 * half + 128)
            wide_bottom[b + 1, 0, :, lane] = low(cut)
            wide_bottom[b + 1, 3, :, lane] = high(cut)
    for side, d, b in zip(sides(pos, 0, x_in, x_out), (0, 5), (0, 3)):
        wide_cot[d] = side(slice(0, 384)).reshape(6, 64, 128)
        for half in range(2):
            cut = slice(384 + 128 * half, 512 + 128 * half)
            lane = slice(128 * half, 128 * half + 128)
            wide_bottom[b, :, :, lane] = side(cut).reshape(4, 32, 128)


def decode(
    pos, fetched, own_bottom, own_cot, g_in, g_out, x_in, x_out,
    encoded, bot_slope, stretch, sort,
    decoded, lifted, dec_grad, skip, sorted_lift, bottom_grad, s_in, s_out,
    lift_all, gstore, bottom, cotangent,
):
    fill_bottom(pos, bottom, cotangent, own_bottom, own_cot, g_in, g_out, x_in, x_out)
    w_up = fetched(0)
    wide = []
    for i in range(4):
        spread = dot(stretch[...], lanes([bottom[i, j] for j in range(4)])).astype(BF)
        for j in range(4):
            cut = slice(256 * j, 256 * j + 256)
            wide.append(lanes([spread[:64, cut], spread[64:, cut]]))
    up = lanes([w_up[a, b].reshape(512, 128) for a in range(2) for b in range(2)])
    value = dot(stacked(wide), up).astype(BF).reshape(4, 4, 64, 512)
    for a in range(2):
        for b in range(2):
            cut = slice(128 * (2 * a + b), 128 * (2 * a + b) + 128)
            for i in range(4):
                for j in range(4):
                    lift_all[2 * i + a, 2 * j + b] = value[i, j, :, cut]
    lifted[...] = lift_all[1:7, 1:7]

    w_dec = fetched(1)
    for d in range(0, 6, 2):
        wide = None
        for depth in range(3):
            window = lanes(
                [
                    cells[d + depth : d + depth + 2, height : height + 6].reshape(768, 128)
                    for height in range(3)
                    for cells in (lift_all, encoded)
                ]
            )
            rows = stacked([lanes([w_dec[depth, height, k] for k in range(3)]) for height in range(3)])
            part = dot(window, rows)
            wide = part if wide is None else wide + part
        pre = gathered(wide, 64, 128)
        sigma = sigmoid(pre)
        cot = cotangent[d : d + 2].reshape(768, 128).astype(F32)
        grad = (cot * slope_of(pre, sigma)).astype(BF).reshape(2, 6, 64, 128)
        value = (pre * sigma).astype(BF).reshape(2, 6, 64, 128)
        gstore[d : d + 2] = grad
        for n in range(2):
            if 1 <= d + n <= 4:
                decoded[d + n - 1] = value[n, 1:5]
                dec_grad[d + n - 1] = grad[n, 1:5]
    pieces = [[], []]
    back_all = transposed(gstore, w_dec)
    for d in range(4):
        back = back_all[256 * d : 256 * d + 256]
        skip[d] = back[:, 128:].astype(BF).reshape(4, 64, 128)
        lift = back[:, :128].astype(BF).reshape(4, 64, 128)
        flat = lanes([lift[h] for h in range(4)])
        pieces[d // 2].append(dot(sort[...], flat).astype(BF))
    rows = []
    for i in range(2):
        for j in range(2):
            rows.append(
                lanes(
                    [
                        pieces[i][a][32 * c : 32 * c + 32, 128 * (2 * j + b) : 128 * (2 * j + b) + 128]
                        for a in range(2)
                        for b in range(2)
                        for c in range(2)
                    ]
                )
            )
    rows = jnp.concatenate(rows, axis=0)
    sorted_lift[...] = rows
    up = lanes([w_up[a, b, c] for a in range(2) for b in range(2) for c in range(2)])
    back = dot_nt(rows, up)
    grad = (back * bot_slope[...]).astype(BF)
    bottom_grad[...] = grad.reshape(2, 2, 32, 256)
    give(pos, 1, s_in, s_out, skip[:, 0].reshape(256, 128), skip[:, 3].reshape(256, 128), slice(0, 256))
    for half in range(2):
        cut = slice(256 + 128 * half, 384 + 128 * half)
        s_in[cut] = grad[:, 128 * half : 128 * half + 128]
        s_out[cut] = grad[:, 128 * half : 128 * half + 128]


def grad_slabs(pos, grad, skip, g_in, g_out, s_in, s_out):
    low, high = sides(pos, 1, g_in, g_out)
    edges = []
    for d in (0, 3):
        cut = slice(64 * d, 64 * d + 64)
        edges.append(stacked([low(cut), skip[d].reshape(256, 128), high(cut)]))
    give(pos, 0, s_in, s_out, edges[0], edges[1], slice(0, 384))
    for half in range(2):
        lane = slice(128 * half, 128 * half + 128)
        for d in range(2):
            cut = slice(256 + 128 * half + 64 * d, 256 + 128 * half + 64 * d + 64)
            line = stacked([low(cut), grad[d, 0, :, lane], grad[d, 1, :, lane], high(cut)])
            at = 384 + 384 * half + 192 * d
            s_in[at : at + 192] = line
            s_out[at : at + 192] = line


def fill_grad(pos, wide_grad, wide_skip, grad, skip, g_in, g_out, x_in, x_out):
    low, high = sides(pos, 1, g_in, g_out)
    for d in range(4):
        cut = slice(64 * d, 64 * d + 64)
        wide_skip[d + 1, 0] = low(cut)
        wide_skip[d + 1, 1:5] = skip[d]
        wide_skip[d + 1, 5] = high(cut)
    for b in range(2):
        wide_grad[b + 2, 2:4] = grad[b]
        for half in range(2):
            cut = slice(256 + 128 * half + 64 * b, 256 + 128 * half + 64 * b + 64)
            lane = slice(128 * half, 128 * half + 128)
            wide_grad[b + 2, 0:2, :, lane] = low(cut).reshape(2, 32, 128)
            wide_grad[b + 2, 4:6, :, lane] = high(cut).reshape(2, 32, 128)
    for side, d, b in zip(sides(pos, 0, x_in, x_out), (0, 5), (0, 4)):
        wide_skip[d] = side(slice(0, 384)).reshape(6, 64, 128)
        for half in range(2):
            cut = slice(384 + 384 * half, 768 + 384 * half)
            lane = slice(128 * half, 128 * half + 128)
            wide_grad[b : b + 2, :, :, lane] = side(cut).reshape(2, 6, 32, 128)


def put(first, keep, send, at, one, two):
    keep[:, at : at + 128] = jnp.where(first, one, two).astype(BF)
    send[:, at : at + 128] = jnp.where(first, two, one).astype(BF)


def decode_weights(pos, lifted, encoded, dec_grad, keep, send):
    first = pos[0] % 2 == 0
    grad = tripled(dec_grad[...].reshape(1024, 128).astype(F32), 64)
    for depth in range(3):
        for height in range(3):
            window = lanes(
                [
                    lifted[depth : depth + 4, height : height + 4].reshape(1024, 128),
                    encoded[depth + 1 : depth + 5, height + 1 : height + 5].reshape(1024, 128),
                ]
            )
            part = dot(grad, window)
            for k in range(3):
                rows = part[k * 128 : k * 128 + 128]
                at = ((depth * 3 + height) * 3 + k) * 128
                put(first, keep, send, at, rows[:, :128], rows[:, 128:])


def spread_row(row, spread):
    cells = row.reshape(4, 32, 128)
    flat = lanes([cells[h] for h in range(4)])
    upper = flat.astype(BF)
    lower = (flat - upper.astype(F32)).astype(BF)
    return dot(spread[...], jnp.concatenate([upper, lower], axis=0))


def bottom_weights(
    pos, sorted_lift, bottom, pooled, bottom_grad,
    keep, send,
):
    first = pos[0] % 2 == 0
    grad = tripled(bottom_grad[...].reshape(128, 256).astype(F32), 32)
    for depth in range(3):
        window = lanes(
            [
                pooled[depth : depth + 2, height : height + 2].reshape(128, 128)
                for height in range(3)
            ]
        )
        part = dot(grad, window)
        for k in range(3):
            rows = part[k * 256 : k * 256 + 256].reshape(16, 2, 8, 384)
            one, two = rows[:, 0].reshape(128, 384), rows[:, 1].reshape(128, 384)
            for height in range(3):
                at = ((depth * 3 + height) * 3 + k) * 128
                cut = slice(height * 128, height * 128 + 128)
                put(first, keep, send, at, one[:, cut], two[:, cut])
    part = dot(
        jnp.transpose(sorted_lift[...].astype(F32)).astype(BF), bottom[...].reshape(128, 256)
    )
    for t in range(8):
        rows = part[t * 128 : t * 128 + 128]
        put(first, keep, send, 3456 + t * 128, rows[:, :128], rows[:, 128:])


def encode_weights(
    pos, fetched, bottom_grad, skip, slope, paired, spread,
    keep, send,
    bstore, turned,
):
    first = pos[0] % 2 == 0
    bstore[...] = jnp.zeros((6, 6, 32, 256), BF)
    bstore[2:4, 2:4] = bottom_grad[...]
    w_bot = fetched(0)
    back = transposed(bstore, w_bot)
    for d in range(4):
        wide = spread_row(back[128 * d : 128 * d + 128], spread)
        for f in (2 * d, 2 * d + 1):
            cells = []
            for h in range(8):
                value = wide[:, h // 2 * 128 : h // 2 * 128 + 128]
                if 2 <= f < 6 and 2 <= h < 6:
                    value = value + skip[f - 2, h - 2].astype(F32)
                cells.append(value * slope[f, h].astype(F32))
            row = jnp.concatenate(cells, axis=0).astype(BF).astype(F32)
            turned[:, f * 512 : f * 512 + 512] = tripled(row, 64)

    lane = lax.broadcasted_iota(jnp.int32, (4096, 128), 1)

    def window(depth, height):
        return paired[depth : depth + 8, height + 1 : height + 9].reshape(4096, 128)

    blocks = [window(0, 0), window(1, 0), window(2, 0)]
    blocks.append(jnp.where(lane < 64, window(0, 2), window(1, 1)))
    blocks.append(jnp.where(lane < 64, window(2, 2), window(2, 1)))
    parts = []
    for n in (0, 2, 4):
        part = dot(turned[...], lanes(blocks[n : n + 2]))
        parts += [part[:, m * 128 : m * 128 + 128] for m in range(part.shape[1] // 128)]
    cut = [[part[k * 128 : k * 128 + 128] for k in range(3)] for part in parts]
    small = lax.broadcasted_iota(jnp.int32, (128, 128), 1)
    final = cut[0] + cut[1] + cut[2] + cut[3]
    final += [jnp.where(small < 64, cut[4][0], cut[4][1]), cut[4][2]]
    for n in range(7):
        put(first, keep, send, n * 128, final[n], final[n + 7])


def encode_back(
    pos, fetched, own_grad, own_skip, g_in, g_out, x_in, x_out, slope, spread,
    pool_grad, input_grad, done,
    gstore, grad, skip,
):
    done[...] = jnp.zeros((8, 128), F32)
    fill_grad(pos, grad, skip, own_grad, own_skip, g_in, g_out, x_in, x_out)
    w_bot = fetched(0)
    back = transposed(grad, w_bot)
    for d in range(4):
        row = back[128 * d : 128 * d + 128]
        if 1 <= d <= 2:
            pool_grad[d - 1] = row.reshape(4, 32, 128)[1:3]
        wide = spread_row(row, spread)
        for f in range(6):
            if (f + 1) // 2 != d:
                continue
            for h in range(6):
                at = (h + 1) // 2 * 128
                value = skip[f, h].astype(F32) + wide[:, at : at + 128]
                gstore[f, h] = (value * slope[f + 1, h + 1].astype(F32)).astype(BF)
    w_enc = fetched(1)
    input_grad[...] = transposed(gstore, w_enc).astype(BF).reshape(4, 4, 64, 64)


def swap(inner, outer, axis):
    count = lax.axis_size(axis)
    pairs = [(i, (i + 1) % count) for i in range(1, count, 2)]
    pairs += [(j, i) for i, j in pairs]
    got = lax.ppermute(inner, axis, [(i, i ^ 1) for i in range(count)])
    return got, lax.ppermute(outer, axis, pairs)


def add_cores(pos, *refs):
    total = refs[-1]
    at = 0
    for keep, got in zip(refs[0:-1:2], refs[1:-1:2]):
        width = keep.shape[1]
        total[:, at : at + width] = (keep[...].astype(F32) + got[...].astype(F32)).astype(BF)
        at += width


def add_heights(pos, parts, chunks):
    filled = parts.shape[2] // 128
    for n in range(9 * chunks.shape[0]):
        if n < filled:
            cut = slice(128 * n, 128 * n + 128)
            total = parts[0, :, cut].astype(F32)
            for j in range(1, 16):
                total = total + parts[j, :, cut].astype(F32)
        else:
            total = jnp.zeros((8, 128), F32)
        at = 128 * (n % 9)
        chunks[n // 9, :, at : at + 128] = total.astype(BF)


def add_depths(pos, parts, copies):
    total = parts[0].astype(F32)
    for j in range(1, 8):
        total = total + parts[j].astype(F32)
    total = total.astype(BF)
    for j in range(8):
        copies[j] = total


def finish(pos, mine, other, grad_enc, grad_bot, grad_up, grad_dec):
    first = pos[0] % 2 == 0

    def block(n):
        cut = slice(128 * (n % 9), 128 * (n % 9) + 128)
        left, right = mine[n // 9, :, cut].astype(F32), other[n // 9, :, cut].astype(F32)
        return jnp.where(first, left, right), jnp.where(first, right, left)

    for t in range(27):
        grad_dec[t, :, :128], grad_dec[t, :, 128:] = block(t)
        grad_bot[t, :8], grad_bot[t, 8:] = block(27 + t)
    for t in range(8):
        grad_up[t, :, :128], grad_up[t, :, 128:] = block(54 + t)
    pairs = [block(62 + n) for n in range(7)]
    pieces = [p[0] for p in pairs] + [p[1] for p in pairs]

    def tap(depth, height, k):
        return (depth * 3 + height) * 3 + k

    for k in range(3):
        for depth in range(3):
            piece = pieces[depth * 3 + k]
            grad_enc[tap(depth, 0, k)] = piece[:, :64]
            grad_enc[tap(depth, 1, k)] = piece[:, 64:]
        grad_enc[tap(0, 2, k)] = pieces[9 + k][:, :64]
        grad_enc[tap(1, 2, k)] = pieces[9 + k][:, 64:]
    grad_enc[tap(2, 2, 0)] = pieces[12][:, :64]
    grad_enc[tap(2, 2, 1)] = pieces[12][:, 64:]
    grad_enc[tap(2, 2, 2)] = pieces[13][:, :64]


def other_core(values):
    return lax.ppermute(values, "gx", [(i, i ^ 1) for i in range(lax.axis_size("gx"))])


def to_owners(part):
    return lax.all_to_all(part.reshape(16, 8, part.shape[1]), "gy", 0, 0, tiled=True)


def over_depths(pos, chunks):
    groups = [[2 * a + b for a in range(8)] for b in range(2)]
    got = lax.all_to_all(chunks, "gx", 0, 0, tiled=True, axis_index_groups=groups)
    (copies,) = call(add_depths, [((8, 8, 1152), BF)], [], pos, got)
    return lax.all_to_all(copies, "gx", 0, 0, tiled=True, axis_index_groups=groups)


def constants():
    w, k = np.arange(64)[:, None], np.arange(32)[None, :]
    mean = np.tile((w // 2 == k).T * 0.125, (1, 4))
    stretch = np.concatenate([w == 2 * k, w == 2 * k + 1], axis=0)
    sort = np.concatenate([(w == 2 * k).T, (w == 2 * k + 1).T], axis=0)
    spread = np.concatenate([(w // 2 == k) * 0.125] * 2, axis=1)
    return [jnp.asarray(v, BF) for v in (mean, stretch, sort, spread)]


def shards(inputs, cotangent, w_enc, w_bot, w_up, w_dec):
    mean, stretch, sort, spread = constants()
    pos = jnp.stack([lax.axis_index("gx"), lax.axis_index("gy")]).astype(jnp.int32)
    own = jnp.concatenate([inputs[:, 0::2], inputs[:, 1::2]], axis=3)
    near = swap(own, own, "gy")
    slabs = call(input_slabs, [((3, 6, 64, 128), BF)] * 2, [], pos, own, *near)
    near += swap(*slabs, "gx")
    paired, encoded, slope, pooled, bot_slope, bottom, *slabs = call(
        encode,
        [
            ((10, 11, 64, 128), BF),
            ((8, 8, 64, 128), BF),
            ((8, 8, 64, 128), BF),
            ((4, 4, 32, 128), BF),
            ((128, 256), F32),
            ((2, 2, 32, 256), BF),
        ]
        + [((384, 128), BF)] * 2,
        [((768, 384), BF)],
        pos, own, *near, cotangent, mean, far=(w_enc, w_bot),
        us=6,
    )
    near = swap(*slabs, "gy")
    slabs = call(bottom_slabs, [((640, 128), BF)] * 2, [], pos, bottom, cotangent, *near)
    near += swap(*slabs, "gx")
    decoded, lifted, dec_grad, skip, sorted_lift, bottom_grad, *slabs = call(
        decode,
        [
            ((4, 4, 64, 128), BF),
            ((6, 6, 64, 128), BF),
            ((4, 4, 64, 128), BF),
            ((4, 4, 64, 128), BF),
            ((128, 1024), BF),
            ((2, 2, 32, 256), BF),
        ]
        + [((512, 128), BF)] * 2,
        [
            ((8, 8, 64, 128), BF),
            ((6, 6, 64, 128), BF),
            ((4, 4, 32, 256), BF),
            ((6, 6, 64, 128), BF),
        ],
        pos, bottom, cotangent, *near, encoded, bot_slope, stretch, sort, far=(w_up, w_dec),
        us=13,
    )
    near = swap(*slabs, "gy")
    keep_enc, send_enc = call(
        encode_weights,
        [((128, 896), BF)] * 2,
        [((6, 6, 32, 256), BF), ((384, 4096), BF)],
        pos, bottom_grad, skip, slope, paired, spread,
        far=(w_bot,),
        us=6,
    )
    keep_bot, send_bot = call(
        bottom_weights,
        [((128, 4480), BF)] * 2,
        [],
        pos, sorted_lift, bottom, pooled, bottom_grad,
        us=2,
    )
    slabs = call(
        grad_slabs, [((1152, 128), BF)] * 2, [], pos, bottom_grad, skip, *near,
        behind=(keep_enc, keep_bot),
    )
    keep, send = call(
        decode_weights,
        [((128, 3456), BF)] * 2,
        [],
        pos, lifted, encoded, dec_grad,
        behind=slabs[:1],
        us=3,
    )
    (part,) = call(
        add_cores, [((128, 8832), BF)], [],
        pos, keep, other_core(send), keep_bot, other_core(send_bot), keep_enc, other_core(send_enc),
    )
    near += swap(*slabs, "gx")
    pool_grad, input_grad, done = call(
        encode_back,
        [((2, 2, 32, 128), F32), ((4, 4, 64, 64), BF), ((8, 128), F32)],
        [((6, 6, 64, 128), BF), ((6, 6, 32, 256), BF), ((6, 6, 64, 128), BF)],
        pos, bottom_grad, skip, *near, slope, spread,
        far=(w_bot, w_enc), behind=(part,),
        us=5,
    )
    (chunks,) = call(
        add_heights, [((8, 8, 1152), BF)], [], pos, to_owners(part), behind=(done,), us=2
    )
    mine = over_depths(pos, chunks)
    other = other_core(mine)
    grads = call(
        finish,
        [((27, 8, 64), F32), ((27, 16, 128), F32), ((8, 8, 256), F32), ((27, 8, 256), F32)],
        [],
        pos, mine, other,
    )
    grad_enc, grad_bot, grad_up, grad_dec = (
        jnp.transpose(grad, (0, 2, 1)).reshape(*shape, grad.shape[2], grad.shape[1])
        for grad, shape in zip(grads, ((3, 3, 3), (3, 3, 3), (2, 2, 2), (3, 3, 3)))
    )
    return (decoded, input_grad, grad_enc, grad_bot, grad_up, grad_dec, pool_grad)


def solution(mesh):
    in_specs = (P("gx", "gy", None, None), P("gx", "gy", None, None), P(), P(), P(), P())
    out_specs = (
        P("gx", "gy", None, None),
        P("gx", "gy", None, None),
        P(None, None, None, None, "gy"),
        P(None, None, None, None, "gy"),
        P(None, None, None, None, "gy"),
        P(None, None, None, None, "gy"),
        P("gx", "gy", None, None),
    )
    return jax.shard_map(shards, mesh=mesh, in_specs=in_specs, out_specs=out_specs, check_vma=False)
```

```python
import jax
import jax.numpy as jnp
import numpy as np
from jax import lax
from jax.experimental import pallas as pl
from jax.experimental.pallas import tpu as pltpu
from jax.sharding import PartitionSpec as P

BF = jnp.bfloat16
F32 = jnp.float32
VMEM_LIMIT = 24 * 1024 * 1024


def dot(a, b):
    return jnp.dot(a, b, preferred_element_type=F32)


def call(kernel, outs, scratch, pos, *args, far=(), behind=(), through=(), us=1):
    held = [pl.BlockSpec(memory_space=pltpu.VMEM)] * len(args)
    waits = [pl.BlockSpec(memory_space=pltpu.HBM)] * len(far)
    waits += [pl.BlockSpec(memory_space=pl.ANY)] * (len(behind) + len(through))
    count = len(args)

    def run(place, *refs):
        own = refs[count + len(waits) :]
        own = own[: len(outs)] + own[len(outs) + len(through) :]
        copies = []
        for n in range(len(far)):
            room = own[len(own) - 1 - len(far) + n]
            copies.append(pltpu.make_async_copy(refs[count + n], room, own[-1].at[n]))
            copies[-1].start()

        def fetched(n):
            copies[n].wait()
            return own[len(own) - 1 - len(far) + n]

        extra = (fetched,) if far else ()
        kept = own[: len(own) - 1 - len(far)] if far else own
        return kernel(place, *extra, *refs[:count], *kept)

    rooms = [pltpu.VMEM(shape, dtype) for shape, dtype in scratch]
    if far:
        rooms += [pltpu.VMEM(a.shape, a.dtype) for a in far]
        rooms.append(pltpu.SemaphoreType.DMA((len(far),)))
    return pl.pallas_call(
        run,
        out_shape=[jax.ShapeDtypeStruct(shape, dtype) for shape, dtype in outs]
        + [jax.ShapeDtypeStruct(a.shape, a.dtype) for a in through],
        in_specs=[pl.BlockSpec(memory_space=pltpu.SMEM)] + held + waits,
        out_specs=[pl.BlockSpec(memory_space=pltpu.VMEM)] * len(outs)
        + [pl.BlockSpec(memory_space=pl.ANY)] * len(through),
        input_output_aliases={
            1 + count + len(far) + len(behind) + n: len(outs) + n for n in range(len(through))
        },
        scratch_shapes=rooms,
        compiler_params=pltpu.CompilerParams(vmem_limit_bytes=VMEM_LIMIT),
        cost_estimate=pl.CostEstimate(
            flops=us * 10**9, transcendentals=0, bytes_accessed=us * 3 * 10**6
        ),
        name=kernel.__name__,
    )(pos, *args, *far, *behind, *through)


def stacked(parts):
    return jnp.concatenate(parts, axis=0)


def sides(pos, axis, inner, outer):
    even = pos[axis] % 2 == 0
    within = (pos[axis] > 0) & (pos[axis] < 15)

    def far_side(at):
        value = outer[at]
        return jnp.where(within, value, jnp.zeros_like(value))

    def low(*at):
        return jnp.where(even, far_side(at), inner[at])

    def high(*at):
        return jnp.where(even, inner[at], far_side(at))

    return low, high


def give(pos, axis, inner, outer, low, high, at=slice(None)):
    even = pos[axis] % 2 == 0
    inner[at] = jnp.where(even, high, low)
    outer[at] = jnp.where(even, low, high)


def dot_nt(a, b):
    return lax.dot_general(a, b, (((1,), (1,)), ((), ())), preferred_element_type=F32)


def before(values, width):
    place = lax.broadcasted_iota(jnp.int32, values.shape, 0) & (width - 1)
    return jnp.where(place == 0, 0.0, pltpu.roll(values, 1, 0))


def after(values, width):
    place = lax.broadcasted_iota(jnp.int32, values.shape, 0) & (width - 1)
    return jnp.where(place == width - 1, 0.0, pltpu.roll(values, values.shape[0] - 1, 0))


def gathered(wide, width, chans):
    taps = [wide[:, k * chans : (k + 1) * chans] for k in range(3)]
    return before(taps[0], width) + taps[1] + after(taps[2], width)


def scattered(wide, width, chans):
    taps = [wide[:, k * chans : (k + 1) * chans] for k in range(3)]
    return after(taps[0], width) + taps[1] + before(taps[2], width)


def tripled(values, width):
    wide = jnp.concatenate([after(values, width), values, before(values, width)], axis=1)
    return jnp.transpose(wide).astype(BF)


def sigmoid(values):
    return 0.5 * jnp.tanh(0.5 * values) + 0.5


def slope_of(values, sigma):
    return sigma * (1.0 + values * (1.0 - sigma))


def lanes(parts):
    return jnp.concatenate(parts, axis=1)


def transposed(cells, weight):
    depths, rows, width, chans = cells.shape
    depths, rows = depths - 2, rows - 2
    taps = [(depth, height) for depth in range(3) for height in range(3)]
    window = lanes(
        [
            cells[2 - d : 2 - d + depths, 2 - h : 2 - h + rows].reshape(depths * rows * width, chans)
            for d, h in taps
        ]
    )
    inner = weight.shape[3]
    turned = lanes([weight[d, h].reshape(3 * inner, chans) for d, h in taps])
    return scattered(dot_nt(window, turned), width, inner)


def input_slabs(pos, own, g_in, g_out, s_in, s_out):
    low, high = sides(pos, 1, g_in, g_out)
    edges = []
    for d in (0, 1):
        cut = slice(d, d + 3)
        edges.append(jnp.concatenate([low(cut), own[cut], high(cut)], axis=1))
    give(pos, 0, s_in, s_out, edges[0], edges[1])


def fill_input(pos, store, own, g_in, g_out, x_in, x_out):
    low, high = sides(pos, 1, g_in, g_out)
    under, over = sides(pos, 0, x_in, x_out)
    lane = lax.broadcasted_iota(jnp.int32, (320, 128), 1)
    for d in range(10):
        if d < 3:
            line = under(d)
        elif d < 7:
            line = jnp.concatenate([low(d - 3), own[d - 3], high(d - 3)], axis=0)
        else:
            line = over(d - 7)
        wide = pltpu.roll(line.reshape(384, 128).astype(F32), 64, 1)
        odd = jnp.where(lane < 64, wide[:320], wide[64:]).astype(BF).reshape(5, 64, 128)
        for m in range(6):
            if m < 5:
                store[d, 2 * m + 1] = odd[m]
            store[d, 2 * m] = line[m]


def encode(
    pos, fetched, own, g_in, g_out, x_in, x_out, cotangent, mean,
    paired, encoded, slope, pooled, bot_slope, bottom, s_in, s_out,
    weight,
):
    fill_input(pos, paired, own, g_in, g_out, x_in, x_out)
    high = pos[0] * 4 - 2
    tall = pos[1] * 4 - 2
    w_enc = fetched(0)
    for depth in range(3):
        for height in range(3):
            at = depth * 256 + height * 64
            weight[at : at + 64, :] = lanes([w_enc[depth, height, k] for k in range(3)])
        weight[depth * 256 + 192 : depth * 256 + 256, :] = jnp.zeros((64, 384), BF)

    place = lax.broadcasted_iota(jnp.int32, (512, 128), 0) // 64 + tall
    across = (place >= 0) & (place < 64)
    for d in range(8):
        window = lanes(
            [
                paired[d + depth, 2 * half + 1 : 2 * half + 9].reshape(512, 128)
                for depth in range(3)
                for half in range(2)
            ]
        )
        pre = gathered(dot(window, weight[...]), 64, 128)
        sigma = sigmoid(pre)
        inside = across & (d + high >= 0) & (d + high < 64)
        encoded[d] = jnp.where(inside, pre * sigma, 0.0).astype(BF).reshape(8, 64, 128)
        slope[d] = jnp.where(inside, slope_of(pre, sigma), 0.0).astype(BF).reshape(8, 64, 128)
    for i in range(4):
        line = lanes(
            [encoded[2 * i : 2 * i + 2, 2 * j : 2 * j + 2].reshape(256, 128) for j in range(4)]
        )
        value = dot(mean[...], line).astype(BF)
        for j in range(4):
            pooled[i, j] = value[:, 128 * j : 128 * j + 128]
    window = lanes(
        [
            pooled[depth : depth + 2, height : height + 2].reshape(128, 128)
            for depth in range(3)
            for height in range(3)
        ]
    )
    w_bot = fetched(1)
    rows = jnp.concatenate(
        [
            lanes([w_bot[depth, height, k] for k in range(3)])
            for depth in range(3)
            for height in range(3)
        ],
        axis=0,
    )
    pre = gathered(dot(window, rows), 32, 256)
    sigma = sigmoid(pre)
    value = (pre * sigma).astype(BF).reshape(2, 2, 32, 256)
    bottom[...] = value
    bot_slope[...] = slope_of(pre, sigma)
    edges = []
    for h, at in ((0, 0), (1, 3)):
        row = value[:, h].reshape(64, 256)
        edges.append(stacked([cotangent[:, at].reshape(256, 128), row[:, :128], row[:, 128:]]))
    give(pos, 1, s_in, s_out, edges[0], edges[1])


def bottom_slabs(pos, bottom, cotangent, g_in, g_out, s_in, s_out):
    low, high = sides(pos, 1, g_in, g_out)
    edges = []
    for d, b in ((0, 0), (3, 1)):
        cot = slice(64 * d, 64 * d + 64)
        parts = [low(cot), cotangent[d].reshape(256, 128), high(cot)]
        for half in range(2):
            cut = slice(256 + 64 * half + 32 * b, 256 + 64 * half + 32 * b + 32)
            lane = slice(128 * half, 128 * half + 128)
            parts += [low(cut), bottom[b, 0, :, lane], bottom[b, 1, :, lane], high(cut)]
        edges.append(stacked(parts))
    give(pos, 0, s_in, s_out, edges[0], edges[1])


def fill_bottom(pos, wide_bottom, wide_cot, bottom, cotangent, g_in, g_out, x_in, x_out):
    low, high = sides(pos, 1, g_in, g_out)
    for d in range(4):
        cut = slice(64 * d, 64 * d + 64)
        wide_cot[d + 1, 0] = low(cut)
        wide_cot[d + 1, 1:5] = cotangent[d]
        wide_cot[d + 1, 5] = high(cut)
    for b in range(2):
        wide_bottom[b + 1, 1:3] = bottom[b]
        for half in range(2):
            cut = slice(256 + 64 * half + 32 * b, 256 + 64 * half + 32 * b + 32)
            lane = slice(128 * half, 128 * half + 128)
            wide_bottom[b + 1, 0, :, lane] = low(cut)
            wide_bottom[b + 1, 3, :, lane] = high(cut)
    for side, d, b in zip(sides(pos, 0, x_in, x_out), (0, 5), (0, 3)):
        wide_cot[d] = side(slice(0, 384)).reshape(6, 64, 128)
        for half in range(2):
            cut = slice(384 + 128 * half, 512 + 128 * half)
            lane = slice(128 * half, 128 * half + 128)
            wide_bottom[b, :, :, lane] = side(cut).reshape(4, 32, 128)


def decode(
    pos, fetched, own_bottom, own_cot, g_in, g_out, x_in, x_out,
    encoded, bot_slope, stretch, sort,
    decoded, lifted, dec_grad, skip, sorted_lift, bottom_grad, s_in, s_out,
    lift_all, gstore, bottom, cotangent,
):
    fill_bottom(pos, bottom, cotangent, own_bottom, own_cot, g_in, g_out, x_in, x_out)
    w_up = fetched(0)
    wide = []
    for i in range(4):
        spread = dot(stretch[...], lanes([bottom[i, j] for j in range(4)])).astype(BF)
        for j in range(4):
            cut = slice(256 * j, 256 * j + 256)
            wide.append(lanes([spread[:64, cut], spread[64:, cut]]))
    up = lanes([w_up[a, b].reshape(512, 128) for a in range(2) for b in range(2)])
    value = dot(stacked(wide), up).astype(BF).reshape(4, 4, 64, 512)
    for a in range(2):
        for b in range(2):
            cut = slice(128 * (2 * a + b), 128 * (2 * a + b) + 128)
            for i in range(4):
                for j in range(4):
                    lift_all[2 * i + a, 2 * j + b] = value[i, j, :, cut]
    lifted[...] = lift_all[1:7, 1:7]

    w_dec = fetched(1)
    for d in range(0, 6, 2):
        wide = None
        for depth in range(3):
            window = lanes(
                [
                    cells[d + depth : d + depth + 2, height : height + 6].reshape(768, 128)
                    for height in range(3)
                    for cells in (lift_all, encoded)
                ]
            )
            rows = stacked([lanes([w_dec[depth, height, k] for k in range(3)]) for height in range(3)])
            part = dot(window, rows)
            wide = part if wide is None else wide + part
        pre = gathered(wide, 64, 128)
        sigma = sigmoid(pre)
        cot = cotangent[d : d + 2].reshape(768, 128).astype(F32)
        grad = (cot * slope_of(pre, sigma)).astype(BF).reshape(2, 6, 64, 128)
        value = (pre * sigma).astype(BF).reshape(2, 6, 64, 128)
        gstore[d : d + 2] = grad
        for n in range(2):
            if 1 <= d + n <= 4:
                decoded[d + n - 1] = value[n, 1:5]
                dec_grad[d + n - 1] = grad[n, 1:5]
    pieces = [[], []]
    back_all = transposed(gstore, w_dec)
    for d in range(4):
        back = back_all[256 * d : 256 * d + 256]
        skip[d] = back[:, 128:].astype(BF).reshape(4, 64, 128)
        lift = back[:, :128].astype(BF).reshape(4, 64, 128)
        flat = lanes([lift[h] for h in range(4)])
        pieces[d // 2].append(dot(sort[...], flat).astype(BF))
    rows = []
    for i in range(2):
        for j in range(2):
            rows.append(
                lanes(
                    [
                        pieces[i][a][32 * c : 32 * c + 32, 128 * (2 * j + b) : 128 * (2 * j + b) + 128]
                        for a in range(2)
                        for b in range(2)
                        for c in range(2)
                    ]
                )
            )
    rows = jnp.concatenate(rows, axis=0)
    sorted_lift[...] = rows
    up = lanes([w_up[a, b, c] for a in range(2) for b in range(2) for c in range(2)])
    back = dot_nt(rows, up)
    grad = (back * bot_slope[...]).astype(BF)
    bottom_grad[...] = grad.reshape(2, 2, 32, 256)
    give(pos, 1, s_in, s_out, skip[:, 0].reshape(256, 128), skip[:, 3].reshape(256, 128), slice(0, 256))
    for half in range(2):
        cut = slice(256 + 128 * half, 384 + 128 * half)
        s_in[cut] = grad[:, 128 * half : 128 * half + 128]
        s_out[cut] = grad[:, 128 * half : 128 * half + 128]


def grad_slabs(pos, grad, skip, g_in, g_out, s_in, s_out):
    low, high = sides(pos, 1, g_in, g_out)
    edges = []
    for d in (0, 3):
        cut = slice(64 * d, 64 * d + 64)
        edges.append(stacked([low(cut), skip[d].reshape(256, 128), high(cut)]))
    give(pos, 0, s_in, s_out, edges[0], edges[1], slice(0, 384))
    for half in range(2):
        lane = slice(128 * half, 128 * half + 128)
        for d in range(2):
            cut = slice(256 + 128 * half + 64 * d, 256 + 128 * half + 64 * d + 64)
            line = stacked([low(cut), grad[d, 0, :, lane], grad[d, 1, :, lane], high(cut)])
            at = 384 + 384 * half + 192 * d
            s_in[at : at + 192] = line
            s_out[at : at + 192] = line


def fill_grad(pos, wide_grad, wide_skip, grad, skip, g_in, g_out, x_in, x_out):
    low, high = sides(pos, 1, g_in, g_out)
    for d in range(4):
        cut = slice(64 * d, 64 * d + 64)
        wide_skip[d + 1, 0] = low(cut)
        wide_skip[d + 1, 1:5] = skip[d]
        wide_skip[d + 1, 5] = high(cut)
    for b in range(2):
        wide_grad[b + 2, 2:4] = grad[b]
        for half in range(2):
            cut = slice(256 + 128 * half + 64 * b, 256 + 128 * half + 64 * b + 64)
            lane = slice(128 * half, 128 * half + 128)
            wide_grad[b + 2, 0:2, :, lane] = low(cut).reshape(2, 32, 128)
            wide_grad[b + 2, 4:6, :, lane] = high(cut).reshape(2, 32, 128)
    for side, d, b in zip(sides(pos, 0, x_in, x_out), (0, 5), (0, 4)):
        wide_skip[d] = side(slice(0, 384)).reshape(6, 64, 128)
        for half in range(2):
            cut = slice(384 + 384 * half, 768 + 384 * half)
            lane = slice(128 * half, 128 * half + 128)
            wide_grad[b : b + 2, :, :, lane] = side(cut).reshape(2, 6, 32, 128)


def put(first, keep, send, at, one, two):
    keep[:, at : at + 128] = jnp.where(first, one, two).astype(BF)
    send[:, at : at + 128] = jnp.where(first, two, one).astype(BF)


def decode_weights(pos, lifted, encoded, dec_grad, keep, send):
    first = pos[0] % 2 == 0
    grad = tripled(dec_grad[...].reshape(1024, 128).astype(F32), 64)
    for depth in range(3):
        for height in range(3):
            window = lanes(
                [
                    lifted[depth : depth + 4, height : height + 4].reshape(1024, 128),
                    encoded[depth + 1 : depth + 5, height + 1 : height + 5].reshape(1024, 128),
                ]
            )
            part = dot(grad, window)
            for k in range(3):
                rows = part[k * 128 : k * 128 + 128]
                at = ((depth * 3 + height) * 3 + k) * 128
                put(first, keep, send, at, rows[:, :128], rows[:, 128:])


def spread_row(row, spread):
    cells = row.reshape(4, 32, 128)
    flat = lanes([cells[h] for h in range(4)])
    upper = flat.astype(BF)
    lower = (flat - upper.astype(F32)).astype(BF)
    return dot(spread[...], jnp.concatenate([upper, lower], axis=0))


def bottom_weights(
    pos, sorted_lift, bottom, pooled, bottom_grad,
    keep, send,
):
    first = pos[0] % 2 == 0
    grad = tripled(bottom_grad[...].reshape(128, 256).astype(F32), 32)
    for depth in range(3):
        window = lanes(
            [
                pooled[depth : depth + 2, height : height + 2].reshape(128, 128)
                for height in range(3)
            ]
        )
        part = dot(grad, window)
        for k in range(3):
            rows = part[k * 256 : k * 256 + 256].reshape(16, 2, 8, 384)
            one, two = rows[:, 0].reshape(128, 384), rows[:, 1].reshape(128, 384)
            for height in range(3):
                at = ((depth * 3 + height) * 3 + k) * 128
                cut = slice(height * 128, height * 128 + 128)
                put(first, keep, send, at, one[:, cut], two[:, cut])
    part = dot(
        jnp.transpose(sorted_lift[...].astype(F32)).astype(BF), bottom[...].reshape(128, 256)
    )
    for t in range(8):
        rows = part[t * 128 : t * 128 + 128]
        put(first, keep, send, 3456 + t * 128, rows[:, :128], rows[:, 128:])


def encode_weights(
    pos, fetched, bottom_grad, skip, slope, paired, spread,
    keep, send,
    bstore, turned,
):
    first = pos[0] % 2 == 0
    bstore[...] = jnp.zeros((6, 6, 32, 256), BF)
    bstore[2:4, 2:4] = bottom_grad[...]
    w_bot = fetched(0)
    back = transposed(bstore, w_bot)
    for d in range(4):
        wide = spread_row(back[128 * d : 128 * d + 128], spread)
        for f in (2 * d, 2 * d + 1):
            cells = []
            for h in range(8):
                value = wide[:, h // 2 * 128 : h // 2 * 128 + 128]
                if 2 <= f < 6 and 2 <= h < 6:
                    value = value + skip[f - 2, h - 2].astype(F32)
                cells.append(value * slope[f, h].astype(F32))
            row = jnp.concatenate(cells, axis=0).astype(BF).astype(F32)
            turned[:, f * 512 : f * 512 + 512] = tripled(row, 64)

    lane = lax.broadcasted_iota(jnp.int32, (4096, 128), 1)

    def window(depth, height):
        return paired[depth : depth + 8, height + 1 : height + 9].reshape(4096, 128)

    blocks = [window(0, 0), window(1, 0), window(2, 0)]
    blocks.append(jnp.where(lane < 64, window(0, 2), window(1, 1)))
    blocks.append(jnp.where(lane < 64, window(2, 2), window(2, 1)))
    parts = []
    for n in (0, 2, 4):
        part = dot(turned[...], lanes(blocks[n : n + 2]))
        parts += [part[:, m * 128 : m * 128 + 128] for m in range(part.shape[1] // 128)]
    cut = [[part[k * 128 : k * 128 + 128] for k in range(3)] for part in parts]
    small = lax.broadcasted_iota(jnp.int32, (128, 128), 1)
    final = cut[0] + cut[1] + cut[2] + cut[3]
    final += [jnp.where(small < 64, cut[4][0], cut[4][1]), cut[4][2]]
    for n in range(7):
        put(first, keep, send, n * 128, final[n], final[n + 7])


def encode_back(
    pos, fetched, own_grad, own_skip, g_in, g_out, x_in, x_out, slope, spread,
    pool_grad, input_grad, done,
    gstore, grad, skip,
):
    done[...] = jnp.zeros((8, 128), F32)
    fill_grad(pos, grad, skip, own_grad, own_skip, g_in, g_out, x_in, x_out)
    w_bot = fetched(0)
    back = transposed(grad, w_bot)
    for d in range(4):
        row = back[128 * d : 128 * d + 128]
        if 1 <= d <= 2:
            pool_grad[d - 1] = row.reshape(4, 32, 128)[1:3]
        wide = spread_row(row, spread)
        for f in range(6):
            if (f + 1) // 2 != d:
                continue
            for h in range(6):
                at = (h + 1) // 2 * 128
                value = skip[f, h].astype(F32) + wide[:, at : at + 128]
                gstore[f, h] = (value * slope[f + 1, h + 1].astype(F32)).astype(BF)
    w_enc = fetched(1)
    input_grad[...] = transposed(gstore, w_enc).astype(BF).reshape(4, 4, 64, 64)


def swap(inner, outer, axis):
    count = lax.axis_size(axis)
    pairs = [(i, (i + 1) % count) for i in range(1, count, 2)]
    pairs += [(j, i) for i, j in pairs]
    got = lax.ppermute(inner, axis, [(i, i ^ 1) for i in range(count)])
    return got, lax.ppermute(outer, axis, pairs)


def add_cores(pos, *refs):
    total = refs[-1]
    at = 0
    for keep, got in zip(refs[0:-1:2], refs[1:-1:2]):
        width = keep.shape[1]
        total[:, at : at + width] = (keep[...].astype(F32) + got[...].astype(F32)).astype(BF)
        at += width


def add_heights(pos, parts, chunks):
    filled = parts.shape[2] // 128
    for n in range(9 * chunks.shape[0]):
        if n < filled:
            cut = slice(128 * n, 128 * n + 128)
            total = parts[0, :, cut].astype(F32)
            for j in range(1, 16):
                total = total + parts[j, :, cut].astype(F32)
        else:
            total = jnp.zeros((8, 128), F32)
        at = 128 * (n % 9)
        chunks[n // 9, :, at : at + 128] = total.astype(BF)


def add_depths(pos, parts, copies):
    total = parts[0].astype(F32)
    for j in range(1, 8):
        total = total + parts[j].astype(F32)
    total = total.astype(BF)
    for j in range(8):
        copies[j] = total


def finish(pos, mine, other, grad_enc, grad_bot, grad_up, grad_dec):
    first = pos[0] % 2 == 0

    def block(n):
        cut = slice(128 * (n % 9), 128 * (n % 9) + 128)
        left, right = mine[n // 9, :, cut].astype(F32), other[n // 9, :, cut].astype(F32)
        return jnp.where(first, left, right), jnp.where(first, right, left)

    for t in range(27):
        grad_dec[t, :, :128], grad_dec[t, :, 128:] = block(t)
        grad_bot[t, :8], grad_bot[t, 8:] = block(27 + t)
    for t in range(8):
        grad_up[t, :, :128], grad_up[t, :, 128:] = block(54 + t)
    pairs = [block(62 + n) for n in range(7)]
    pieces = [p[0] for p in pairs] + [p[1] for p in pairs]

    def tap(depth, height, k):
        return (depth * 3 + height) * 3 + k

    for k in range(3):
        for depth in range(3):
            piece = pieces[depth * 3 + k]
            grad_enc[tap(depth, 0, k)] = piece[:, :64]
            grad_enc[tap(depth, 1, k)] = piece[:, 64:]
        grad_enc[tap(0, 2, k)] = pieces[9 + k][:, :64]
        grad_enc[tap(1, 2, k)] = pieces[9 + k][:, 64:]
    grad_enc[tap(2, 2, 0)] = pieces[12][:, :64]
    grad_enc[tap(2, 2, 1)] = pieces[12][:, 64:]
    grad_enc[tap(2, 2, 2)] = pieces[13][:, :64]


def other_core(values):
    return lax.ppermute(values, "gx", [(i, i ^ 1) for i in range(lax.axis_size("gx"))])


def to_owners(part):
    return lax.all_to_all(part.reshape(16, 8, part.shape[1]), "gy", 0, 0, tiled=True)


def over_depths(pos, chunks):
    groups = [[2 * a + b for a in range(8)] for b in range(2)]
    got = lax.all_to_all(chunks, "gx", 0, 0, tiled=True, axis_index_groups=groups)
    (copies,) = call(add_depths, [((8, 8, 1152), BF)], [], pos, got)
    return lax.all_to_all(copies, "gx", 0, 0, tiled=True, axis_index_groups=groups)


def constants():
    w, k = np.arange(64)[:, None], np.arange(32)[None, :]
    mean = np.tile((w // 2 == k).T * 0.125, (1, 4))
    stretch = np.concatenate([w == 2 * k, w == 2 * k + 1], axis=0)
    sort = np.concatenate([(w == 2 * k).T, (w == 2 * k + 1).T], axis=0)
    spread = np.concatenate([(w // 2 == k) * 0.125] * 2, axis=1)
    return [jnp.asarray(v, BF) for v in (mean, stretch, sort, spread)]


def shards(inputs, cotangent, w_enc, w_bot, w_up, w_dec):
    mean, stretch, sort, spread = constants()
    pos = jnp.stack([lax.axis_index("gx"), lax.axis_index("gy")]).astype(jnp.int32)
    own = jnp.concatenate([inputs[:, 0::2], inputs[:, 1::2]], axis=3)
    near = swap(own, own, "gy")
    slabs = call(input_slabs, [((3, 6, 64, 128), BF)] * 2, [], pos, own, *near)
    near += swap(*slabs, "gx")
    paired, encoded, slope, pooled, bot_slope, bottom, *slabs = call(
        encode,
        [
            ((10, 11, 64, 128), BF),
            ((8, 8, 64, 128), BF),
            ((8, 8, 64, 128), BF),
            ((4, 4, 32, 128), BF),
            ((128, 256), F32),
            ((2, 2, 32, 256), BF),
        ]
        + [((384, 128), BF)] * 2,
        [((768, 384), BF)],
        pos, own, *near, cotangent, mean, far=(w_enc, w_bot),
        us=6,
    )
    near = swap(*slabs, "gy")
    slabs = call(bottom_slabs, [((640, 128), BF)] * 2, [], pos, bottom, cotangent, *near)
    near += swap(*slabs, "gx")
    decoded, lifted, dec_grad, skip, sorted_lift, bottom_grad, *slabs = call(
        decode,
        [
            ((4, 4, 64, 128), BF),
            ((6, 6, 64, 128), BF),
            ((4, 4, 64, 128), BF),
            ((4, 4, 64, 128), BF),
            ((128, 1024), BF),
            ((2, 2, 32, 256), BF),
        ]
        + [((512, 128), BF)] * 2,
        [
            ((8, 8, 64, 128), BF),
            ((6, 6, 64, 128), BF),
            ((4, 4, 32, 256), BF),
            ((6, 6, 64, 128), BF),
        ],
        pos, bottom, cotangent, *near, encoded, bot_slope, stretch, sort, far=(w_up, w_dec),
        us=13,
    )
    near = swap(*slabs, "gy")
    keep_dec, send_dec = call(
        decode_weights,
        [((128, 3456), BF)] * 2,
        [],
        pos, lifted, encoded, dec_grad,
        us=3,
    )
    got_dec = other_core(send_dec)
    keep_bot, send_bot = call(
        bottom_weights,
        [((128, 4480), BF)] * 2,
        [],
        pos, sorted_lift, bottom, pooled, bottom_grad,
        us=2,
    )
    got_bot = other_core(send_bot)
    keep_enc, send_enc = call(
        encode_weights,
        [((128, 896), BF)] * 2,
        [((6, 6, 32, 256), BF), ((384, 4096), BF)],
        pos, bottom_grad, skip, slope, paired, spread,
        far=(w_bot,), us=6,
    )
    *slabs, send_enc = call(
        grad_slabs, [((1152, 128), BF)] * 2, [], pos, bottom_grad, skip, *near,
        behind=(keep_dec, keep_bot), through=(send_enc,),
    )
    (part,) = call(
        add_cores, [((128, 8832), BF)], [],
        pos, keep_dec, got_dec, keep_bot, got_bot, keep_enc, other_core(send_enc),
        behind=slabs[:1],
    )
    near += swap(*slabs, "gx")
    pool_grad, input_grad, done = call(
        encode_back,
        [((2, 2, 32, 128), F32), ((4, 4, 64, 64), BF), ((8, 128), F32)],
        [((6, 6, 64, 128), BF), ((6, 6, 32, 256), BF), ((6, 6, 64, 128), BF)],
        pos, bottom_grad, skip, *near, slope, spread,
        far=(w_bot, w_enc), behind=(part,),
        us=5,
    )
    (chunks,) = call(
        add_heights, [((8, 8, 1152), BF)], [], pos, to_owners(part), behind=(done,), us=2
    )
    mine = over_depths(pos, chunks)
    other = other_core(mine)
    grads = call(
        finish,
        [((27, 8, 64), F32), ((27, 16, 128), F32), ((8, 8, 256), F32), ((27, 8, 256), F32)],
        [],
        pos, mine, other,
    )
    grad_enc, grad_bot, grad_up, grad_dec = (
        jnp.transpose(grad, (0, 2, 1)).reshape(*shape, grad.shape[2], grad.shape[1])
        for grad, shape in zip(grads, ((3, 3, 3), (3, 3, 3), (2, 2, 2), (3, 3, 3)))
    )
    return (decoded, input_grad, grad_enc, grad_bot, grad_up, grad_dec, pool_grad)


def solution(mesh):
    in_specs = (P("gx", "gy", None, None), P("gx", "gy", None, None), P(), P(), P(), P())
    out_specs = (
        P("gx", "gy", None, None),
        P("gx", "gy", None, None),
        P(None, None, None, None, "gy"),
        P(None, None, None, None, "gy"),
        P(None, None, None, None, "gy"),
        P(None, None, None, None, "gy"),
        P("gx", "gy", None, None),
    )
    return jax.shard_map(shards, mesh=mesh, in_specs=in_specs, out_specs=out_specs, check_vma=False)
```
